32 devices in a mesh: row: 8 (over y, x, core), col: 4 (over z).
Axes of the slice: x: 2, y: 2, z: 4, core: 2. Of those that a mesh axis runs over, the one named last changes fastest.
Arguments:
- fine_blocks: bfloat16 [8, 4, 64, 128, 128], P('row', 'col'), may hold values from -0.5 to 0.5
- fine_rows: int32 [8, 4, 64], P('row', 'col'), may hold values from 0 to 7
- fine_cols: int32 [8, 4, 64], P('row', 'col'), may hold values from 0 to 39
- fine_counts: int32 [8, 4], P('row', 'col'), may hold values from 8 to 64, as said below
- prolong_blocks: bfloat16 [8, 4, 12, 128, 128], P('row', 'col'), may hold values from -1.5 to 1.5
- prolong_codes: int32 [8, 4, 12], P('row', 'col'), may hold values from 0 to 15, as said below
- prolong_counts: int32 [8, 4], P('row', 'col'), may hold values from 6 to 12, as said below
- second_blocks: bfloat16 [8, 4, 2, 128, 128], P('row', 'col'), may hold values from -0.25 to 0.25
- second_aggs: int32 [8, 4, 2], P('row', 'col'), may hold values from 0 to 1
Outputs:
- coarse_one: bfloat16 [8, 4, 2, 5, 2, 128, 128], P('row', 'col')
- coarse_two: float32 [8, 2, 3, 2, 128, 128], P('row')
The draws below stay inside these ranges and needn't reach their ends.
Inputs may be any that keep to these rules, and one draw needn't show every extreme that they name: Slots from fine_counts[r, c] to 63 are padding and are ignored; in every draw some device has all 64 slots live. `fine_cols`: a source outside the grid of devices contributes nothing. `prolong_codes`: the live slots of one device name distinct blocks. Slots from prolong_counts[r, c] to 11 are padding and are ignored; in every draw some device has all 12 slots live.
All inputs are finite; a program needn't handle non-finite values.
Results may differ from the reference program's by a relative error of at most 0.0057.
Values may be sent and summed in bfloat16 or wider, within the bound.
No kernel may reach another device: no remote copies, remote signals or barrier semaphores. Data moves between devices by JAX's collectives and lax.ppermute only.
A program may use at most 64 MiB of HBM per device.

```python
import jax
import jax.numpy as jnp
from jax import lax

BS = 128
FB = 8
CB = 2
NA = 64
NP = 12
G2 = 2
NR = 8
NC = 4


def skewed_counts(key, lowest, highest, fullest):
    key_base, key_heavy, key_chosen = jax.random.split(key, 3)
    counts = jax.random.randint(key_base, (NR * NC,), lowest, highest + 1)
    heavy_rows = jax.random.randint(key_heavy, (NR * NC,), 0, 8) == 0
    counts = jnp.where(heavy_rows, fullest, counts)
    chosen = jax.random.randint(key_chosen, (), 0, NR * NC)
    counts = counts.at[chosen].set(fullest)
    return counts.reshape(NR, NC).astype(jnp.int32)


def draw_fine_counts(key, part):
    return skewed_counts(jax.random.fold_in(key, 11), NA // 8, NA // 2, NA)


def draw_prolong_counts(key, part):
    return skewed_counts(jax.random.fold_in(key, 23), NP // 2, NP, NP)


def draw_prolong_codes(key, part):
    device_keys = jax.random.split(jax.random.fold_in(key, 37), NR * NC)
    orders = jax.vmap(lambda one_key: jax.random.permutation(one_key, FB * CB))(device_keys)
    return orders[:, :NP].reshape(NR, NC, NP).astype(jnp.int32)


def with_ends(drawn, rng, smallest, high):
    longest = drawn.shape.index(max(drawn.shape))
    spots = []
    for shift in (0, 1):
        where = [jax.random.randint(jax.random.fold_in(rng, axis), (), 0, length) for axis, length in enumerate(drawn.shape)]
        where[longest] = (where[longest] + shift) % drawn.shape[longest]
        spots.append(tuple(where))
    return drawn.at[spots[0]].set(smallest).at[spots[1]].set(high)


def block_scale(key, extent, cuts, low, high):
    gain, own = 1.0, jax.random.fold_in(key, 6)
    for axis_at, shards_of in cuts:
        heights = jnp.exp(jax.random.uniform(jax.random.fold_in(own, axis_at), (shards_of,), jnp.float32, low / len(cuts), high / len(cuts)))
        gain = gain * jnp.repeat(heights, extent[axis_at] // shards_of).reshape([-1 if axis == axis_at else 1 for axis in range(len(extent))])
    return gain


def noise(stream_key, dims, scale, reach, cuts=(), kind=jnp.bfloat16):
    level = block_scale(stream_key, dims, cuts, -0.22, 0.18) if cuts else 1.0
    values = jax.random.normal(stream_key, dims, jnp.float32) * scale * level
    return jnp.minimum(jnp.maximum(values, -reach), reach).astype(kind)


def setup_inputs(seed: int = 0) -> dict:
    splits = jax.random.split(jax.random.key(seed), 10)
    fine_blocks = noise(splits[0], (NR, NC, NA, BS, BS), 0.09, 0.5, ((0, 8), (1, 4)))
    fine_rows = with_ends(jax.random.randint(splits[1], (NR, NC, NA), 0, FB), jax.random.fold_in(splits[1], 1), 0, FB - 1).astype(jnp.int32)
    fine_cols = with_ends(jax.random.randint(splits[2], (NR, NC, NA), 0, 5 * FB), jax.random.fold_in(splits[2], 1), 0, (5 * FB) - 1).astype(jnp.int32)
    fine_counts = draw_fine_counts(jax.random.fold_in(splits[9], 71), 0)
    prolong_blocks = noise(splits[4], (NR, NC, NP, BS, BS), 0.25, 1.5, ((0, 8), (1, 4)))
    prolong_codes = draw_prolong_codes(jax.random.fold_in(splits[9], 71), 0)
    prolong_counts = draw_prolong_counts(jax.random.fold_in(splits[9], 71), 0)
    second_blocks = noise(splits[7], (NR, NC, CB, BS, BS), 0.04, 0.25, ((0, 8), (1, 4)))
    second_aggs = with_ends(jax.random.randint(splits[8], (NR, NC, CB), 0, G2), jax.random.fold_in(splits[8], 1), 0, G2 - 1).astype(jnp.int32)
    return dict(fine_blocks=fine_blocks, fine_rows=fine_rows, fine_cols=fine_cols, fine_counts=fine_counts, prolong_blocks=prolong_blocks, prolong_codes=prolong_codes, prolong_counts=prolong_counts, second_blocks=second_blocks, second_aggs=second_aggs)


OFFSETS = ((0, 0), (0, -1), (0, 1), (-1, 0), (1, 0))
HIGHEST = lax.Precision.HIGHEST


def neighbour_blocks(table, row_at, col_at):
    gathered = []
    for row_step, col_step in OFFSETS:
        row_near = row_at + row_step
        col_near = col_at + col_step
        inside = (row_near >= 0) & (row_near < NR) & (col_near >= 0) & (col_near < NC)
        found = table[jnp.clip(row_near, 0, NR - 1), jnp.clip(col_near, 0, NC - 1)]
        gathered.append(jnp.where(inside, found, jnp.zeros_like(found)))
    return jnp.stack(gathered, axis=0)


def reference(fine_blocks, fine_rows, fine_cols, fine_counts, prolong_blocks, prolong_codes, prolong_counts, second_blocks, second_aggs):
    devices_flat = jnp.arange(NR * NC, dtype=jnp.int32)

    def dense_one(device_at):
        row_at = device_at // NC
        col_at = device_at % NC
        live_slots = jnp.arange(NP, dtype=jnp.int32) < prolong_counts[row_at, col_at]
        slot_codes = prolong_codes[row_at, col_at]
        placing = ((slot_codes[:, None] == jnp.arange(FB * CB, dtype=jnp.int32)[None, :]) & live_slots[:, None]).astype(jnp.float32)
        values = prolong_blocks[row_at, col_at].astype(jnp.float32)
        return jnp.einsum('kq,kxy->qxy', placing, values, precision=HIGHEST).astype(jnp.bfloat16)

    dense_all = lax.map(dense_one, devices_flat).reshape(NR, NC, FB * CB, BS, BS)

    def level_one(device_at):
        row_at = device_at // NC
        col_at = device_at % NC
        near_p = neighbour_blocks(dense_all, row_at, col_at).reshape(5 * FB, CB, BS, BS)
        columns = fine_cols[row_at, col_at]
        fetched = near_p[columns].astype(jnp.float32)
        blocks = fine_blocks[row_at, col_at].astype(jnp.float32)
        products = jnp.einsum('kxy,kjyz->kjxz', blocks, fetched, precision=HIGHEST)
        live_slots = jnp.arange(NA, dtype=jnp.int32) < fine_counts[row_at, col_at]
        products = jnp.where(live_slots[:, None, None, None], products, jnp.zeros_like(products))
        target = fine_rows[row_at, col_at] * 5 + columns // FB
        summed = jax.ops.segment_sum(products, target, num_segments=5 * FB)
        fine_product = lax.optimization_barrier(summed.astype(jnp.bfloat16)).astype(jnp.float32)
        fine_product = fine_product.reshape(FB, 5, CB, BS, BS)
        own_p = dense_all[row_at, col_at].reshape(FB, CB, BS, BS).astype(jnp.float32)
        result = jnp.einsum('iJxy,isjxz->Jsjyz', own_p, fine_product, precision=HIGHEST)
        return result.astype(jnp.bfloat16)

    coarse_one = lax.map(level_one, devices_flat).reshape(NR, NC, CB, 5, CB, BS, BS)

    member = (second_aggs[..., None] == jnp.arange(G2, dtype=jnp.int32)).astype(second_blocks.dtype)
    lifted_all = second_blocks[:, :, :, None] * member[..., None, None]

    def row_total(row_at):
        def one_device(col_at):
            near = neighbour_blocks(lifted_all, row_at, col_at).astype(jnp.float32)
            coarse = lax.optimization_barrier(coarse_one[row_at, col_at]).astype(jnp.float32)
            inside = jnp.einsum('Jsjxy,sjayz->Jaxz', coarse[:, 0:3], near[0:3], precision=HIGHEST)
            before = jnp.einsum('Jjxy,jayz->Jaxz', coarse[:, 3], near[3], precision=HIGHEST)
            beyond = jnp.einsum('Jjxy,jayz->Jaxz', coarse[:, 4], near[4], precision=HIGHEST)
            stacked = jnp.stack([inside, before, beyond], axis=1)
            half_prod = lax.optimization_barrier(stacked.astype(jnp.bfloat16)).astype(jnp.float32)
            own_lift = lifted_all[row_at, col_at].astype(jnp.float32)
            return jnp.einsum('Jaxy,Jgbxz->agbyz', own_lift, half_prod, precision=HIGHEST)

        terms = lax.map(one_device, jnp.arange(NC, dtype=jnp.int32))
        return jnp.sum(terms, axis=0)

    coarse_two = lax.map(row_total, jnp.arange(NR, dtype=jnp.int32))
    return coarse_one, coarse_two
```

```python
import functools
import math

import jax
import jax.numpy as jnp
from jax import lax
from jax.experimental import pallas as pl
from jax.experimental.pallas import tpu as pltpu
from jax.sharding import PartitionSpec as P

FB = 8
CB = 2
G2 = 2
NS = 5
PB = FB * CB
UNROLL = 4
META = 16
F32 = jnp.float32
BF16 = jnp.bfloat16

VMEM = pl.BlockSpec(memory_space=pltpu.VMEM)
SMEM = pl.BlockSpec(memory_space=pltpu.SMEM)
ANY = pl.BlockSpec(memory_space=pl.ANY)


def pack_kernel(codes, count, aggs, blocks, second, out, tile, sems):
    n_p, n_s = blocks.shape[0], second.shape[0]
    first = pltpu.make_async_copy(blocks, out.at[0:n_p], sems.at[0])
    first.start()
    after = pltpu.make_async_copy(second, out.at[n_p : n_p + n_s], sems.at[1])
    after.start()
    slots = codes.shape[0]
    lane = lax.broadcasted_iota(jnp.int32, tile.shape, 1)
    word = jnp.zeros(tile.shape, jnp.int32)
    for k in range(slots):
        word = jnp.where(lane == k, jnp.where(k < count[0], codes[k], PB), word)
    for j in range(CB):
        word = jnp.where(lane == slots + j, aggs[j], word)
    tile[...] = word.astype(F32).astype(BF16)
    last = pltpu.make_async_copy(tile, out.at[n_p + n_s : n_p + n_s + META], sems.at[2])
    last.start()
    first.wait()
    after.wait()
    last.wait()


def main_kernel(
    slots, size, cols_n, rows, cols, count, fine, own, left, right, up, down,
    c_one, *rest,
):
    sends = rest[:cols_n]
    dense, turned, acc, lift, terms, words, codes, sem = rest[cols_n:]
    near = (own, left, right, up, down)
    tail = (slots + CB) * size
    for s in range(NS):
        word = near[s][tail : tail + META, :].astype(F32).astype(jnp.int32)
        words[s : s + 1, :] = word[0:1, :]
    fetch = pltpu.make_async_copy(words, codes, sem)
    fetch.start()
    zero = jnp.zeros((size, size), BF16)
    for s in range(NS):
        for q in range(PB):
            dense[s * (PB + 1) + q] = zero
    acc[...] = jnp.zeros_like(acc)
    fetch.wait()
    for s in range(NS):
        for k in range(slots):
            dense[s * (PB + 1) + codes[s, k]] = near[s][k * size : (k + 1) * size, :]
        for j in range(CB):
            block = near[s][(slots + j) * size : (slots + j + 1) * size, :]
            for a in range(G2):
                lift[s, j * size : (j + 1) * size, a * size : (a + 1) * size] = jnp.where(
                    codes[s, slots + j] == a, block, zero
                )
    for i in range(FB):
        for j in range(CB):
            turned[j * size : (j + 1) * size, i * size : (i + 1) * size] = dense[i * CB + j].T

    def step(t, carry):
        products, targets = [], []
        for u in range(UNROLL):
            k = t * UNROLL + u
            live = k < count[0]
            at = jnp.where(live, cols[k], 0)
            s = at // FB
            base = s * (PB + 1) + (at - s * FB) * CB
            wide = jnp.concatenate([dense[base + j] for j in range(CB)], axis=1)
            products.append(jnp.dot(fine[k], wide, preferred_element_type=F32))
            targets.append(jnp.where(live, s * FB + rows[k], NS * FB))
        for u in range(UNROLL):
            acc[targets[u]] += products[u]
        return carry

    lax.fori_loop(0, (count[0] + UNROLL - 1) // UNROLL, step, 0)

    halves = [None, None, None]
    for s in range(NS):
        product = acc[s * FB : (s + 1) * FB].reshape(FB * size, CB * size).astype(BF16)
        coarse = jnp.dot(turned[...], product, preferred_element_type=F32).astype(BF16)
        for i in range(CB):
            for j in range(CB):
                c_one[i, s, j] = coarse[i * size : (i + 1) * size, j * size : (j + 1) * size]
        part = jnp.dot(coarse, lift[s], preferred_element_type=F32)
        g = 0 if s < 3 else s - 2
        halves[g] = part if halves[g] is None else halves[g] + part
    lift_t = lift[0].T
    for g in range(3):
        terms[g * G2 * size : (g + 1) * G2 * size, :] = jnp.dot(
            lift_t, halves[g].astype(BF16), preferred_element_type=F32
        )
    chunk = terms.shape[0] // cols_n
    me = lax.axis_index("col")
    for d in range(cols_n):
        to = lax.rem(me + d, cols_n)
        part = terms[pl.ds(pl.multiple_of(to * chunk, chunk), chunk), :]
        sends[d][...] = part.astype(BF16)


def sum_kernel(*refs):
    total = refs[0][...].astype(F32)
    for ref in refs[1:-1]:
        total = total + ref[...].astype(F32)
    refs[-1][...] = total.astype(BF16)


def spread_kernel(size, cols_n, *refs):
    out = refs[-1]
    chunk = refs[0].shape[0]
    unit = math.gcd(chunk, size)
    per = size // unit
    me = lax.axis_index("col")
    for d in range(cols_n):
        owner = lax.rem(me - d + cols_n, cols_n)
        for t in range(chunk // unit):
            at = owner * (chunk // unit) + t
            g = at // (G2 * per)
            a = lax.rem(at // per, G2)
            h = pl.multiple_of(lax.rem(at, per) * unit, unit)
            for b in range(G2):
                out[a, g, b, pl.ds(h, unit), :] = refs[d][
                    t * unit : (t + 1) * unit, b * size : (b + 1) * size
                ].astype(F32)


def shift(x, axis, step, wrap):
    n = lax.axis_size(axis)
    pairs = [(i, (i + step) % n) for i in range(n) if wrap or 0 <= i + step < n]
    return lax.ppermute(x, axis, pairs)


def per_device(
    fine_blocks, fine_rows, fine_cols, fine_counts, prolong_blocks, prolong_codes,
    prolong_counts, second_blocks, second_aggs,
):
    slots, size = prolong_blocks.shape[2], prolong_blocks.shape[3]
    cols_n = lax.axis_size("col")
    packed_rows = (slots + CB) * size + META
    packed = pl.pallas_call(
        pack_kernel,
        out_shape=jax.ShapeDtypeStruct((packed_rows, size), BF16),
        in_specs=[SMEM, SMEM, SMEM, ANY, ANY],
        out_specs=ANY,
        scratch_shapes=[pltpu.VMEM((META, size), BF16), pltpu.SemaphoreType.DMA((3,))],
        name="pack",
    )(
        prolong_codes[0, 0],
        prolong_counts[0],
        second_aggs[0, 0],
        prolong_blocks.reshape(slots * size, size),
        second_blocks.reshape(CB * size, size),
    )
    left = shift(packed, "col", 1, False)
    right = shift(packed, "col", -1, False)
    up = shift(packed, "row", 1, False)
    down = shift(packed, "row", -1, False)

    chunk = 3 * G2 * size // cols_n
    piece = jax.ShapeDtypeStruct((chunk, G2 * size), BF16)
    c_one, *sends = pl.pallas_call(
        functools.partial(main_kernel, slots, size, cols_n),
        out_shape=[jax.ShapeDtypeStruct((CB, NS, CB, size, size), BF16)] + [piece] * cols_n,
        in_specs=[SMEM] * 3 + [VMEM] * 6,
        out_specs=[VMEM] * (1 + cols_n),
        scratch_shapes=[
            pltpu.VMEM((NS * (PB + 1), size, size), BF16),
            pltpu.VMEM((CB * size, FB * size), BF16),
            pltpu.VMEM((NS * FB + 1, size, CB * size), F32),
            pltpu.VMEM((NS, CB * size, G2 * size), BF16),
            pltpu.VMEM((3 * G2 * size, G2 * size), F32),
            pltpu.VMEM((8, size), jnp.int32),
            pltpu.SMEM((8, size), jnp.int32),
            pltpu.SemaphoreType.DMA,
        ],
        compiler_params=pltpu.CompilerParams(vmem_limit_bytes=40 * 1024 * 1024),
        name="products",
    )(
        fine_rows[0, 0], fine_cols[0, 0], fine_counts[0], fine_blocks[0, 0],
        packed, left, right, up, down,
    )
    parts = [sends[0]] + [shift(sends[d], "col", d, True) for d in range(1, cols_n)]
    total = pl.pallas_call(
        sum_kernel, out_shape=piece, in_specs=[VMEM] * cols_n, out_specs=VMEM, name="total"
    )(*parts)
    gathered = [total] + [shift(total, "col", d, True) for d in range(1, cols_n)]
    c_two = pl.pallas_call(
        functools.partial(spread_kernel, size, cols_n),
        out_shape=jax.ShapeDtypeStruct((G2, 3, G2, size, size), F32),
        in_specs=[VMEM] * cols_n,
        out_specs=VMEM,
        name="spread",
    )(*gathered)
    return (c_one[None, None], c_two[None])


def solution(mesh):
    in_specs = (
        P("row", "col", None, None, None),
        P("row", "col", None),
        P("row", "col", None),
        P("row", "col"),
        P("row", "col", None, None, None),
        P("row", "col", None),
        P("row", "col"),
        P("row", "col", None, None, None),
        P("row", "col", None),
    )
    out_specs = (
        P("row", "col", None, None, None, None, None),
        P("row", None, None, None, None, None),
    )
    return jax.shard_map(
        per_device, mesh=mesh, in_specs=in_specs, out_specs=out_specs, check_vma=False
    )
```

```python
import functools
import math

import jax
import jax.numpy as jnp
from jax import lax
from jax.experimental import pallas as pl
from jax.experimental.pallas import tpu as pltpu
from jax.sharding import PartitionSpec as P

FB = 8
CB = 2
G2 = 2
NS = 5
PB = FB * CB
UNROLL = 4
META = 16
F32 = jnp.float32
BF16 = jnp.bfloat16

VMEM = pl.BlockSpec(memory_space=pltpu.VMEM)
SMEM = pl.BlockSpec(memory_space=pltpu.SMEM)
SMALL = pltpu.CompilerParams(vmem_limit_bytes=4 * 1024 * 1024)
LARGE = pltpu.CompilerParams(vmem_limit_bytes=20 * 1024 * 1024)


def pack_kernel(codes, count, aggs, blocks, second, out):
    n_p, n_s = blocks.shape[0], second.shape[0]
    slots = codes.shape[0]
    out[0:n_p, :] = blocks[...]
    out[n_p : n_p + n_s, :] = second[...]
    lane = lax.broadcasted_iota(jnp.int32, (META, out.shape[1]), 1)
    word = jnp.zeros(lane.shape, jnp.int32)
    for k in range(slots):
        word = jnp.where(lane == k, jnp.where(k < count[0], codes[k], PB), word)
    for j in range(CB):
        word = jnp.where(lane == slots + j, aggs[j], word)
    out[n_p + n_s : n_p + n_s + META, :] = word.astype(F32).astype(BF16)


def slot_products(s, size, table, rows, cols, order, begin, end, fine, near, acc, base):
    def step(t, carry):
        products, targets = [], []
        for u in range(UNROLL):
            at = begin + t * UNROLL + u
            live = at < end
            k = order[jnp.minimum(at, end - 1)]
            m = cols[k] - s * FB
            parts = []
            for j in range(CB):
                slot = table[s, m * CB + j]
                first = pl.multiple_of(jnp.maximum(slot, 0) * size, size)
                block = near[pl.ds(first, size), :]
                parts.append(jnp.where(slot >= 0, block, jnp.zeros_like(block)))
            wide = jnp.concatenate(parts, axis=1)
            products.append(jnp.dot(fine[k], wide, preferred_element_type=F32))
            targets.append(jnp.where(live, base + rows[k], acc.shape[0] - 1))
        for u in range(UNROLL):
            acc[targets[u]] += products[u]
        return carry

    lax.fori_loop(0, (end - begin + UNROLL - 1) // UNROLL, step, 0)


def fill_table(s, slots, table, code_of):
    for q in range(PB + 1):
        table[s, q] = -1
    for k in range(slots):
        table[s, code_of(k)] = k


def lift_of(near, slots, size, agg_of):
    lines = []
    for j in range(CB):
        block = near[(slots + j) * size : (slots + j + 1) * size, :]
        lines.append(
            jnp.concatenate(
                [jnp.where(agg_of(j) == a, block, jnp.zeros_like(block)) for a in range(G2)],
                axis=1,
            )
        )
    return jnp.concatenate(lines, axis=0)


def coarse_of(turned, acc, base, size):
    product = acc[base : base + FB].reshape(FB * size, CB * size).astype(BF16)
    return jnp.dot(turned, product, preferred_element_type=F32).astype(BF16)


def own_kernel(
    slots, size, rows, cols, count, codes, p_count, aggs, fine, own,
    turned, coarse, half, lift_t, order, bounds, acc, table, fill,
):
    total = order.shape[0]
    for s in range(NS):
        fill[s] = 0

    def tally(k, carry):
        s = cols[k] // FB
        fill[s] += 1
        return carry

    lax.fori_loop(0, count[0], tally, 0)
    at = jnp.int32(0)
    for s in range(NS):
        n = fill[s]
        bounds[s] = at
        fill[s] = at
        at = at + n
    bounds[NS] = at

    def place(k, carry):
        s = cols[k] // FB
        order[fill[s]] = k
        fill[s] += 1
        return carry

    lax.fori_loop(0, count[0], place, 0)
    fill_table(0, slots, table, lambda k: jnp.where(k < p_count[0], codes[k], PB))
    for i in range(FB):
        for j in range(CB):
            slot = table[0, i * CB + j]
            block = own[pl.ds(pl.multiple_of(jnp.maximum(slot, 0) * size, size), size), :]
            block = jnp.where(slot >= 0, block, jnp.zeros_like(block))
            turned[j * size : (j + 1) * size, i * size : (i + 1) * size] = block.T
    acc[...] = jnp.zeros_like(acc)
    slot_products(0, size, table, rows, cols, order, 0, bounds[1], fine, own, acc, 0)
    coarse[...] = coarse_of(turned[...], acc, 0, size)
    lift = lift_of(own, slots, size, lambda j: aggs[j])
    half[...] = jnp.dot(coarse[...], lift, preferred_element_type=F32)
    lift_t[...] = lift.T


def near_kernel(
    slots, size, cols_n, rows, cols, order, bounds, fine, turned, coarse0, half0, lift_t,
    left, right, up, down, c_one, *rest,
):
    sends = rest[:cols_n]
    acc, terms, words, codes, table, sem = rest[cols_n:]
    near = (None, left, right, up, down)
    tail = (slots + CB) * size
    for s in range(1, NS):
        word = near[s][tail : tail + META, :].astype(F32).astype(jnp.int32)
        words[s : s + 1, :] = word[0:1, :]
    fetch = pltpu.make_async_copy(words, codes, sem)
    fetch.start()
    acc[...] = jnp.zeros_like(acc)
    fetch.wait()
    halves = [half0[...], None, None]
    for s in range(NS):
        if s == 0:
            coarse = coarse0[...]
        else:
            fill_table(s, slots, table, lambda k: codes[s, k])
            base = (s - 1) * FB
            slot_products(
                s, size, table, rows, cols, order, bounds[s], bounds[s + 1], fine, near[s], acc, base
            )
            coarse = coarse_of(turned[...], acc, base, size)
            lift = lift_of(near[s], slots, size, lambda j: codes[s, slots + j])
            part = jnp.dot(coarse, lift, preferred_element_type=F32)
            g = 0 if s < 3 else s - 2
            halves[g] = part if halves[g] is None else halves[g] + part
        for i in range(CB):
            for j in range(CB):
                c_one[i, s, j] = coarse[i * size : (i + 1) * size, j * size : (j + 1) * size]
    for g in range(3):
        terms[g * G2 * size : (g + 1) * G2 * size, :] = jnp.dot(
            lift_t[...], halves[g].astype(BF16), preferred_element_type=F32
        )
    chunk = terms.shape[0] // cols_n
    me = lax.axis_index("col")
    for d in range(cols_n):
        to = lax.rem(me + d, cols_n)
        part = terms[pl.ds(pl.multiple_of(to * chunk, chunk), chunk), :]
        sends[d][...] = part.astype(BF16)


def sum_kernel(*refs):
    total = refs[0][...].astype(F32)
    for ref in refs[1:-1]:
        total = total + ref[...].astype(F32)
    refs[-1][...] = total.astype(BF16)


def spread_kernel(size, cols_n, *refs):
    out = refs[-1]
    chunk = refs[0].shape[0]
    unit = math.gcd(chunk, size)
    per = size // unit
    me = lax.axis_index("col")
    for d in range(cols_n):
        owner = lax.rem(me - d + cols_n, cols_n)
        for t in range(chunk // unit):
            at = owner * (chunk // unit) + t
            g = at // (G2 * per)
            a = lax.rem(at // per, G2)
            h = pl.multiple_of(lax.rem(at, per) * unit, unit)
            for b in range(G2):
                out[a, g, b, pl.ds(h, unit), :] = refs[d][
                    t * unit : (t + 1) * unit, b * size : (b + 1) * size
                ].astype(F32)


def shift(x, axis, step, wrap):
    n = lax.axis_size(axis)
    pairs = [(i, (i + step) % n) for i in range(n) if wrap or 0 <= i + step < n]
    return lax.ppermute(x, axis, pairs)


def per_device(
    fine_blocks, fine_rows, fine_cols, fine_counts, prolong_blocks, prolong_codes,
    prolong_counts, second_blocks, second_aggs,
):
    slots, size = prolong_blocks.shape[2], prolong_blocks.shape[3]
    cols_n = lax.axis_size("col")
    packed_rows = (slots + CB) * size + META
    grid_slots = fine_blocks.shape[2]
    wide = CB * size
    packed = pl.pallas_call(
        pack_kernel,
        out_shape=jax.ShapeDtypeStruct((packed_rows, size), BF16),
        in_specs=[SMEM] * 3 + [VMEM] * 2,
        out_specs=VMEM,
        compiler_params=SMALL,
        name="pack",
    )(
        prolong_codes[0, 0],
        prolong_counts[0],
        second_aggs[0, 0],
        prolong_blocks.reshape(slots * size, size),
        second_blocks.reshape(CB * size, size),
    )
    up = shift(packed, "row", 1, False)
    down = shift(packed, "row", -1, False)
    left = shift(packed, "col", 1, False)
    right = shift(packed, "col", -1, False)

    turned, coarse0, half0, lift_t, order, bounds = pl.pallas_call(
        functools.partial(own_kernel, slots, size),
        out_shape=[
            jax.ShapeDtypeStruct((wide, FB * size), BF16),
            jax.ShapeDtypeStruct((wide, wide), BF16),
            jax.ShapeDtypeStruct((wide, G2 * size), F32),
            jax.ShapeDtypeStruct((G2 * size, wide), BF16),
            jax.ShapeDtypeStruct((grid_slots,), jnp.int32),
            jax.ShapeDtypeStruct((8,), jnp.int32),
        ],
        in_specs=[SMEM] * 6 + [VMEM] * 2,
        out_specs=[VMEM] * 4 + [SMEM] * 2,
        scratch_shapes=[
            pltpu.VMEM((FB + 1, size, wide), F32),
            pltpu.SMEM((NS, PB + 1), jnp.int32),
            pltpu.SMEM((8,), jnp.int32),
        ],
        compiler_params=LARGE,
        cost_estimate=pl.CostEstimate(flops=10**9, bytes_accessed=4 * 10**6, transcendentals=0),
        name="own_source",
    )(
        fine_rows[0, 0], fine_cols[0, 0], fine_counts[0],
        prolong_codes[0, 0], prolong_counts[0], second_aggs[0, 0],
        fine_blocks[0, 0], packed,
    )

    chunk = 3 * G2 * size // cols_n
    piece = jax.ShapeDtypeStruct((chunk, G2 * size), BF16)
    c_one, *sends = pl.pallas_call(
        functools.partial(near_kernel, slots, size, cols_n),
        out_shape=[jax.ShapeDtypeStruct((CB, NS, CB, size, size), BF16)] + [piece] * cols_n,
        in_specs=[SMEM] * 4 + [VMEM] * 9,
        out_specs=[VMEM] * (1 + cols_n),
        scratch_shapes=[
            pltpu.VMEM(((NS - 1) * FB + 1, size, wide), F32),
            pltpu.VMEM((3 * G2 * size, G2 * size), F32),
            pltpu.VMEM((8, size), jnp.int32),
            pltpu.SMEM((8, size), jnp.int32),
            pltpu.SMEM((NS, PB + 1), jnp.int32),
            pltpu.SemaphoreType.DMA,
        ],
        compiler_params=LARGE,
        name="near_sources",
    )(
        fine_rows[0, 0], fine_cols[0, 0], order, bounds, fine_blocks[0, 0],
        turned, coarse0, half0, lift_t, left, right, up, down,
    )
    parts = [sends[0]] + [shift(sends[d], "col", d, True) for d in range(1, cols_n)]
    total = pl.pallas_call(
        sum_kernel, out_shape=piece, in_specs=[VMEM] * cols_n, out_specs=VMEM,
        compiler_params=SMALL, name="total"
    )(*parts)
    gathered = [total] + [shift(total, "col", d, True) for d in range(1, cols_n)]
    c_two = pl.pallas_call(
        functools.partial(spread_kernel, size, cols_n),
        out_shape=jax.ShapeDtypeStruct((G2, 3, G2, size, size), F32),
        in_specs=[VMEM] * cols_n,
        out_specs=VMEM,
        compiler_params=SMALL,
        name="spread",
    )(*gathered)
    return (c_one[None, None], c_two[None])


def solution(mesh):
    in_specs = (
        P("row", "col", None, None, None),
        P("row", "col", None),
        P("row", "col", None),
        P("row", "col"),
        P("row", "col", None, None, None),
        P("row", "col", None),
        P("row", "col"),
        P("row", "col", None, None, None),
        P("row", "col", None),
    )
    out_specs = (
        P("row", "col", None, None, None, None, None),
        P("row", None, None, None, None, None),
    )
    return jax.shard_map(
        per_device, mesh=mesh, in_specs=in_specs, out_specs=out_specs, check_vma=False
    )
```

```python
import functools
import math

import jax
import jax.numpy as jnp
from jax import lax
from jax.experimental import pallas as pl
from jax.experimental.pallas import tpu as pltpu
from jax.sharding import PartitionSpec as P

FB = 8
CB = 2
G2 = 2
NS = 5
PB = FB * CB
UNROLL = 4
META = 16
F32 = jnp.float32
BF16 = jnp.bfloat16

VMEM = pl.BlockSpec(memory_space=pltpu.VMEM)
SMEM = pl.BlockSpec(memory_space=pltpu.SMEM)
ANY = pl.BlockSpec(memory_space=pl.ANY)
SMALL = pltpu.CompilerParams(vmem_limit_bytes=4 * 1024 * 1024)
LARGE = pltpu.CompilerParams(vmem_limit_bytes=20 * 1024 * 1024)


def pack_kernel(codes, count, aggs, blocks, second, out, held, sems):
    n_p, n_s = blocks.shape[0], second.shape[0]
    slots = codes.shape[0]
    first = pltpu.make_async_copy(blocks, held.at[0:n_p], sems.at[0])
    after = pltpu.make_async_copy(second, held.at[n_p : n_p + n_s], sems.at[1])
    first.start()
    after.start()
    lane = lax.broadcasted_iota(jnp.int32, (META, out.shape[1]), 1)
    word = jnp.zeros(lane.shape, jnp.int32)
    for k in range(slots):
        word = jnp.where(lane == k, jnp.where(k < count[0], codes[k], PB), word)
    for j in range(CB):
        word = jnp.where(lane == slots + j, aggs[j], word)
    held[n_p + n_s : n_p + n_s + META, :] = word.astype(F32).astype(BF16)
    first.wait()
    after.wait()
    whole = pltpu.make_async_copy(held, out, sems.at[2])
    whole.start()
    whole.wait()


def slot_products(s, size, table, rows, cols, order, begin, end, fine, near, acc, base):
    def step(t, carry):
        products, targets = [], []
        for u in range(UNROLL):
            at = begin + t * UNROLL + u
            live = at < end
            k = order[jnp.minimum(at, end - 1)]
            m = cols[k] - s * FB
            parts = []
            for j in range(CB):
                slot = table[s, m * CB + j]
                first = pl.multiple_of(jnp.maximum(slot, 0) * size, size)
                block = near[pl.ds(first, size), :]
                parts.append(jnp.where(slot >= 0, block, jnp.zeros_like(block)))
            wide = jnp.concatenate(parts, axis=1)
            products.append(jnp.dot(fine[k], wide, preferred_element_type=F32))
            targets.append(jnp.where(live, base + rows[k], acc.shape[0] - 1))
        for u in range(UNROLL):
            acc[targets[u]] += products[u]
        return carry

    lax.fori_loop(0, (end - begin + UNROLL - 1) // UNROLL, step, 0)


def fill_table(s, slots, table, code_of):
    for q in range(PB + 1):
        table[s, q] = -1
    for k in range(slots):
        table[s, code_of(k)] = k


def lift_of(near, slots, size, agg_of):
    lines = []
    for j in range(CB):
        block = near[(slots + j) * size : (slots + j + 1) * size, :]
        lines.append(
            jnp.concatenate(
                [jnp.where(agg_of(j) == a, block, jnp.zeros_like(block)) for a in range(G2)],
                axis=1,
            )
        )
    return jnp.concatenate(lines, axis=0)


def coarse_of(turned, acc, base, size):
    product = acc[base : base + FB].reshape(FB * size, CB * size).astype(BF16)
    return jnp.dot(turned, product, preferred_element_type=F32).astype(BF16)


def own_kernel(
    slots, size, rows, cols, count, codes, p_count, aggs, fine, own,
    turned, coarse, half, lift_t, order, bounds, acc, table, fill,
):
    total = order.shape[0]
    for s in range(NS):
        fill[s] = 0

    def tally(k, carry):
        s = cols[k] // FB
        fill[s] += 1
        return carry

    lax.fori_loop(0, count[0], tally, 0)
    at = jnp.int32(0)
    for s in range(NS):
        n = fill[s]
        bounds[s] = at
        fill[s] = at
        at = at + n
    bounds[NS] = at

    def place(k, carry):
        s = cols[k] // FB
        order[fill[s]] = k
        fill[s] += 1
        return carry

    lax.fori_loop(0, count[0], place, 0)
    fill_table(0, slots, table, lambda k: jnp.where(k < p_count[0], codes[k], PB))
    for i in range(FB):
        for j in range(CB):
            slot = table[0, i * CB + j]
            block = own[pl.ds(pl.multiple_of(jnp.maximum(slot, 0) * size, size), size), :]
            block = jnp.where(slot >= 0, block, jnp.zeros_like(block))
            turned[j * size : (j + 1) * size, i * size : (i + 1) * size] = block.T
    acc[...] = jnp.zeros_like(acc)
    slot_products(0, size, table, rows, cols, order, 0, bounds[1], fine, own, acc, 0)
    coarse[...] = coarse_of(turned[...], acc, 0, size)
    lift = lift_of(own, slots, size, lambda j: aggs[j])
    half[...] = jnp.dot(coarse[...], lift, preferred_element_type=F32)
    lift_t[...] = lift.T


def near_kernel(
    slots, size, cols_n, rows, cols, order, bounds, fine, turned, coarse0, half0, lift_t,
    left, right, up, down, c_one, sends, acc, terms, words, codes, table, sem,
):
    near = (None, left, right, up, down)
    tail = (slots + CB) * size
    for s in range(1, NS):
        word = near[s][tail : tail + META, :].astype(F32).astype(jnp.int32)
        words[s : s + 1, :] = word[0:1, :]
    fetch = pltpu.make_async_copy(words, codes, sem)
    fetch.start()
    acc[...] = jnp.zeros_like(acc)
    fetch.wait()
    halves = [half0[...], None, None]
    for s in range(NS):
        if s == 0:
            coarse = coarse0[...]
        else:
            fill_table(s, slots, table, lambda k: codes[s, k])
            base = (s - 1) * FB
            slot_products(
                s, size, table, rows, cols, order, bounds[s], bounds[s + 1], fine, near[s], acc, base
            )
            coarse = coarse_of(turned[...], acc, base, size)
            lift = lift_of(near[s], slots, size, lambda j: codes[s, slots + j])
            part = jnp.dot(coarse, lift, preferred_element_type=F32)
            g = 0 if s < 3 else s - 2
            halves[g] = part if halves[g] is None else halves[g] + part
        for i in range(CB):
            for j in range(CB):
                c_one[i, s, j] = coarse[i * size : (i + 1) * size, j * size : (j + 1) * size]
    for g in range(3):
        terms[g * G2 * size : (g + 1) * G2 * size, :] = jnp.dot(
            lift_t[...], halves[g].astype(BF16), preferred_element_type=F32
        )
    chunk = terms.shape[0] // cols_n
    for to in range(cols_n):
        sends[to] = terms[to * chunk : (to + 1) * chunk, :].astype(BF16)


def sum_kernel(parts, out):
    total = parts[0].astype(F32)
    for c in range(1, parts.shape[0]):
        total = total + parts[c].astype(F32)
    for c in range(parts.shape[0]):
        out[c] = total.astype(BF16)


def spread_kernel(size, parts, out):
    chunk = parts.shape[1]
    unit = math.gcd(chunk, size)
    per = size // unit
    for owner in range(parts.shape[0]):
        for t in range(chunk // unit):
            at = owner * (chunk // unit) + t
            g, a, h = at // (G2 * per), at // per % G2, at % per * unit
            for b in range(G2):
                out[a, g, b, h : h + unit, :] = parts[
                    owner, t * unit : (t + 1) * unit, b * size : (b + 1) * size
                ].astype(F32)


def shift(x, axis, step, wrap):
    n = lax.axis_size(axis)
    pairs = [(i, (i + step) % n) for i in range(n) if wrap or 0 <= i + step < n]
    return lax.ppermute(x, axis, pairs)


def per_device(
    fine_blocks, fine_rows, fine_cols, fine_counts, prolong_blocks, prolong_codes,
    prolong_counts, second_blocks, second_aggs,
):
    slots, size = prolong_blocks.shape[2], prolong_blocks.shape[3]
    cols_n = lax.axis_size("col")
    packed_rows = (slots + CB) * size + META
    grid_slots = fine_blocks.shape[2]
    wide = CB * size
    packed = pl.pallas_call(
        pack_kernel,
        out_shape=jax.ShapeDtypeStruct((packed_rows, size), BF16),
        in_specs=[SMEM] * 3 + [ANY] * 2,
        out_specs=ANY,
        scratch_shapes=[pltpu.VMEM((packed_rows, size), BF16), pltpu.SemaphoreType.DMA((3,))],
        compiler_params=pltpu.CompilerParams(vmem_limit_bytes=60 * 1024 * 1024),
        name="pack",
    )(
        prolong_codes[0, 0],
        prolong_counts[0],
        second_aggs[0, 0],
        prolong_blocks.reshape(slots * size, size),
        second_blocks.reshape(CB * size, size),
    )
    up = shift(packed, "row", 1, False)
    down = shift(packed, "row", -1, False)
    left = shift(packed, "col", 1, False)
    right = shift(packed, "col", -1, False)

    turned, coarse0, half0, lift_t, order, bounds = pl.pallas_call(
        functools.partial(own_kernel, slots, size),
        out_shape=[
            jax.ShapeDtypeStruct((wide, FB * size), BF16),
            jax.ShapeDtypeStruct((wide, wide), BF16),
            jax.ShapeDtypeStruct((wide, G2 * size), F32),
            jax.ShapeDtypeStruct((G2 * size, wide), BF16),
            jax.ShapeDtypeStruct((grid_slots,), jnp.int32),
            jax.ShapeDtypeStruct((8,), jnp.int32),
        ],
        in_specs=[SMEM] * 6 + [VMEM] * 2,
        out_specs=[VMEM] * 4 + [SMEM] * 2,
        scratch_shapes=[
            pltpu.VMEM((FB + 1, size, wide), F32),
            pltpu.SMEM((NS, PB + 1), jnp.int32),
            pltpu.SMEM((8,), jnp.int32),
        ],
        compiler_params=LARGE,
        cost_estimate=pl.CostEstimate(flops=10**9, bytes_accessed=4 * 10**6, transcendentals=0),
        name="own_source",
    )(
        fine_rows[0, 0], fine_cols[0, 0], fine_counts[0],
        prolong_codes[0, 0], prolong_counts[0], second_aggs[0, 0],
        fine_blocks[0, 0], packed,
    )

    chunk = 3 * G2 * size // cols_n
    pieces = jax.ShapeDtypeStruct((cols_n, chunk, G2 * size), BF16)
    c_one, sends = pl.pallas_call(
        functools.partial(near_kernel, slots, size, cols_n),
        out_shape=[jax.ShapeDtypeStruct((CB, NS, CB, size, size), BF16), pieces],
        in_specs=[SMEM] * 4 + [VMEM] * 9,
        out_specs=[VMEM] * 2,
        scratch_shapes=[
            pltpu.VMEM(((NS - 1) * FB + 1, size, wide), F32),
            pltpu.VMEM((3 * G2 * size, G2 * size), F32),
            pltpu.VMEM((8, size), jnp.int32),
            pltpu.SMEM((8, size), jnp.int32),
            pltpu.SMEM((NS, PB + 1), jnp.int32),
            pltpu.SemaphoreType.DMA,
        ],
        compiler_params=LARGE,
        name="near_sources",
    )(
        fine_rows[0, 0], fine_cols[0, 0], order, bounds, fine_blocks[0, 0],
        turned, coarse0, half0, lift_t, left, right, up, down,
    )
    parts = lax.all_to_all(sends, "col", 0, 0)
    total = pl.pallas_call(
        sum_kernel, out_shape=pieces, in_specs=[VMEM], out_specs=VMEM,
        compiler_params=SMALL, name="total",
    )(parts)
    gathered = lax.all_to_all(total, "col", 0, 0)
    c_two = pl.pallas_call(
        functools.partial(spread_kernel, size),
        out_shape=jax.ShapeDtypeStruct((G2, 3, G2, size, size), F32),
        in_specs=[VMEM],
        out_specs=VMEM,
        compiler_params=SMALL,
        name="spread",
    )(gathered)
    return (c_one[None, None], c_two[None])


def solution(mesh):
    in_specs = (
        P("row", "col", None, None, None),
        P("row", "col", None),
        P("row", "col", None),
        P("row", "col"),
        P("row", "col", None, None, None),
        P("row", "col", None),
        P("row", "col"),
        P("row", "col", None, None, None),
        P("row", "col", None),
    )
    out_specs = (
        P("row", "col", None, None, None, None, None),
        P("row", None, None, None, None, None),
    )
    return jax.shard_map(
        per_device, mesh=mesh, in_specs=in_specs, out_specs=out_specs, check_vma=False
    )
```

```python
import functools
import math

import jax
import jax.numpy as jnp
from jax import lax
from jax.experimental import pallas as pl
from jax.experimental.pallas import tpu as pltpu
from jax.sharding import PartitionSpec as P

FB = 8
CB = 2
G2 = 2
NS = 5
PB = FB * CB
UNROLL = 4
META = 16
F32 = jnp.float32
BF16 = jnp.bfloat16

VMEM = pl.BlockSpec(memory_space=pltpu.VMEM)
SMEM = pl.BlockSpec(memory_space=pltpu.SMEM)
ANY = pl.BlockSpec(memory_space=pl.ANY)
SMALL = pltpu.CompilerParams(vmem_limit_bytes=4 * 1024 * 1024)
LARGE = pltpu.CompilerParams(vmem_limit_bytes=20 * 1024 * 1024)


def pack_kernel(
    codes, count, aggs, rows, cols, f_count, blocks, second, out, ints, held, sems
):
    n_p, n_s = blocks.shape[0], second.shape[0]
    slots = codes.shape[0]
    first = pltpu.make_async_copy(blocks, held.at[0:n_p], sems.at[0])
    after = pltpu.make_async_copy(second, held.at[n_p : n_p + n_s], sems.at[1])
    first.start()
    after.start()
    lane = lax.broadcasted_iota(jnp.int32, (META, out.shape[1]), 1)
    word = jnp.zeros(lane.shape, jnp.int32)
    for k in range(slots):
        word = jnp.where(lane == k, jnp.where(k < count[0], codes[k], PB), word)
    for j in range(CB):
        word = jnp.where(lane == slots + j, aggs[j], word)
    held[n_p + n_s : n_p + n_s + META, :] = word.astype(F32).astype(BF16)
    first.wait()
    after.wait()
    whole = pltpu.make_async_copy(held, out, sems.at[2])
    whole.start()
    cap = cols.shape[0]
    for k in range(cap):
        ints[k] = cols[k]
        ints[cap + k] = rows[k]
    for k in range(slots):
        ints[2 * cap + k] = jnp.where(k < count[0], codes[k], PB)
    for j in range(CB):
        ints[2 * cap + slots + j] = aggs[j]
    ints[2 * cap + slots + CB] = f_count[0]
    whole.wait()


def slot_products(s, size, table, plan, cap, fine, near, acc, base):
    begin, end = plan[3 * cap + s], plan[3 * cap + s + 1]

    def step(t, carry):
        products, targets = [], []
        for u in range(UNROLL):
            at = begin + t * UNROLL + u
            live = at < end
            at = jnp.minimum(at, end - 1)
            m = plan[cap + at] - s * FB
            parts = []
            for j in range(CB):
                slot = table[s, m * CB + j]
                first = pl.multiple_of(jnp.maximum(slot, 0) * size, size)
                block = near[pl.ds(first, size), :]
                parts.append(jnp.where(slot >= 0, block, jnp.zeros_like(block)))
            wide = jnp.concatenate(parts, axis=1)
            products.append(jnp.dot(fine[plan[at]], wide, preferred_element_type=F32))
            targets.append(jnp.where(live, base + plan[2 * cap + at], acc.shape[0] - 1))
        for u in range(UNROLL):
            acc[targets[u]] += products[u]
        return carry

    lax.fori_loop(0, (end - begin + UNROLL - 1) // UNROLL, step, 0)


def fill_table(s, slots, table, code_of):
    for q in range(PB + 1):
        table[s, q] = -1
    for k in range(slots):
        table[s, code_of(k)] = k


def lift_of(near, slots, size, agg_of):
    lines = []
    for j in range(CB):
        block = near[(slots + j) * size : (slots + j + 1) * size, :]
        lines.append(
            jnp.concatenate(
                [jnp.where(agg_of(j) == a, block, jnp.zeros_like(block)) for a in range(G2)],
                axis=1,
            )
        )
    return jnp.concatenate(lines, axis=0)


def coarse_of(turned, acc, base, size, tile):
    product = acc[base : base + FB].reshape(FB * size, CB * size).astype(BF16)
    coarse = jnp.dot(turned, product, preferred_element_type=F32).astype(BF16)
    for i in range(CB):
        for j in range(CB):
            tile[i, j] = coarse[i * size : (i + 1) * size, j * size : (j + 1) * size]
    return coarse


def own_kernel(
    slots, size, ints, fine, own, turned, half, lift_t, plan, c_one, acc, tile, table, fill, sem
):
    cap = fine.shape[0]
    count = ints[2 * cap + slots + CB]
    for s in range(NS):
        fill[s] = 0

    def tally(k, carry):
        fill[ints[k] // FB] += 1
        return carry

    lax.fori_loop(0, count, tally, 0)
    at = jnp.int32(0)
    for s in range(NS):
        n = fill[s]
        plan[3 * cap + s] = at
        fill[s] = at
        at = at + n
    plan[3 * cap + NS] = at

    def place(k, carry):
        col = ints[k]
        s = col // FB
        to = fill[s]
        plan[to] = k
        plan[cap + to] = col
        plan[2 * cap + to] = ints[cap + k]
        fill[s] = to + 1
        return carry

    lax.fori_loop(0, count, place, 0)
    fill_table(0, slots, table, lambda k: ints[2 * cap + k])
    acc[...] = jnp.zeros_like(acc)
    for i in range(FB):
        for j in range(CB):
            slot = table[0, i * CB + j]
            block = own[pl.ds(pl.multiple_of(jnp.maximum(slot, 0) * size, size), size), :]
            block = jnp.where(slot >= 0, block, jnp.zeros_like(block))
            turned[j * size : (j + 1) * size, i * size : (i + 1) * size] = block.T
    slot_products(0, size, table, plan, cap, fine, own, acc, 0)
    coarse = coarse_of(turned[...], acc, 0, size, tile)
    store = pltpu.make_async_copy(tile, c_one.at[:, 0], sem)
    store.start()
    lift = lift_of(own, slots, size, lambda j: ints[2 * cap + slots + j])
    half[...] = jnp.dot(coarse, lift, preferred_element_type=F32)
    lift_t[...] = lift.T
    store.wait()


def near_coarse(sources, near, slots, size, plan, fine, turned, c_one, acc, tiles, words, codes, table, sems):
    cap = fine.shape[0]
    tail = (slots + CB) * size
    for s, ref in zip(sources, near):
        word = ref[tail : tail + META, :].astype(F32).astype(jnp.int32)
        words[s : s + 1, :] = word[0:1, :]
    fetch = pltpu.make_async_copy(words, codes, sems.at[0])
    fetch.start()
    acc[...] = jnp.zeros_like(acc)
    fetch.wait()
    parts, stores = [], []
    for n, (s, ref) in enumerate(zip(sources, near)):
        fill_table(s, slots, table, lambda k: codes[s, k])
        slot_products(s, size, table, plan, cap, fine, ref, acc, n * FB)
        coarse = coarse_of(turned[...], acc, n * FB, size, tiles.at[n])
        store = pltpu.make_async_copy(tiles.at[n], c_one.at[:, s], sems.at[1 + n])
        store.start()
        stores.append(store)
        lift = lift_of(ref, slots, size, lambda j: codes[s, slots + j])
        parts.append(jnp.dot(coarse, lift, preferred_element_type=F32))
    return parts, stores


def side_kernel(slots, size, plan, fine, turned, half, lift_t, left, right, c_in, c_one, term, *scratch):
    parts, stores = near_coarse((1, 2), (left, right), slots, size, plan, fine, turned, c_one, *scratch)
    whole = (half[...] + parts[0] + parts[1]).astype(BF16)
    term[...] = jnp.dot(lift_t[...], whole, preferred_element_type=F32)
    for store in stores:
        store.wait()


def row_kernel(slots, size, cols_n, plan, fine, turned, term, lift_t, up, down, c_in, c_one, *rest):
    sends, terms, scratch = rest[:cols_n], rest[cols_n], rest[cols_n + 1 :]
    parts, stores = near_coarse((3, 4), (up, down), slots, size, plan, fine, turned, c_one, *scratch)
    terms[0] = term[...]
    for g in range(2):
        terms[1 + g] = jnp.dot(lift_t[...], parts[g].astype(BF16), preferred_element_type=F32)
    chunk = terms.shape[1] // cols_n
    me = lax.axis_index("col")
    for d in range(cols_n):
        to = pl.multiple_of(lax.rem(me + d, cols_n) * chunk, chunk)
        for g in range(3):
            sends[d][g] = terms[g, pl.ds(to, chunk), :].astype(BF16)
    for store in stores:
        store.wait()


def sum_kernel(*refs):
    total = refs[0][...].astype(F32)
    for ref in refs[1:-1]:
        total = total + ref[...].astype(F32)
    refs[-1][...] = total.astype(BF16)


def spread_kernel(size, cols_n, *refs):
    out = refs[-1]
    chunk = refs[0].shape[1]
    unit = math.gcd(chunk, size)
    per = size // unit
    me = lax.axis_index("col")
    for d in range(cols_n):
        owner = lax.rem(me - d + cols_n, cols_n)
        for t in range(chunk // unit):
            at = owner * (chunk // unit) + t
            a = at // per
            h = pl.multiple_of(lax.rem(at, per) * unit, unit)
            for g in range(3):
                for b in range(G2):
                    out[a, g, b, pl.ds(h, unit), :] = refs[d][
                        g, t * unit : (t + 1) * unit, b * size : (b + 1) * size
                    ].astype(F32)


def shift(x, axis, step, wrap):
    n = lax.axis_size(axis)
    pairs = [(i, (i + step) % n) for i in range(n) if wrap or 0 <= i + step < n]
    return lax.ppermute(x, axis, pairs)


def per_device(
    fine_blocks, fine_rows, fine_cols, fine_counts, prolong_blocks, prolong_codes,
    prolong_counts, second_blocks, second_aggs,
):
    slots, size = prolong_blocks.shape[2], prolong_blocks.shape[3]
    cols_n = lax.axis_size("col")
    packed_rows = (slots + CB) * size + META
    grid_slots = fine_blocks.shape[2]
    wide = CB * size
    packed, ints = pl.pallas_call(
        pack_kernel,
        out_shape=[
            jax.ShapeDtypeStruct((packed_rows, size), BF16),
            jax.ShapeDtypeStruct((2 * grid_slots + slots + CB + 2,), jnp.int32),
        ],
        in_specs=[SMEM] * 6 + [ANY] * 2,
        out_specs=[ANY, SMEM],
        scratch_shapes=[pltpu.VMEM((packed_rows, size), BF16), pltpu.SemaphoreType.DMA((3,))],
        compiler_params=pltpu.CompilerParams(vmem_limit_bytes=60 * 1024 * 1024),
        name="pack",
    )(
        prolong_codes[0, 0],
        prolong_counts[0],
        second_aggs[0, 0],
        fine_rows[0, 0],
        fine_cols[0, 0],
        fine_counts[0],
        prolong_blocks.reshape(slots * size, size),
        second_blocks.reshape(CB * size, size),
    )
    up = shift(packed, "row", 1, False)
    down = shift(packed, "row", -1, False)
    left = shift(packed, "col", 1, False)
    right = shift(packed, "col", -1, False)

    c_shape = jax.ShapeDtypeStruct((CB, NS, CB, size, size), BF16)
    square = jax.ShapeDtypeStruct((wide, G2 * size), F32)
    table = pltpu.SMEM((NS, PB + 1), jnp.int32)
    turned, half, lift_t, plan, c_one = pl.pallas_call(
        functools.partial(own_kernel, slots, size),
        out_shape=[
            jax.ShapeDtypeStruct((wide, FB * size), BF16),
            square,
            jax.ShapeDtypeStruct((G2 * size, wide), BF16),
            jax.ShapeDtypeStruct((3 * grid_slots + 8,), jnp.int32),
            c_shape,
        ],
        in_specs=[SMEM] + [VMEM] * 2,
        out_specs=[VMEM] * 3 + [SMEM, ANY],
        scratch_shapes=[
            pltpu.VMEM((FB + 1, size, wide), F32),
            pltpu.VMEM((CB, CB, size, size), BF16),
            table,
            pltpu.SMEM((8,), jnp.int32),
            pltpu.SemaphoreType.DMA,
        ],
        compiler_params=LARGE,
        cost_estimate=pl.CostEstimate(flops=10**9, bytes_accessed=4 * 10**6, transcendentals=0),
        name="own_source",
    )(ints, fine_blocks[0, 0], packed)

    near_scratch = [
        pltpu.VMEM((2 * FB + 1, size, wide), F32),
        pltpu.VMEM((2, CB, CB, size, size), BF16),
        pltpu.VMEM((8, size), jnp.int32),
        pltpu.SMEM((8, size), jnp.int32),
        table,
        pltpu.SemaphoreType.DMA((3,)),
    ]
    c_one, term = pl.pallas_call(
        functools.partial(side_kernel, slots, size),
        out_shape=[c_shape, square],
        in_specs=[SMEM] + [VMEM] * 6 + [ANY],
        out_specs=[ANY, VMEM],
        input_output_aliases={7: 0},
        scratch_shapes=near_scratch,
        compiler_params=LARGE,
        name="col_sources",
    )(plan, fine_blocks[0, 0], turned, half, lift_t, left, right, c_one)

    chunk = G2 * size // cols_n
    piece = jax.ShapeDtypeStruct((3, chunk, G2 * size), BF16)
    c_one, *sends = pl.pallas_call(
        functools.partial(row_kernel, slots, size, cols_n),
        out_shape=[c_shape] + [piece] * cols_n,
        in_specs=[SMEM] + [VMEM] * 6 + [ANY],
        out_specs=[ANY] + [VMEM] * cols_n,
        input_output_aliases={7: 0},
        scratch_shapes=[pltpu.VMEM((3, G2 * size, G2 * size), F32)] + near_scratch,
        compiler_params=LARGE,
        name="row_sources",
    )(plan, fine_blocks[0, 0], turned, term, lift_t, up, down, c_one)

    parts = [sends[0]] + [shift(sends[d], "col", d, True) for d in range(1, cols_n)]
    total = pl.pallas_call(
        sum_kernel, out_shape=piece, in_specs=[VMEM] * cols_n, out_specs=VMEM,
        compiler_params=SMALL, name="total",
    )(*parts)
    gathered = [total] + [shift(total, "col", d, True) for d in range(1, cols_n)]
    c_two = pl.pallas_call(
        functools.partial(spread_kernel, size, cols_n),
        out_shape=jax.ShapeDtypeStruct((G2, 3, G2, size, size), F32),
        in_specs=[VMEM] * cols_n,
        out_specs=VMEM,
        compiler_params=SMALL,
        name="spread",
    )(*gathered)
    return (c_one[None, None], c_two[None])


def solution(mesh):
    in_specs = (
        P("row", "col", None, None, None),
        P("row", "col", None),
        P("row", "col", None),
        P("row", "col"),
        P("row", "col", None, None, None),
        P("row", "col", None),
        P("row", "col"),
        P("row", "col", None, None, None),
        P("row", "col", None),
    )
    out_specs = (
        P("row", "col", None, None, None, None, None),
        P("row", None, None, None, None, None),
    )
    return jax.shard_map(
        per_device, mesh=mesh, in_specs=in_specs, out_specs=out_specs, check_vma=False
    )
```

```python
import functools
import math

import jax
import jax.numpy as jnp
from jax import lax
from jax.experimental import pallas as pl
from jax.experimental.pallas import tpu as pltpu
from jax.sharding import PartitionSpec as P

FB = 8
CB = 2
G2 = 2
NS = 5
PB = FB * CB
UNROLL = 4
META = 16
F32 = jnp.float32
BF16 = jnp.bfloat16

VMEM = pl.BlockSpec(memory_space=pltpu.VMEM)
HBM = pl.BlockSpec(memory_space=pltpu.HBM)
SMALL = pltpu.CompilerParams(vmem_limit_bytes=4 * 1024 * 1024)
SMEM = pl.BlockSpec(memory_space=pltpu.SMEM)
LARGE = pltpu.CompilerParams(vmem_limit_bytes=20 * 1024 * 1024)
WHOLE = pltpu.CompilerParams(vmem_limit_bytes=60 * 1024 * 1024)


def pack_kernel(
    codes, count, aggs, rows, cols, f_count, blocks, second, out, ints, held, sems
):
    n_p, n_s = blocks.shape[0], second.shape[0]
    slots, cap = codes.shape[0], cols.shape[0]
    copies = [
        pltpu.make_async_copy(blocks, held.at[0:n_p], sems.at[0]),
        pltpu.make_async_copy(second, held.at[n_p : n_p + n_s], sems.at[1]),
    ]
    for copy in copies:
        copy.start()
    lane = lax.broadcasted_iota(jnp.int32, (META, out.shape[1]), 1)
    word = jnp.zeros(lane.shape, jnp.int32)
    for k in range(slots):
        code = jnp.where(k < count[0], codes[k], PB)
        ints[cap + k] = code
        word = jnp.where(lane == k, code, word)
    for j in range(CB):
        ints[cap + slots + j] = aggs[j]
        word = jnp.where(lane == slots + j, aggs[j], word)
    ints[cap + slots + CB] = f_count[0]
    held[n_p + n_s : n_p + n_s + META, :] = word.astype(F32).astype(BF16)
    for copy in copies:
        copy.wait()
    whole = pltpu.make_async_copy(held, out, sems.at[2])
    whole.start()
    for k in range(cap):
        ints[k] = cols[k] * FB + rows[k]
    whole.wait()


def fill_table(s, slots, table, code_of):
    for q in range(PB + 1):
        table[s, q] = -1
    for k in range(slots):
        table[s, code_of(k)] = k


def block_at(s, q, size, table, near):
    slot = table[s, q]
    block = near[pl.ds(pl.multiple_of(jnp.maximum(slot, 0) * size, size), size), :]
    return jnp.where(slot >= 0, block, jnp.zeros_like(block))


def lift_of(near, slots, size, agg_of):
    lines = []
    for j in range(CB):
        block = near[(slots + j) * size : (slots + j + 1) * size, :]
        lines.append(
            jnp.concatenate(
                [jnp.where(agg_of(j) == a, block, jnp.zeros_like(block)) for a in range(G2)],
                axis=1,
            )
        )
    return jnp.concatenate(lines, axis=0)


def dense_of(s, size, table, near, dense):
    for i in range(FB):
        for j in range(CB):
            dense[i * size : (i + 1) * size, j * size : (j + 1) * size] = block_at(
                s, i * CB + j, size, table, near
            )


def coarse_of(size, weight, dense, tile):
    coarse = jnp.dot(weight, dense[...], preferred_element_type=F32).astype(BF16)
    for i in range(CB):
        for j in range(CB):
            tile[i, j] = coarse[i * size : (i + 1) * size, j * size : (j + 1) * size]
    return coarse


def own_kernel(
    slots, size, ints, fine, own, weights, half, lift_t, c_one, turned, acc, dense, tile, table, sem
):
    acc[...] = jnp.zeros_like(acc)
    cap = fine.shape[0]
    fill_table(0, slots, table, lambda k: ints[cap + k])
    for i in range(FB):
        for j in range(CB):
            block = block_at(0, i * CB + j, size, table, own)
            turned[i, j * size : (j + 1) * size, :] = block.T
    count = ints[cap + slots + CB]

    def step(t, carry):
        products, targets = [], []
        for u in range(UNROLL):
            k = t * UNROLL + u
            at = jnp.where(k < count, ints[k], NS * FB * FB)
            col = at // FB
            products.append(jnp.dot(turned[at - col * FB], fine[k], preferred_element_type=F32))
            targets.append(col)
        for u in range(UNROLL):
            acc[targets[u]] += products[u]
        return carry

    lax.fori_loop(0, (count + UNROLL - 1) // UNROLL, step, 0)
    own_weight = jnp.concatenate([acc[m].astype(BF16) for m in range(FB)], axis=1)
    dense_of(0, size, table, own, dense)
    coarse = coarse_of(size, own_weight, dense, tile)
    store = pltpu.make_async_copy(tile, c_one.at[:, 0], sem)
    store.start()
    for s in range(1, NS):
        for m in range(FB):
            weights[s - 1, :, m * size : (m + 1) * size] = acc[s * FB + m].astype(BF16)
    lift = lift_of(own, slots, size, lambda j: ints[cap + slots + j])
    half[...] = jnp.dot(coarse, lift, preferred_element_type=F32)
    lift_t[...] = lift.T
    store.wait()


def near_coarse(
    sources, near, slots, size, weights, c_one, dense, tiles, words, codes, table, sems
):
    tail = (slots + CB) * size
    for n, ref in enumerate(near):
        word = ref[tail : tail + META, :].astype(F32).astype(jnp.int32)
        words[n : n + 1, :] = word[0:1, :]
    fetch = pltpu.make_async_copy(words, codes, sems.at[0])
    fetch.start()
    fetch.wait()
    parts, stores = [], []
    for n, (s, ref) in enumerate(zip(sources, near)):
        fill_table(n, slots, table, lambda k: codes[n, k])
        dense_of(n, size, table, ref, dense.at[n])
        coarse = coarse_of(size, weights[s - 1], dense.at[n], tiles.at[n])
        store = pltpu.make_async_copy(tiles.at[n], c_one.at[:, s], sems.at[1 + n])
        store.start()
        stores.append(store)
        lift = lift_of(ref, slots, size, lambda j: codes[n, slots + j])
        parts.append(jnp.dot(coarse, lift, preferred_element_type=F32))
    return parts, stores


def side_kernel(slots, size, weights, half, lift_t, left, right, c_in, c_one, term, *scratch):
    parts, stores = near_coarse((1, 2), (left, right), slots, size, weights, c_one, *scratch)
    whole = (half[...] + parts[0] + parts[1]).astype(BF16)
    term[...] = jnp.dot(lift_t[...], whole, preferred_element_type=F32)
    for store in stores:
        store.wait()


def row_kernel(slots, size, cols_n, weights, term, lift_t, up, down, c_in, c_one, *rest):
    sends, terms, scratch = rest[:cols_n], rest[cols_n], rest[cols_n + 1 :]
    parts, stores = near_coarse((3, 4), (up, down), slots, size, weights, c_one, *scratch)
    terms[0] = term[...]
    for g in range(2):
        terms[1 + g] = jnp.dot(lift_t[...], parts[g].astype(BF16), preferred_element_type=F32)
    chunk = terms.shape[1] // cols_n
    me = lax.axis_index("col")
    for d in range(cols_n):
        to = pl.multiple_of(lax.rem(me + d, cols_n) * chunk, chunk)
        sends[d][...] = terms[:, pl.ds(to, chunk), :].astype(sends[d].dtype)
    for store in stores:
        store.wait()


def sum_kernel(*refs):
    total = refs[0][...]
    for ref in refs[1:-1]:
        total = total + ref[...].astype(F32)
    refs[-1][...] = total.astype(BF16)


def spread_kernel(size, cols_n, *refs):
    out = refs[-1]
    chunk = refs[0].shape[1]
    unit = math.gcd(chunk, size)
    per = size // unit
    me = lax.axis_index("col")
    for d in range(cols_n):
        owner = lax.rem(me - d + cols_n, cols_n)
        for t in range(chunk // unit):
            at = owner * (chunk // unit) + t
            a = at // per
            h = pl.multiple_of(lax.rem(at, per) * unit, unit)
            for g in range(3):
                for b in range(G2):
                    out[a, g, b, pl.ds(h, unit), :] = refs[d][
                        g, t * unit : (t + 1) * unit, b * size : (b + 1) * size
                    ].astype(F32)


def shift(x, axis, step, wrap):
    n = lax.axis_size(axis)
    pairs = [(i, (i + step) % n) for i in range(n) if wrap or 0 <= i + step < n]
    return lax.ppermute(x, axis, pairs)


def per_device(
    fine_blocks, fine_rows, fine_cols, fine_counts, prolong_blocks, prolong_codes,
    prolong_counts, second_blocks, second_aggs,
):
    slots, size = prolong_blocks.shape[2], prolong_blocks.shape[3]
    cap = fine_blocks.shape[2]
    cols_n = lax.axis_size("col")
    packed_rows = (slots + CB) * size + META
    wide = CB * size
    dma = pltpu.SemaphoreType.DMA
    packed, ints = pl.pallas_call(
        pack_kernel,
        out_shape=[
            jax.ShapeDtypeStruct((packed_rows, size), BF16),
            jax.ShapeDtypeStruct((cap + slots + CB + 2,), jnp.int32),
        ],
        in_specs=[SMEM] * 6 + [HBM] * 2,
        out_specs=[HBM, SMEM],
        scratch_shapes=[
            pltpu.VMEM((packed_rows, size), BF16),
            dma((3,)),
        ],
        compiler_params=WHOLE,
        name="pack",
    )(
        prolong_codes[0, 0], prolong_counts[0], second_aggs[0, 0],
        fine_rows[0, 0], fine_cols[0, 0], fine_counts[0],
        prolong_blocks.reshape(slots * size, size),
        second_blocks.reshape(CB * size, size),
    )
    up = shift(packed, "row", 1, False)
    down = shift(packed, "row", -1, False)
    left = shift(packed, "col", 1, False)
    right = shift(packed, "col", -1, False)

    c_shape = jax.ShapeDtypeStruct((CB, NS, CB, size, size), BF16)
    table = pltpu.SMEM((NS, PB + 1), jnp.int32)
    weights, half, lift_t, c_one = pl.pallas_call(
        functools.partial(own_kernel, slots, size),
        out_shape=[
            jax.ShapeDtypeStruct((NS - 1, wide, FB * size), BF16),
            jax.ShapeDtypeStruct((wide, G2 * size), F32),
            jax.ShapeDtypeStruct((G2 * size, wide), BF16),
            c_shape,
        ],
        in_specs=[SMEM, VMEM, VMEM],
        out_specs=[VMEM] * 3 + [HBM],
        scratch_shapes=[
            pltpu.VMEM((FB, wide, size), BF16),
            pltpu.VMEM((NS * FB + 1, wide, size), F32),
            pltpu.VMEM((FB * size, wide), BF16),
            pltpu.VMEM((CB, CB, size, size), BF16),
            table,
            dma,
        ],
        compiler_params=LARGE,
        cost_estimate=pl.CostEstimate(flops=10**9, bytes_accessed=4 * 10**6, transcendentals=0),
        name="own_source",
    )(ints, fine_blocks[0, 0], packed)

    near_scratch = [
        pltpu.VMEM((2, FB * size, wide), BF16),
        pltpu.VMEM((2, CB, CB, size, size), BF16),
        pltpu.VMEM((8, size), jnp.int32),
        pltpu.SMEM((8, size), jnp.int32),
        table,
        dma((3,)),
    ]
    square = jax.ShapeDtypeStruct((wide, G2 * size), F32)
    c_one, term = pl.pallas_call(
        functools.partial(side_kernel, slots, size),
        out_shape=[c_shape, square],
        in_specs=[VMEM] * 5 + [HBM],
        out_specs=[HBM, VMEM],
        input_output_aliases={5: 0},
        scratch_shapes=near_scratch,
        compiler_params=LARGE,
        name="col_sources",
    )(weights, half, lift_t, left, right, c_one)

    chunk = G2 * size // cols_n
    kept = jax.ShapeDtypeStruct((3, chunk, G2 * size), F32)
    piece = jax.ShapeDtypeStruct(kept.shape, BF16)
    c_one, *sends = pl.pallas_call(
        functools.partial(row_kernel, slots, size, cols_n),
        out_shape=[c_shape, kept] + [piece] * (cols_n - 1),
        in_specs=[VMEM] * 5 + [HBM],
        out_specs=[HBM] + [VMEM] * cols_n,
        input_output_aliases={5: 0},
        scratch_shapes=[pltpu.VMEM((3, G2 * size, G2 * size), F32)] + near_scratch,
        compiler_params=LARGE,
        name="row_sources",
    )(weights, term, lift_t, up, down, c_one)
    parts = [sends[0]] + [shift(sends[d], "col", d, True) for d in range(1, cols_n)]
    total = pl.pallas_call(
        sum_kernel, out_shape=piece, in_specs=[VMEM] * cols_n, out_specs=VMEM,
        compiler_params=SMALL, name="total",
    )(*parts)
    gathered = [total] + [shift(total, "col", d, True) for d in range(1, cols_n)]
    c_two = pl.pallas_call(
        functools.partial(spread_kernel, size, cols_n),
        out_shape=jax.ShapeDtypeStruct((G2, 3, G2, size, size), F32),
        in_specs=[VMEM] * cols_n,
        out_specs=VMEM,
        compiler_params=SMALL,
        name="spread",
    )(*gathered)
    return (c_one[None, None], c_two[None])


def solution(mesh):
    in_specs = (
        P("row", "col", None, None, None),
        P("row", "col", None),
        P("row", "col", None),
        P("row", "col"),
        P("row", "col", None, None, None),
        P("row", "col", None),
        P("row", "col"),
        P("row", "col", None, None, None),
        P("row", "col", None),
    )
    out_specs = (
        P("row", "col", None, None, None, None, None),
        P("row", None, None, None, None, None),
    )
    return jax.shard_map(
        per_device, mesh=mesh, in_specs=in_specs, out_specs=out_specs, check_vma=False
    )
```

```python
import functools
import math

import jax
import jax.numpy as jnp
from jax import lax
from jax.experimental import pallas as pl
from jax.experimental.pallas import tpu as pltpu
from jax.sharding import PartitionSpec as P

FB = 8
CB = 2
G2 = 2
NS = 5
PB = FB * CB
UNROLL = 4
META = 16
F32 = jnp.float32
BF16 = jnp.bfloat16

VMEM = pl.BlockSpec(memory_space=pltpu.VMEM)
HBM = pl.BlockSpec(memory_space=pltpu.HBM)
SMALL = pltpu.CompilerParams(vmem_limit_bytes=4 * 1024 * 1024)
SMEM = pl.BlockSpec(memory_space=pltpu.SMEM)
LARGE = pltpu.CompilerParams(vmem_limit_bytes=20 * 1024 * 1024)
WHOLE = pltpu.CompilerParams(vmem_limit_bytes=60 * 1024 * 1024)


def pack_kernel(codes, count, aggs, blocks, second, out, held, sems):
    n_p, n_s = blocks.shape[0], second.shape[0]
    slots = codes.shape[0]
    copies = [
        pltpu.make_async_copy(blocks, held.at[0:n_p], sems.at[0]),
        pltpu.make_async_copy(second, held.at[n_p : n_p + n_s], sems.at[1]),
    ]
    for copy in copies:
        copy.start()
    lane = lax.broadcasted_iota(jnp.int32, (META, out.shape[1]), 1)
    word = jnp.zeros(lane.shape, jnp.int32)
    for k in range(slots):
        word = jnp.where(lane == k, jnp.where(k < count[0], codes[k], PB), word)
    for j in range(CB):
        word = jnp.where(lane == slots + j, aggs[j], word)
    held[n_p + n_s : n_p + n_s + META, :] = word.astype(F32).astype(BF16)
    for copy in copies:
        copy.wait()
    whole = pltpu.make_async_copy(held, out, sems.at[2])
    whole.start()
    whole.wait()


def fill_table(s, slots, table, code_of):
    for q in range(PB + 1):
        table[s, q] = -1
    for k in range(slots):
        table[s, code_of(k)] = k


def block_at(s, q, size, table, near):
    slot = table[s, q]
    block = near[pl.ds(pl.multiple_of(jnp.maximum(slot, 0) * size, size), size), :]
    return jnp.where(slot >= 0, block, jnp.zeros_like(block))


def lift_of(near, slots, size, agg_of):
    lines = []
    for j in range(CB):
        block = near[(slots + j) * size : (slots + j + 1) * size, :]
        lines.append(
            jnp.concatenate(
                [jnp.where(agg_of(j) == a, block, jnp.zeros_like(block)) for a in range(G2)],
                axis=1,
            )
        )
    return jnp.concatenate(lines, axis=0)


def dense_of(s, size, table, near, dense):
    for i in range(FB):
        for j in range(CB):
            dense[i * size : (i + 1) * size, j * size : (j + 1) * size] = block_at(
                s, i * CB + j, size, table, near
            )


def coarse_of(size, weight, dense, tile):
    coarse = jnp.dot(weight, dense[...], preferred_element_type=F32).astype(BF16)
    for i in range(CB):
        for j in range(CB):
            tile[i, j] = coarse[i * size : (i + 1) * size, j * size : (j + 1) * size]
    return coarse


def own_kernel(
    slots, size, rows, cols, count, codes, p_count, aggs, fine_at, own_at, stock_at, more_at, c_one,
    fine, own, stock, more, turned, acc, dense, tile, table, sems,
):
    fetch_own = pltpu.make_async_copy(own_at, own, sems.at[0])
    fetch_own.start()
    fetch_fine = pltpu.make_async_copy(fine_at, fine, sems.at[1])
    fetch_fine.start()
    acc[...] = jnp.zeros_like(acc)
    fill_table(0, slots, table, lambda k: jnp.where(k < p_count[0], codes[k], PB))
    fetch_own.wait()
    for i in range(FB):
        for j in range(CB):
            block = block_at(0, i * CB + j, size, table, own)
            turned[i, j * size : (j + 1) * size, :] = block.T
    fetch_fine.wait()

    def step(t, carry):
        products, targets = [], []
        for u in range(UNROLL):
            k = t * UNROLL + u
            products.append(jnp.dot(turned[rows[k]], fine[k], preferred_element_type=F32))
            targets.append(jnp.where(k < count[0], cols[k], NS * FB))
        for u in range(UNROLL):
            acc[targets[u]] += products[u]
        return carry

    lax.fori_loop(0, (count[0] + UNROLL - 1) // UNROLL, step, 0)
    stores = []
    for s in range(1, NS):
        for m in range(FB):
            stock[s - 1, :, m * size : (m + 1) * size] = acc[s * FB + m].astype(BF16)
        stores.append(pltpu.make_async_copy(stock.at[s - 1], stock_at.at[s - 1], sems.at[1 + s]))
        stores[-1].start()
    own_weight = jnp.concatenate([acc[m].astype(BF16) for m in range(FB)], axis=1)
    dense_of(0, size, table, own, dense)
    coarse = coarse_of(size, own_weight, dense, tile)
    lift = lift_of(own, slots, size, lambda j: aggs[j])
    wide = CB * size
    more[0] = lift.T
    more[1] = coarse
    more[2] = lift
    stores.append(pltpu.make_async_copy(more, more_at, sems.at[0]))
    stores[-1].start()
    stores.append(pltpu.make_async_copy(tile, c_one.at[:, 0], sems.at[1]))
    stores[-1].start()
    for store in stores:
        store.wait()


def near_coarse(
    sources, near, slots, size, stock, c_one, dense, tiles, words, codes, table, sems
):
    tail = (slots + CB) * size
    for n, ref in enumerate(near):
        word = ref[tail : tail + META, :].astype(F32).astype(jnp.int32)
        words[n : n + 1, :] = word[0:1, :]
    fetch = pltpu.make_async_copy(words, codes, sems.at[0])
    fetch.start()
    fetch.wait()
    parts, stores = [], []
    for n, (s, ref) in enumerate(zip(sources, near)):
        fill_table(n, slots, table, lambda k: codes[n, k])
        dense_of(n, size, table, ref, dense.at[n])
        coarse = coarse_of(size, stock[s - 1], dense.at[n], tiles.at[n])
        store = pltpu.make_async_copy(tiles.at[n], c_one.at[:, s], sems.at[1 + n])
        store.start()
        stores.append(store)
        lift = lift_of(ref, slots, size, lambda j: codes[n, slots + j])
        parts.append(jnp.dot(coarse, lift, preferred_element_type=F32))
    return parts, stores


def half_kernel(more, lift_t, half):
    lift_t[...] = more[0]
    half[...] = jnp.dot(more[1], more[2], preferred_element_type=F32)


def side_kernel(slots, size, stock, lift_t, half, left, right, c_in, c_one, term, *scratch):
    parts, stores = near_coarse((1, 2), (left, right), slots, size, stock, c_one, *scratch)
    whole = (half[...] + parts[0] + parts[1]).astype(BF16)
    term[...] = jnp.dot(lift_t[...], whole, preferred_element_type=F32)
    for store in stores:
        store.wait()


def row_kernel(slots, size, cols_n, stock, lift_t, term, other, pair, c_in, c_one, *rest):
    sends, terms, scratch = rest[:cols_n], rest[cols_n], rest[cols_n + 1 :]
    odd = lax.rem(lax.axis_index("row"), 2)
    sources = (3 + odd, 4 - odd)
    parts, stores = near_coarse(sources, (other, pair), slots, size, stock, c_one, *scratch)
    terms[0] = term[...]
    for n in range(2):
        terms[sources[n] - 2] = jnp.dot(lift_t[...], parts[n].astype(BF16), preferred_element_type=F32)
    chunk = terms.shape[1] // cols_n
    me = lax.axis_index("col")
    for d in range(cols_n):
        to = pl.multiple_of(lax.rem(me + d, cols_n) * chunk, chunk)
        sends[d][...] = terms[:, pl.ds(to, chunk), :].astype(sends[d].dtype)
    for store in stores:
        store.wait()


def sum_kernel(*refs):
    total = refs[0][...]
    for ref in refs[1:-1]:
        total = total + ref[...].astype(F32)
    refs[-1][...] = total.astype(BF16)


def spread_kernel(size, cols_n, *refs):
    out = refs[-1]
    chunk = refs[0].shape[1]
    unit = math.gcd(chunk, size)
    per = size // unit
    me = lax.axis_index("col")
    for d in range(cols_n):
        owner = lax.rem(me - d + cols_n, cols_n)
        for t in range(chunk // unit):
            at = owner * (chunk // unit) + t
            a = at // per
            h = pl.multiple_of(lax.rem(at, per) * unit, unit)
            for g in range(3):
                for b in range(G2):
                    out[a, g, b, pl.ds(h, unit), :] = refs[d][
                        g, t * unit : (t + 1) * unit, b * size : (b + 1) * size
                    ].astype(F32)


def shift(x, axis, step, wrap):
    n = lax.axis_size(axis)
    pairs = [(i, (i + step) % n) for i in range(n) if wrap or 0 <= i + step < n]
    return lax.ppermute(x, axis, pairs)


def swap(x, axis, pairs):
    return lax.ppermute(x, axis, pairs + [(j, i) for i, j in pairs])


def per_device(
    fine_blocks, fine_rows, fine_cols, fine_counts, prolong_blocks, prolong_codes,
    prolong_counts, second_blocks, second_aggs,
):
    slots, size = prolong_blocks.shape[2], prolong_blocks.shape[3]
    cap = fine_blocks.shape[2]
    cols_n = lax.axis_size("col")
    packed_rows = (slots + CB) * size + META
    wide = CB * size
    dma = pltpu.SemaphoreType.DMA
    packed = pl.pallas_call(
        pack_kernel,
        out_shape=jax.ShapeDtypeStruct((packed_rows, size), BF16),
        in_specs=[SMEM] * 3 + [HBM] * 2,
        out_specs=HBM,
        scratch_shapes=[pltpu.VMEM((packed_rows, size), BF16), dma((3,))],
        compiler_params=WHOLE,
        name="pack",
    )(
        prolong_codes[0, 0], prolong_counts[0], second_aggs[0, 0],
        prolong_blocks.reshape(slots * size, size),
        second_blocks.reshape(CB * size, size),
    )
    rows_n = lax.axis_size("row")
    pair = swap(packed, "row", [(i, i + 1) for i in range(0, rows_n - 1, 2)])
    other = swap(packed, "row", [(i, i + 1) for i in range(1, rows_n - 1, 2)])
    left = shift(packed, "col", 1, False)
    right = shift(packed, "col", -1, False)

    c_shape = jax.ShapeDtypeStruct((CB, NS, CB, size, size), BF16)
    table = pltpu.SMEM((NS, PB + 1), jnp.int32)
    stock, more, c_one = pl.pallas_call(
        functools.partial(own_kernel, slots, size),
        out_shape=[
            jax.ShapeDtypeStruct((NS - 1, wide, FB * size), BF16),
            jax.ShapeDtypeStruct((3, wide, G2 * size), BF16),
            c_shape,
        ],
        in_specs=[SMEM] * 6 + [HBM] * 2,
        out_specs=[HBM] * 3,
        scratch_shapes=[
            pltpu.VMEM((cap, size, size), BF16),
            pltpu.VMEM((packed_rows, size), BF16),
            pltpu.VMEM((NS - 1, wide, FB * size), BF16),
            pltpu.VMEM((3, wide, G2 * size), BF16),
            pltpu.VMEM((FB, wide, size), BF16),
            pltpu.VMEM((NS * FB + 1, wide, size), F32),
            pltpu.VMEM((FB * size, wide), BF16),
            pltpu.VMEM((CB, CB, size, size), BF16),
            table,
            dma((6,)),
        ],
        compiler_params=WHOLE,
        cost_estimate=pl.CostEstimate(flops=10**9, bytes_accessed=4 * 10**6, transcendentals=0),
        name="own_source",
    )(
        fine_rows[0, 0], fine_cols[0, 0], fine_counts[0],
        prolong_codes[0, 0], prolong_counts[0], second_aggs[0, 0],
        fine_blocks[0, 0], packed,
    )

    near_scratch = [
        pltpu.VMEM((2, FB * size, wide), BF16),
        pltpu.VMEM((2, CB, CB, size, size), BF16),
        pltpu.VMEM((8, size), jnp.int32),
        pltpu.SMEM((8, size), jnp.int32),
        table,
        dma((3,)),
    ]
    square = jax.ShapeDtypeStruct((wide, G2 * size), F32)
    lift_t, half = pl.pallas_call(
        half_kernel,
        out_shape=[jax.ShapeDtypeStruct((G2 * size, wide), BF16), square],
        in_specs=[VMEM],
        out_specs=[VMEM] * 2,
        compiler_params=SMALL,
        cost_estimate=pl.CostEstimate(flops=10**9, bytes_accessed=4 * 10**6, transcendentals=0),
        name="own_half",
    )(more)
    c_one, term = pl.pallas_call(
        functools.partial(side_kernel, slots, size),
        out_shape=[c_shape, square],
        in_specs=[VMEM] * 5 + [HBM],
        out_specs=[HBM, VMEM],
        input_output_aliases={5: 0},
        scratch_shapes=near_scratch,
        compiler_params=LARGE,
        name="col_sources",
    )(stock, lift_t, half, left, right, c_one)

    chunk = G2 * size // cols_n
    kept = jax.ShapeDtypeStruct((3, chunk, G2 * size), F32)
    piece = jax.ShapeDtypeStruct(kept.shape, BF16)
    c_one, *sends = pl.pallas_call(
        functools.partial(row_kernel, slots, size, cols_n),
        out_shape=[c_shape, kept] + [piece] * (cols_n - 1),
        in_specs=[VMEM] * 5 + [HBM],
        out_specs=[HBM] + [VMEM] * cols_n,
        input_output_aliases={5: 0},
        scratch_shapes=[pltpu.VMEM((3, G2 * size, G2 * size), F32)] + near_scratch,
        compiler_params=LARGE,
        name="row_sources",
    )(stock, lift_t, term, other, pair, c_one)
    parts = [sends[0]] + [shift(sends[d], "col", d, True) for d in range(1, cols_n)]
    total = pl.pallas_call(
        sum_kernel, out_shape=piece, in_specs=[VMEM] * cols_n, out_specs=VMEM,
        compiler_params=SMALL, name="total",
    )(*parts)
    gathered = [total] + [shift(total, "col", d, True) for d in range(1, cols_n)]
    c_two = pl.pallas_call(
        functools.partial(spread_kernel, size, cols_n),
        out_shape=jax.ShapeDtypeStruct((G2, 3, G2, size, size), F32),
        in_specs=[VMEM] * cols_n,
        out_specs=VMEM,
        compiler_params=SMALL,
        name="spread",
    )(*gathered)
    return (c_one[None, None], c_two[None])


def solution(mesh):
    in_specs = (
        P("row", "col", None, None, None),
        P("row", "col", None),
        P("row", "col", None),
        P("row", "col"),
        P("row", "col", None, None, None),
        P("row", "col", None),
        P("row", "col"),
        P("row", "col", None, None, None),
        P("row", "col", None),
    )
    out_specs = (
        P("row", "col", None, None, None, None, None),
        P("row", None, None, None, None, None),
    )
    return jax.shard_map(
        per_device, mesh=mesh, in_specs=in_specs, out_specs=out_specs, check_vma=False
    )
```

```python
import functools
import math

import jax
import jax.numpy as jnp
from jax import lax
from jax.experimental import pallas as pl
from jax.experimental.pallas import tpu as pltpu
from jax.sharding import PartitionSpec as P

FB = 8
CB = 2
G2 = 2
NS = 5
PB = FB * CB
UNROLL = 8
META = 16
F32 = jnp.float32
BF16 = jnp.bfloat16

VMEM = pl.BlockSpec(memory_space=pltpu.VMEM)
HBM = pl.BlockSpec(memory_space=pltpu.HBM)
SMALL = pltpu.CompilerParams(vmem_limit_bytes=4 * 1024 * 1024)
SMEM = pl.BlockSpec(memory_space=pltpu.SMEM)
LARGE = pltpu.CompilerParams(vmem_limit_bytes=20 * 1024 * 1024)
WHOLE = pltpu.CompilerParams(vmem_limit_bytes=60 * 1024 * 1024)


def pack_kernel(codes, count, aggs, blocks, second, out, held, sems):
    n_p, n_s = blocks.shape[0], second.shape[0]
    slots = codes.shape[0]
    copies = [
        pltpu.make_async_copy(blocks, held.at[0:n_p], sems.at[0]),
        pltpu.make_async_copy(second, held.at[n_p : n_p + n_s], sems.at[1]),
    ]
    for copy in copies:
        copy.start()
    lane = lax.broadcasted_iota(jnp.int32, (META, out.shape[1]), 1)
    word = jnp.zeros(lane.shape, jnp.int32)
    for k in range(slots):
        word = jnp.where(lane == k, jnp.where(k < count[0], codes[k], PB), word)
    for j in range(CB):
        word = jnp.where(lane == slots + j, aggs[j], word)
    held[n_p + n_s : n_p + n_s + META, :] = word.astype(F32).astype(BF16)
    for copy in copies:
        copy.wait()
    whole = pltpu.make_async_copy(held, out, sems.at[2])
    whole.start()
    whole.wait()


def fill_table(s, slots, table, code_of):
    for q in range(PB + 1):
        table[s, q] = -1
    for k in range(slots):
        table[s, code_of(k)] = k


def block_at(s, q, size, table, near):
    slot = table[s, q]
    block = near[pl.ds(pl.multiple_of(jnp.maximum(slot, 0) * size, size), size), :]
    return jnp.where(slot >= 0, block, jnp.zeros_like(block))


def lift_of(near, slots, size, agg_of):
    lines = []
    for j in range(CB):
        block = near[(slots + j) * size : (slots + j + 1) * size, :]
        lines.append(
            jnp.concatenate(
                [jnp.where(agg_of(j) == a, block, jnp.zeros_like(block)) for a in range(G2)],
                axis=1,
            )
        )
    return jnp.concatenate(lines, axis=0)


def dense_of(s, size, table, near, dense):
    for i in range(FB):
        for j in range(CB):
            dense[i * size : (i + 1) * size, j * size : (j + 1) * size] = block_at(
                s, i * CB + j, size, table, near
            )


def coarse_of(size, weight, dense, tile):
    coarse = jnp.dot(weight, dense[...], preferred_element_type=F32).astype(BF16)
    for i in range(CB):
        for j in range(CB):
            tile[i, j] = coarse[i * size : (i + 1) * size, j * size : (j + 1) * size]
    return coarse


def own_kernel(
    slots, size, rows, cols, count, codes, p_count, aggs, fine_at, own_at,
    stock_at, half_at, lift_at, token, c_one,
    fine, own, stock, half, lift_t, turned, acc, dense, tile, table, sems,
):
    fetch_own = pltpu.make_async_copy(own_at, own, sems.at[0])
    fetch_own.start()
    fetch_fine = pltpu.make_async_copy(fine_at, fine, sems.at[1])
    fetch_fine.start()
    acc[...] = jnp.zeros_like(acc)
    turned[...] = jnp.zeros_like(turned)
    token[...] = jnp.zeros_like(token)
    code_of = lambda k: jnp.where(k < p_count[0], codes[k], PB)
    fill_table(0, slots, table, code_of)
    fetch_own.wait()
    for k in range(slots):
        i = code_of(k) // CB
        j = pl.multiple_of((code_of(k) - i * CB) * size, size)
        turned[i, pl.ds(j, size), :] = own[k * size : (k + 1) * size, :].T
    fetch_fine.wait()

    def step(t, carry):
        products, targets = [], []
        for u in range(UNROLL):
            k = t * UNROLL + u
            products.append(jnp.dot(turned[rows[k]], fine[k], preferred_element_type=F32))
            targets.append(jnp.where(k < count[0], cols[k], NS * FB))
        for u in range(UNROLL):
            acc[targets[u]] += products[u]
        return carry

    lax.fori_loop(0, (count[0] + UNROLL - 1) // UNROLL, step, 0)
    stores = []
    for s in range(1, NS):
        for m in range(FB):
            stock[s - 1, :, m * size : (m + 1) * size] = acc[s * FB + m].astype(BF16)
        stores.append(pltpu.make_async_copy(stock.at[s - 1], stock_at.at[s - 1], sems.at[1 + s]))
        stores[-1].start()
    own_weight = jnp.concatenate([acc[m].astype(BF16) for m in range(FB)], axis=1)
    dense_of(0, size, table, own, dense)
    coarse = coarse_of(size, own_weight, dense, tile)
    lift = lift_of(own, slots, size, lambda j: aggs[j])
    lift_t[...] = lift.T
    half[...] = jnp.dot(coarse, lift, preferred_element_type=F32)
    stores.append(pltpu.make_async_copy(lift_t, lift_at, sems.at[0]))
    stores[-1].start()
    stores.append(pltpu.make_async_copy(half, half_at, sems.at[6]))
    stores[-1].start()
    stores.append(pltpu.make_async_copy(tile, c_one.at[:, 0], sems.at[1]))
    stores[-1].start()
    for store in stores:
        store.wait()


def near_coarse(
    sources, near, slots, size, stock, c_one, dense, tiles, words, codes, table, sems
):
    tail = (slots + CB) * size
    for n, ref in enumerate(near):
        word = ref[tail : tail + META, :].astype(F32).astype(jnp.int32)
        words[n : n + 1, :] = word[0:1, :]
    fetch = pltpu.make_async_copy(words, codes, sems.at[0])
    fetch.start()
    fetch.wait()
    parts, stores = [], []
    for n, (s, ref) in enumerate(zip(sources, near)):
        fill_table(n, slots, table, lambda k: codes[n, k])
        dense_of(n, size, table, ref, dense.at[n])
        coarse = coarse_of(size, stock[s - 1], dense.at[n], tiles.at[n])
        store = pltpu.make_async_copy(tiles.at[n], c_one.at[:, s], sems.at[1 + n])
        store.start()
        stores.append(store)
        lift = lift_of(ref, slots, size, lambda j: codes[n, slots + j])
        parts.append(jnp.dot(coarse, lift, preferred_element_type=F32))
    return parts, stores


def pass_kernel(token, out):
    out[...] = token[...]


def side_kernel(slots, size, stock, lift_t, half, left, right, token, c_in, c_one, term, *scratch):
    parts, stores = near_coarse((1, 2), (left, right), slots, size, stock, c_one, *scratch)
    whole = (half[...] + parts[0] + parts[1]).astype(BF16)
    term[...] = jnp.dot(lift_t[...], whole, preferred_element_type=F32)
    for store in stores:
        store.wait()


def row_kernel(slots, size, cols_n, stock, lift_t, term, other, pair, c_in, c_one, *rest):
    sends, terms, scratch = rest[:cols_n], rest[cols_n], rest[cols_n + 1 :]
    odd = lax.rem(lax.axis_index("row"), 2)
    sources = (3 + odd, 4 - odd)
    parts, stores = near_coarse(sources, (other, pair), slots, size, stock, c_one, *scratch)
    terms[0] = term[...]
    for n in range(2):
        terms[sources[n] - 2] = jnp.dot(lift_t[...], parts[n].astype(BF16), preferred_element_type=F32)
    chunk = terms.shape[1] // cols_n
    me = lax.axis_index("col")
    for d in range(cols_n):
        to = pl.multiple_of(lax.rem(me + d, cols_n) * chunk, chunk)
        sends[d][...] = terms[:, pl.ds(to, chunk), :].astype(sends[d].dtype)
    for store in stores:
        store.wait()


def sum_kernel(*refs):
    total = refs[0][...]
    for ref in refs[1:-1]:
        total = total + ref[...].astype(F32)
    refs[-1][...] = total.astype(BF16)


def spread_kernel(size, steps, *refs):
    out = refs[-1]
    chunk = refs[0].shape[1]
    unit = math.gcd(chunk, size)
    per = size // unit
    me = lax.axis_index("col")
    for n, d in enumerate(steps):
        owner = lax.rem(me - d + len(steps), len(steps))
        for t in range(chunk // unit):
            at = owner * (chunk // unit) + t
            a = at // per
            h = pl.multiple_of(lax.rem(at, per) * unit, unit)
            for g in range(3):
                for b in range(G2):
                    out[a, g, b, pl.ds(h, unit), :] = refs[n][
                        g, t * unit : (t + 1) * unit, b * size : (b + 1) * size
                    ].astype(F32)


def shift(x, axis, step, wrap):
    n = lax.axis_size(axis)
    pairs = [(i, (i + step) % n) for i in range(n) if wrap or 0 <= i + step < n]
    return lax.ppermute(x, axis, pairs)


def swap(x, axis, pairs):
    return lax.ppermute(x, axis, pairs + [(j, i) for i, j in pairs])


def per_device(
    fine_blocks, fine_rows, fine_cols, fine_counts, prolong_blocks, prolong_codes,
    prolong_counts, second_blocks, second_aggs,
):
    slots, size = prolong_blocks.shape[2], prolong_blocks.shape[3]
    cap = fine_blocks.shape[2]
    cols_n = lax.axis_size("col")
    packed_rows = (slots + CB) * size + META
    wide = CB * size
    dma = pltpu.SemaphoreType.DMA
    packed = pl.pallas_call(
        pack_kernel,
        out_shape=jax.ShapeDtypeStruct((packed_rows, size), BF16),
        in_specs=[SMEM] * 3 + [HBM] * 2,
        out_specs=HBM,
        scratch_shapes=[pltpu.VMEM((packed_rows, size), BF16), dma((3,))],
        compiler_params=WHOLE,
        name="pack",
    )(
        prolong_codes[0, 0], prolong_counts[0], second_aggs[0, 0],
        prolong_blocks.reshape(slots * size, size),
        second_blocks.reshape(CB * size, size),
    )
    rows_n = lax.axis_size("row")
    pair = swap(packed, "row", [(i, i + 1) for i in range(0, rows_n - 1, 2)])
    other = swap(packed, "row", [(i, i + 1) for i in range(1, rows_n - 1, 2)])
    left = shift(packed, "col", 1, False)
    right = shift(packed, "col", -1, False)

    c_shape = jax.ShapeDtypeStruct((CB, NS, CB, size, size), BF16)
    square = jax.ShapeDtypeStruct((wide, G2 * size), F32)
    mark = jax.ShapeDtypeStruct((8, size), F32)
    table = pltpu.SMEM((NS, PB + 1), jnp.int32)
    stock, half, lift_t, token, c_one = pl.pallas_call(
        functools.partial(own_kernel, slots, size),
        out_shape=[
            jax.ShapeDtypeStruct((NS - 1, wide, FB * size), BF16),
            square,
            jax.ShapeDtypeStruct((G2 * size, wide), BF16),
            mark,
            c_shape,
        ],
        in_specs=[SMEM] * 6 + [HBM] * 2,
        out_specs=[HBM] * 3 + [VMEM, HBM],
        scratch_shapes=[
            pltpu.VMEM((cap, size, size), BF16),
            pltpu.VMEM((packed_rows, size), BF16),
            pltpu.VMEM((NS - 1, wide, FB * size), BF16),
            pltpu.VMEM((wide, G2 * size), F32),
            pltpu.VMEM((G2 * size, wide), BF16),
            pltpu.VMEM((FB + 1, wide, size), BF16),
            pltpu.VMEM((NS * FB + 1, wide, size), F32),
            pltpu.VMEM((FB * size, wide), BF16),
            pltpu.VMEM((CB, CB, size, size), BF16),
            table,
            dma((7,)),
        ],
        compiler_params=WHOLE,
        cost_estimate=pl.CostEstimate(flops=10**9, bytes_accessed=4 * 10**6, transcendentals=0),
        name="own_source",
    )(
        fine_rows[0, 0], fine_cols[0, 0], fine_counts[0],
        prolong_codes[0, 0], prolong_counts[0], second_aggs[0, 0],
        fine_blocks[0, 0], packed,
    )

    near_scratch = [
        pltpu.VMEM((2, FB * size, wide), BF16),
        pltpu.VMEM((2, CB, CB, size, size), BF16),
        pltpu.VMEM((8, size), jnp.int32),
        pltpu.SMEM((8, size), jnp.int32),
        table,
        dma((3,)),
    ]
    token = pl.pallas_call(
        pass_kernel,
        out_shape=mark,
        in_specs=[VMEM],
        out_specs=VMEM,
        compiler_params=SMALL,
        cost_estimate=pl.CostEstimate(flops=10**9, bytes_accessed=4 * 10**6, transcendentals=0),
        name="pass_on",
    )(token)
    c_one, term = pl.pallas_call(
        functools.partial(side_kernel, slots, size),
        out_shape=[c_shape, square],
        in_specs=[VMEM] * 6 + [HBM],
        out_specs=[HBM, VMEM],
        input_output_aliases={6: 0},
        scratch_shapes=near_scratch,
        compiler_params=LARGE,
        name="col_sources",
    )(stock, lift_t, half, left, right, token, c_one)

    chunk = G2 * size // cols_n
    kept = jax.ShapeDtypeStruct((3, chunk, G2 * size), F32)
    piece = jax.ShapeDtypeStruct(kept.shape, BF16)
    c_one, *sends = pl.pallas_call(
        functools.partial(row_kernel, slots, size, cols_n),
        out_shape=[c_shape, kept] + [piece] * (cols_n - 1),
        in_specs=[VMEM] * 5 + [HBM],
        out_specs=[HBM] + [VMEM] * cols_n,
        input_output_aliases={5: 0},
        scratch_shapes=[pltpu.VMEM((3, G2 * size, G2 * size), F32)] + near_scratch,
        compiler_params=LARGE,
        name="row_sources",
    )(stock, lift_t, term, other, pair, c_one)
    steps = sorted(range(1, cols_n), key=lambda d: -min(d, cols_n - d))
    parts = [sends[0]] + [shift(sends[d], "col", d, True) for d in steps]
    total = pl.pallas_call(
        sum_kernel, out_shape=piece, in_specs=[VMEM] * cols_n, out_specs=VMEM,
        compiler_params=SMALL, name="total",
    )(*parts)
    gathered = [total] + [shift(total, "col", d, True) for d in steps]
    c_two = pl.pallas_call(
        functools.partial(spread_kernel, size, [0] + steps),
        out_shape=jax.ShapeDtypeStruct((G2, 3, G2, size, size), F32),
        in_specs=[VMEM] * cols_n,
        out_specs=VMEM,
        compiler_params=SMALL,
        name="spread",
    )(*gathered)
    return (c_one[None, None], c_two[None])


def solution(mesh):
    in_specs = (
        P("row", "col", None, None, None),
        P("row", "col", None),
        P("row", "col", None),
        P("row", "col"),
        P("row", "col", None, None, None),
        P("row", "col", None),
        P("row", "col"),
        P("row", "col", None, None, None),
        P("row", "col", None),
    )
    out_specs = (
        P("row", "col", None, None, None, None, None),
        P("row", None, None, None, None, None),
    )
    return jax.shard_map(
        per_device, mesh=mesh, in_specs=in_specs, out_specs=out_specs, check_vma=False
    )
```

```python
import functools
import math

import jax
import jax.numpy as jnp
from jax import lax
from jax.experimental import pallas as pl
from jax.experimental.pallas import tpu as pltpu
from jax.sharding import PartitionSpec as P

FB = 8
CB = 2
G2 = 2
NS = 5
PB = FB * CB
UNROLL = 8
META = 16
F32 = jnp.float32
BF16 = jnp.bfloat16

VMEM = pl.BlockSpec(memory_space=pltpu.VMEM)
HBM = pl.BlockSpec(memory_space=pltpu.HBM)
SMALL = pltpu.CompilerParams(vmem_limit_bytes=4 * 1024 * 1024)
SMEM = pl.BlockSpec(memory_space=pltpu.SMEM)
LARGE = pltpu.CompilerParams(vmem_limit_bytes=20 * 1024 * 1024)
WHOLE = pltpu.CompilerParams(vmem_limit_bytes=60 * 1024 * 1024)


def pack_kernel(
    codes_at, count_at, aggs_at, blocks, second, out, held, codes, count, aggs, table, sems
):
    n_p, n_s = blocks.shape[0], second.shape[0]
    slots, cut = codes_at.shape[-1], n_p // 2
    small = [
        pltpu.make_async_copy(a, b, sems.at[n])
        for n, (a, b) in enumerate([(codes_at, codes), (count_at, count), (aggs_at, aggs)])
    ]
    large = [
        pltpu.make_async_copy(blocks.at[0:cut], held.at[0:cut], sems.at[3]),
        pltpu.make_async_copy(blocks.at[cut:n_p], held.at[cut:n_p], sems.at[4]),
        pltpu.make_async_copy(second, held.at[n_p : n_p + n_s], sems.at[5]),
    ]
    for copy in small + large:
        copy.start()
    for copy in small:
        copy.wait()
    fill_table(0, slots, table, lambda k: jnp.where(k < count[0, 0], codes[0, 0, k], PB))
    lane = lax.broadcasted_iota(jnp.int32, (META, out.shape[1]), 1)
    word = jnp.zeros(lane.shape, jnp.int32)
    for q in range(PB):
        word = jnp.where(lane == q, table[0, q], word)
    for j in range(CB):
        word = jnp.where(lane == PB + j, aggs[0, 0, j], word)
    held[n_p + n_s : n_p + n_s + META, :] = word.astype(F32).astype(BF16)
    large[0].wait()
    stores = [pltpu.make_async_copy(held.at[0:cut], out.at[0:cut], sems.at[6])]
    stores[0].start()
    large[1].wait()
    large[2].wait()
    rest = pl.ds(cut, out.shape[0] - cut)
    stores.append(pltpu.make_async_copy(held.at[rest], out.at[rest], sems.at[7]))
    stores[1].start()
    for store in stores:
        store.wait()


def fill_table(s, slots, table, code_of):
    for q in range(PB + 1):
        table[s, q] = -1
    for k in range(slots):
        table[s, code_of(k)] = k


def block_at(s, q, size, table, near):
    slot = table[s, q]
    block = near[pl.ds(pl.multiple_of(jnp.maximum(slot, 0) * size, size), size), :]
    return jnp.where(slot >= 0, block, jnp.zeros_like(block))


def lift_of(near, slots, size, agg_of):
    lines = []
    for j in range(CB):
        block = near[(slots + j) * size : (slots + j + 1) * size, :]
        lines.append(
            jnp.concatenate(
                [jnp.where(agg_of(j) == a, block, jnp.zeros_like(block)) for a in range(G2)],
                axis=1,
            )
        )
    return jnp.concatenate(lines, axis=0)


def dense_of(s, size, table, near, dense):
    for i in range(FB):
        for j in range(CB):
            dense[i * size : (i + 1) * size, j * size : (j + 1) * size] = block_at(
                s, i * CB + j, size, table, near
            )


def coarse_of(size, weight, dense, tile):
    coarse = jnp.dot(weight, dense[...], preferred_element_type=F32).astype(BF16)
    for i in range(CB):
        for j in range(CB):
            tile[i, j] = coarse[i * size : (i + 1) * size, j * size : (j + 1) * size]
    return coarse


def own_kernel(
    slots, size, rows, cols, count, codes, p_count, aggs, fine_at, own_at, stock_at, more_at, c_one,
    fine, own, stock, more, turned, acc, dense, tile, table, sems,
):
    fetch_own = pltpu.make_async_copy(own_at, own, sems.at[0])
    fetch_own.start()
    fetch_fine = pltpu.make_async_copy(fine_at, fine, sems.at[1])
    fetch_fine.start()
    acc[...] = jnp.zeros_like(acc)
    turned[...] = jnp.zeros_like(turned)
    code_of = lambda k: jnp.where(k < p_count[0], codes[k], PB)
    fill_table(0, slots, table, code_of)
    fetch_own.wait()
    for k in range(slots):
        i = code_of(k) // CB
        j = pl.multiple_of((code_of(k) - i * CB) * size, size)
        turned[i, pl.ds(j, size), :] = own[k * size : (k + 1) * size, :].T
    fetch_fine.wait()

    def step(t, carry):
        products, targets = [], []
        for u in range(UNROLL):
            k = t * UNROLL + u
            products.append(jnp.dot(turned[rows[k]], fine[k], preferred_element_type=F32))
            targets.append(jnp.where(k < count[0], cols[k], NS * FB))
        for u in range(UNROLL):
            acc[targets[u]] += products[u]
        return carry

    lax.fori_loop(0, (count[0] + UNROLL - 1) // UNROLL, step, 0)
    stores = []
    for s in range(1, NS):
        for m in range(FB):
            stock[s - 1, :, m * size : (m + 1) * size] = acc[s * FB + m].astype(BF16)
        stores.append(pltpu.make_async_copy(stock.at[s - 1], stock_at.at[s - 1], sems.at[1 + s]))
        stores[-1].start()
    own_weight = jnp.concatenate([acc[m].astype(BF16) for m in range(FB)], axis=1)
    dense_of(0, size, table, own, dense)
    coarse = coarse_of(size, own_weight, dense, tile)
    lift = lift_of(own, slots, size, lambda j: aggs[j])
    wide = CB * size
    more[0] = lift.T
    more[1] = coarse
    more[2] = lift
    stores.append(pltpu.make_async_copy(more, more_at, sems.at[0]))
    stores[-1].start()
    stores.append(pltpu.make_async_copy(tile, c_one.at[:, 0], sems.at[1]))
    stores[-1].start()
    for store in stores:
        store.wait()


def near_coarse(
    sources, near, slots, size, stock, c_one, dense, tiles, words, codes, sems
):
    tail = (slots + CB) * size
    for n, ref in enumerate(near):
        word = ref[tail : tail + META, :].astype(F32).astype(jnp.int32)
        words[n : n + 1, :] = word[0:1, :]
    fetch = pltpu.make_async_copy(words, codes, sems.at[0])
    fetch.start()
    fetch.wait()
    parts, stores = [], []
    for n, (s, ref) in enumerate(zip(sources, near)):
        dense_of(n, size, codes, ref, dense.at[n])
        coarse = coarse_of(size, stock[s - 1], dense.at[n], tiles.at[n])
        store = pltpu.make_async_copy(tiles.at[n], c_one.at[:, s], sems.at[1 + n])
        store.start()
        stores.append(store)
        lift = lift_of(ref, slots, size, lambda j: codes[n, PB + j])
        parts.append(jnp.dot(coarse, lift, preferred_element_type=F32))
    return parts, stores


def half_kernel(more, lift_t, half):
    lift_t[...] = more[0]
    half[...] = jnp.dot(more[1], more[2], preferred_element_type=F32)


def side_kernel(slots, size, stock, lift_t, half, left, right, c_in, c_one, term, *scratch):
    parts, stores = near_coarse((1, 2), (left, right), slots, size, stock, c_one, *scratch)
    whole = (half[...] + parts[0] + parts[1]).astype(BF16)
    term[...] = jnp.dot(lift_t[...], whole, preferred_element_type=F32)
    for store in stores:
        store.wait()


def row_kernel(slots, size, cols_n, stock, lift_t, term, other, pair, c_in, c_one, *rest):
    sends, terms, scratch = rest[:cols_n], rest[cols_n], rest[cols_n + 1 :]
    odd = lax.rem(lax.axis_index("row"), 2)
    sources = (3 + odd, 4 - odd)
    parts, stores = near_coarse(sources, (other, pair), slots, size, stock, c_one, *scratch)
    terms[0] = term[...]
    for n in range(2):
        terms[sources[n] - 2] = jnp.dot(lift_t[...], parts[n].astype(BF16), preferred_element_type=F32)
    chunk = terms.shape[1] // cols_n
    me = lax.axis_index("col")
    for d in range(cols_n):
        to = pl.multiple_of(lax.rem(me + d, cols_n) * chunk, chunk)
        sends[d][...] = terms[:, pl.ds(to, chunk), :].astype(sends[d].dtype)
    for store in stores:
        store.wait()


def sum_kernel(*refs):
    total = refs[0][...]
    for ref in refs[1:-1]:
        total = total + ref[...].astype(F32)
    refs[-1][...] = total.astype(BF16)


def spread_kernel(size, cols_n, *refs):
    out = refs[-1]
    chunk = refs[0].shape[1]
    unit = math.gcd(chunk, size)
    per = size // unit
    me = lax.axis_index("col")
    for d in range(cols_n):
        owner = lax.rem(me - d + cols_n, cols_n)
        for t in range(chunk // unit):
            at = owner * (chunk // unit) + t
            a = at // per
            h = pl.multiple_of(lax.rem(at, per) * unit, unit)
            for g in range(3):
                for b in range(G2):
                    out[a, g, b, pl.ds(h, unit), :] = refs[d][
                        g, t * unit : (t + 1) * unit, b * size : (b + 1) * size
                    ].astype(F32)


def shift(x, axis, step, wrap):
    n = lax.axis_size(axis)
    pairs = [(i, (i + step) % n) for i in range(n) if wrap or 0 <= i + step < n]
    return lax.ppermute(x, axis, pairs)


def swap(x, axis, pairs):
    return lax.ppermute(x, axis, pairs + [(j, i) for i, j in pairs])


def per_device(
    fine_blocks, fine_rows, fine_cols, fine_counts, prolong_blocks, prolong_codes,
    prolong_counts, second_blocks, second_aggs,
):
    slots, size = prolong_blocks.shape[2], prolong_blocks.shape[3]
    cap = fine_blocks.shape[2]
    cols_n = lax.axis_size("col")
    packed_rows = (slots + CB) * size + META
    wide = CB * size
    dma = pltpu.SemaphoreType.DMA
    packed = pl.pallas_call(
        pack_kernel,
        out_shape=jax.ShapeDtypeStruct((packed_rows, size), BF16),
        in_specs=[HBM] * 5,
        out_specs=HBM,
        scratch_shapes=[
            pltpu.VMEM((packed_rows, size), BF16),
            pltpu.SMEM(prolong_codes.shape, jnp.int32),
            pltpu.SMEM(prolong_counts.shape, jnp.int32),
            pltpu.SMEM(second_aggs.shape, jnp.int32),
            pltpu.SMEM((1, PB + 1), jnp.int32),
            dma((8,)),
        ],
        compiler_params=WHOLE,
        name="pack",
    )(
        prolong_codes, prolong_counts, second_aggs,
        prolong_blocks.reshape(slots * size, size),
        second_blocks.reshape(CB * size, size),
    )
    rows_n = lax.axis_size("row")
    pair = swap(packed, "row", [(i, i + 1) for i in range(0, rows_n - 1, 2)])
    other = swap(packed, "row", [(i, i + 1) for i in range(1, rows_n - 1, 2)])
    left = shift(packed, "col", 1, False)
    right = shift(packed, "col", -1, False)

    c_shape = jax.ShapeDtypeStruct((CB, NS, CB, size, size), BF16)
    table = pltpu.SMEM((1, PB + 1), jnp.int32)
    stock, more, c_one = pl.pallas_call(
        functools.partial(own_kernel, slots, size),
        out_shape=[
            jax.ShapeDtypeStruct((NS - 1, wide, FB * size), BF16),
            jax.ShapeDtypeStruct((3, wide, G2 * size), BF16),
            c_shape,
        ],
        in_specs=[SMEM] * 6 + [HBM] * 2,
        out_specs=[HBM] * 3,
        scratch_shapes=[
            pltpu.VMEM((cap, size, size), BF16),
            pltpu.VMEM((packed_rows, size), BF16),
            pltpu.VMEM((NS - 1, wide, FB * size), BF16),
            pltpu.VMEM((3, wide, G2 * size), BF16),
            pltpu.VMEM((FB + 1, wide, size), BF16),
            pltpu.VMEM((NS * FB + 1, wide, size), F32),
            pltpu.VMEM((FB * size, wide), BF16),
            pltpu.VMEM((CB, CB, size, size), BF16),
            table,
            dma((6,)),
        ],
        compiler_params=WHOLE,
        cost_estimate=pl.CostEstimate(flops=10**9, bytes_accessed=4 * 10**6, transcendentals=0),
        name="own_source",
    )(
        fine_rows[0, 0], fine_cols[0, 0], fine_counts[0],
        prolong_codes[0, 0], prolong_counts[0], second_aggs[0, 0],
        fine_blocks[0, 0], packed,
    )

    near_scratch = [
        pltpu.VMEM((2, FB * size, wide), BF16),
        pltpu.VMEM((2, CB, CB, size, size), BF16),
        pltpu.VMEM((8, size), jnp.int32),
        pltpu.SMEM((8, size), jnp.int32),
        dma((3,)),
    ]
    square = jax.ShapeDtypeStruct((wide, G2 * size), F32)
    lift_t, half = pl.pallas_call(
        half_kernel,
        out_shape=[jax.ShapeDtypeStruct((G2 * size, wide), BF16), square],
        in_specs=[VMEM],
        out_specs=[VMEM] * 2,
        compiler_params=SMALL,
        cost_estimate=pl.CostEstimate(flops=10**9, bytes_accessed=4 * 10**6, transcendentals=0),
        name="own_half",
    )(more)
    c_one, term = pl.pallas_call(
        functools.partial(side_kernel, slots, size),
        out_shape=[c_shape, square],
        in_specs=[VMEM] * 5 + [HBM],
        out_specs=[HBM, VMEM],
        input_output_aliases={5: 0},
        scratch_shapes=near_scratch,
        compiler_params=LARGE,
        name="col_sources",
    )(stock, lift_t, half, left, right, c_one)

    chunk = G2 * size // cols_n
    kept = jax.ShapeDtypeStruct((3, chunk, G2 * size), F32)
    piece = jax.ShapeDtypeStruct(kept.shape, BF16)
    c_one, *sends = pl.pallas_call(
        functools.partial(row_kernel, slots, size, cols_n),
        out_shape=[c_shape, kept] + [piece] * (cols_n - 1),
        in_specs=[VMEM] * 5 + [HBM],
        out_specs=[HBM] + [VMEM] * cols_n,
        input_output_aliases={5: 0},
        scratch_shapes=[pltpu.VMEM((3, G2 * size, G2 * size), F32)] + near_scratch,
        compiler_params=LARGE,
        name="row_sources",
    )(stock, lift_t, term, other, pair, c_one)
    parts = [sends[0]] + [shift(sends[d], "col", d, True) for d in range(1, cols_n)]
    total = pl.pallas_call(
        sum_kernel, out_shape=piece, in_specs=[VMEM] * cols_n, out_specs=VMEM,
        compiler_params=SMALL, name="total",
    )(*parts)
    gathered = [total] + [shift(total, "col", d, True) for d in range(1, cols_n)]
    c_two = pl.pallas_call(
        functools.partial(spread_kernel, size, cols_n),
        out_shape=jax.ShapeDtypeStruct((G2, 3, G2, size, size), F32),
        in_specs=[VMEM] * cols_n,
        out_specs=VMEM,
        compiler_params=SMALL,
        name="spread",
    )(*gathered)
    return (c_one[None, None], c_two[None])


def solution(mesh):
    in_specs = (
        P("row", "col", None, None, None),
        P("row", "col", None),
        P("row", "col", None),
        P("row", "col"),
        P("row", "col", None, None, None),
        P("row", "col", None),
        P("row", "col"),
        P("row", "col", None, None, None),
        P("row", "col", None),
    )
    out_specs = (
        P("row", "col", None, None, None, None, None),
        P("row", None, None, None, None, None),
    )
    return jax.shard_map(
        per_device, mesh=mesh, in_specs=in_specs, out_specs=out_specs, check_vma=False
    )
```

```python
import functools
import math

import jax
import jax.numpy as jnp
from jax import lax
from jax.experimental import pallas as pl
from jax.experimental.pallas import tpu as pltpu
from jax.sharding import PartitionSpec as P

FB = 8
CB = 2
G2 = 2
NS = 5
PB = FB * CB
UNROLL = 8
META = 16
F32 = jnp.float32
BF16 = jnp.bfloat16

VMEM = pl.BlockSpec(memory_space=pltpu.VMEM)
HBM = pl.BlockSpec(memory_space=pltpu.HBM)
SMALL = pltpu.CompilerParams(vmem_limit_bytes=4 * 1024 * 1024)
SMEM = pl.BlockSpec(memory_space=pltpu.SMEM)
LARGE = pltpu.CompilerParams(vmem_limit_bytes=20 * 1024 * 1024)
WHOLE = pltpu.CompilerParams(vmem_limit_bytes=60 * 1024 * 1024)


def pack_kernel(
    codes_at, count_at, aggs_at, blocks, second, out, held, codes, count, aggs, table, sems
):
    n_p, n_s = blocks.shape[0], second.shape[0]
    slots, cut = codes_at.shape[-1], n_p // 2
    small = [
        pltpu.make_async_copy(a, b, sems.at[n])
        for n, (a, b) in enumerate([(codes_at, codes), (count_at, count), (aggs_at, aggs)])
    ]
    large = [
        pltpu.make_async_copy(blocks.at[0:cut], held.at[0:cut], sems.at[3]),
        pltpu.make_async_copy(blocks.at[cut:n_p], held.at[cut:n_p], sems.at[4]),
        pltpu.make_async_copy(second, held.at[n_p : n_p + n_s], sems.at[5]),
    ]
    for copy in small + large:
        copy.start()
    for copy in small:
        copy.wait()
    fill_table(0, slots, table, lambda k: jnp.where(k < count[0, 0], codes[0, 0, k], PB))
    lane = lax.broadcasted_iota(jnp.int32, (META, out.shape[1]), 1)
    word = jnp.zeros(lane.shape, jnp.int32)
    for q in range(PB):
        word = jnp.where(lane == q, table[0, q], word)
    for j in range(CB):
        word = jnp.where(lane == PB + j, aggs[0, 0, j], word)
    held[n_p + n_s : n_p + n_s + META, :] = word.astype(F32).astype(BF16)
    large[0].wait()
    stores = [pltpu.make_async_copy(held.at[0:cut], out.at[0:cut], sems.at[6])]
    stores[0].start()
    large[1].wait()
    large[2].wait()
    rest = pl.ds(cut, out.shape[0] - cut)
    stores.append(pltpu.make_async_copy(held.at[rest], out.at[rest], sems.at[7]))
    stores[1].start()
    for store in stores:
        store.wait()


def fill_table(s, slots, table, code_of):
    for q in range(PB + 1):
        table[s, q] = -1
    for k in range(slots):
        table[s, code_of(k)] = k


def block_at(s, q, size, table, near):
    slot = table[s, q]
    block = near[pl.ds(pl.multiple_of(jnp.maximum(slot, 0) * size, size), size), :]
    return jnp.where(slot >= 0, block, jnp.zeros_like(block))


def lift_of(near, slots, size, agg_of):
    lines = []
    for j in range(CB):
        block = near[(slots + j) * size : (slots + j + 1) * size, :]
        lines.append(
            jnp.concatenate(
                [jnp.where(agg_of(j) == a, block, jnp.zeros_like(block)) for a in range(G2)],
                axis=1,
            )
        )
    return jnp.concatenate(lines, axis=0)


def dense_of(s, size, table, near, dense):
    for i in range(FB):
        for j in range(CB):
            dense[i * size : (i + 1) * size, j * size : (j + 1) * size] = block_at(
                s, i * CB + j, size, table, near
            )


def coarse_of(size, weight, dense, tile):
    coarse = jnp.dot(weight, dense[...], preferred_element_type=F32).astype(BF16)
    for i in range(CB):
        for j in range(CB):
            tile[i, j] = coarse[i * size : (i + 1) * size, j * size : (j + 1) * size]
    return coarse


def own_kernel(
    slots, size, rows, cols, count, codes, p_count, aggs, fine_at, own_at,
    col_at, row_at, more_at, c_one,
    fine, own, stock, more, turned, acc, dense, tile, table, sems,
):
    fetch_own = pltpu.make_async_copy(own_at, own, sems.at[0])
    fetch_own.start()
    fetch_fine = pltpu.make_async_copy(fine_at, fine, sems.at[1])
    fetch_fine.start()
    acc[...] = jnp.zeros_like(acc)
    turned[...] = jnp.zeros_like(turned)
    code_of = lambda k: jnp.where(k < p_count[0], codes[k], PB)
    fill_table(0, slots, table, code_of)
    fetch_own.wait()
    for k in range(slots):
        i = code_of(k) // CB
        j = pl.multiple_of((code_of(k) - i * CB) * size, size)
        turned[i, pl.ds(j, size), :] = own[k * size : (k + 1) * size, :].T
    fetch_fine.wait()

    def step(t, carry):
        products, targets = [], []
        for u in range(UNROLL):
            k = t * UNROLL + u
            products.append(jnp.dot(turned[rows[k]], fine[k], preferred_element_type=F32))
            targets.append(jnp.where(k < count[0], cols[k], NS * FB))
        for u in range(UNROLL):
            acc[targets[u]] += products[u]
        return carry

    lax.fori_loop(0, (count[0] + UNROLL - 1) // UNROLL, step, 0)
    stores = []
    for s in range(1, NS):
        for m in range(FB):
            stock[s - 1, :, m * size : (m + 1) * size] = acc[s * FB + m].astype(BF16)
        stock_at, n = (col_at, s - 1) if s < 3 else (row_at, s - 3)
        stores.append(pltpu.make_async_copy(stock.at[s - 1], stock_at.at[n], sems.at[1 + s]))
        stores[-1].start()
    own_weight = jnp.concatenate([acc[m].astype(BF16) for m in range(FB)], axis=1)
    dense_of(0, size, table, own, dense)
    coarse = coarse_of(size, own_weight, dense, tile)
    lift = lift_of(own, slots, size, lambda j: aggs[j])
    wide = CB * size
    more[0] = lift.T
    more[1] = coarse
    more[2] = lift
    stores.append(pltpu.make_async_copy(more, more_at, sems.at[0]))
    stores[-1].start()
    stores.append(pltpu.make_async_copy(tile, c_one.at[:, 0], sems.at[1]))
    stores[-1].start()
    for store in stores:
        store.wait()


def near_coarse(
    base, sources, near, slots, size, stock, c_one, dense, tiles, words, codes, sems
):
    tail = (slots + CB) * size
    for n, ref in enumerate(near):
        word = ref[tail : tail + META, :].astype(F32).astype(jnp.int32)
        words[n : n + 1, :] = word[0:1, :]
    fetch = pltpu.make_async_copy(words, codes, sems.at[0])
    fetch.start()
    fetch.wait()
    parts, stores = [], []
    for n, (s, ref) in enumerate(zip(sources, near)):
        dense_of(n, size, codes, ref, dense.at[n])
        coarse = coarse_of(size, stock[s - base], dense.at[n], tiles.at[n])
        store = pltpu.make_async_copy(tiles.at[n], c_one.at[:, s], sems.at[1 + n])
        store.start()
        stores.append(store)
        lift = lift_of(ref, slots, size, lambda j: codes[n, PB + j])
        parts.append(jnp.dot(coarse, lift, preferred_element_type=F32))
    return parts, stores


def half_kernel(more, lift_t, half):
    lift_t[...] = more[0]
    half[...] = jnp.dot(more[1], more[2], preferred_element_type=F32)


def side_kernel(slots, size, stock, lift_t, half, right, left, c_in, c_one, term, *scratch):
    parts, stores = near_coarse(1, (2, 1), (right, left), slots, size, stock, c_one, *scratch)
    whole = (half[...] + parts[0] + parts[1]).astype(BF16)
    term[...] = jnp.dot(lift_t[...], whole, preferred_element_type=F32)
    for store in stores:
        store.wait()


def row_kernel(slots, size, cols_n, stock, lift_t, term, other, pair, c_in, c_one, *rest):
    sends, terms, scratch = rest[:cols_n], rest[cols_n], rest[cols_n + 1 :]
    odd = lax.rem(lax.axis_index("row"), 2)
    sources = (3 + odd, 4 - odd)
    parts, stores = near_coarse(3, sources, (other, pair), slots, size, stock, c_one, *scratch)
    terms[0] = term[...]
    for n in range(2):
        terms[sources[n] - 2] = jnp.dot(lift_t[...], parts[n].astype(BF16), preferred_element_type=F32)
    chunk = terms.shape[1] // cols_n
    me = lax.axis_index("col")
    for d in range(cols_n):
        to = pl.multiple_of(lax.rem(me + d, cols_n) * chunk, chunk)
        sends[d][...] = terms[:, pl.ds(to, chunk), :].astype(sends[d].dtype)
    for store in stores:
        store.wait()


def sum_kernel(*refs):
    total = refs[0][...]
    for ref in refs[1:-1]:
        total = total + ref[...].astype(F32)
    refs[-1][...] = total.astype(BF16)


def spread_kernel(size, cols_n, *refs):
    parts, out_at, out, sems = refs[:cols_n], refs[cols_n], refs[cols_n + 1], refs[cols_n + 2]
    chunk = parts[0].shape[1]
    unit = math.gcd(chunk, size)
    per = size // unit
    me = lax.axis_index("col")
    stores = []
    for d in range(cols_n):
        owner = lax.rem(me - d + cols_n, cols_n)
        for t in range(chunk // unit):
            at = owner * (chunk // unit) + t
            a = at // per
            rows = pl.ds(pl.multiple_of(lax.rem(at, per) * unit, unit), unit)
            for g in range(3):
                for b in range(G2):
                    out[a, g, b, rows, :] = parts[d][
                        g, t * unit : (t + 1) * unit, b * size : (b + 1) * size
                    ].astype(F32)
            spot = (a, slice(None), slice(None), rows)
            stores.append(pltpu.make_async_copy(out.at[spot], out_at.at[spot], sems.at[len(stores)]))
            stores[-1].start()
    for store in stores:
        store.wait()


def shift(x, axis, step, wrap):
    n = lax.axis_size(axis)
    pairs = [(i, (i + step) % n) for i in range(n) if wrap or 0 <= i + step < n]
    return lax.ppermute(x, axis, pairs)


def swap(x, axis, pairs):
    return lax.ppermute(x, axis, pairs + [(j, i) for i, j in pairs])


def per_device(
    fine_blocks, fine_rows, fine_cols, fine_counts, prolong_blocks, prolong_codes,
    prolong_counts, second_blocks, second_aggs,
):
    slots, size = prolong_blocks.shape[2], prolong_blocks.shape[3]
    cap = fine_blocks.shape[2]
    cols_n = lax.axis_size("col")
    packed_rows = (slots + CB) * size + META
    wide = CB * size
    dma = pltpu.SemaphoreType.DMA
    packed = pl.pallas_call(
        pack_kernel,
        out_shape=jax.ShapeDtypeStruct((packed_rows, size), BF16),
        in_specs=[HBM] * 5,
        out_specs=HBM,
        scratch_shapes=[
            pltpu.VMEM((packed_rows, size), BF16),
            pltpu.SMEM(prolong_codes.shape, jnp.int32),
            pltpu.SMEM(prolong_counts.shape, jnp.int32),
            pltpu.SMEM(second_aggs.shape, jnp.int32),
            pltpu.SMEM((1, PB + 1), jnp.int32),
            dma((8,)),
        ],
        compiler_params=WHOLE,
        name="pack",
    )(
        prolong_codes, prolong_counts, second_aggs,
        prolong_blocks.reshape(slots * size, size),
        second_blocks.reshape(CB * size, size),
    )
    rows_n = lax.axis_size("row")
    pair = swap(packed, "row", [(i, i + 1) for i in range(0, rows_n - 1, 2)])
    other = swap(packed, "row", [(i, i + 1) for i in range(1, rows_n - 1, 2)])
    right = shift(packed, "col", -1, False)
    left = shift(packed, "col", 1, False)

    c_shape = jax.ShapeDtypeStruct((CB, NS, CB, size, size), BF16)
    table = pltpu.SMEM((1, PB + 1), jnp.int32)
    col_stock, row_stock, more, c_one = pl.pallas_call(
        functools.partial(own_kernel, slots, size),
        out_shape=[
            jax.ShapeDtypeStruct((2, wide, FB * size), BF16),
            jax.ShapeDtypeStruct((2, wide, FB * size), BF16),
            jax.ShapeDtypeStruct((3, wide, G2 * size), BF16),
            c_shape,
        ],
        in_specs=[SMEM] * 6 + [HBM] * 2,
        out_specs=[HBM] * 4,
        scratch_shapes=[
            pltpu.VMEM((cap, size, size), BF16),
            pltpu.VMEM((packed_rows, size), BF16),
            pltpu.VMEM((NS - 1, wide, FB * size), BF16),
            pltpu.VMEM((3, wide, G2 * size), BF16),
            pltpu.VMEM((FB + 1, wide, size), BF16),
            pltpu.VMEM((NS * FB + 1, wide, size), F32),
            pltpu.VMEM((FB * size, wide), BF16),
            pltpu.VMEM((CB, CB, size, size), BF16),
            table,
            dma((6,)),
        ],
        compiler_params=WHOLE,
        cost_estimate=pl.CostEstimate(flops=10**9, bytes_accessed=4 * 10**6, transcendentals=0),
        name="own_source",
    )(
        fine_rows[0, 0], fine_cols[0, 0], fine_counts[0],
        prolong_codes[0, 0], prolong_counts[0], second_aggs[0, 0],
        fine_blocks[0, 0], packed,
    )

    near_scratch = [
        pltpu.VMEM((2, FB * size, wide), BF16),
        pltpu.VMEM((2, CB, CB, size, size), BF16),
        pltpu.VMEM((8, size), jnp.int32),
        pltpu.SMEM((8, size), jnp.int32),
        dma((3,)),
    ]
    square = jax.ShapeDtypeStruct((wide, G2 * size), F32)
    lift_t, half = pl.pallas_call(
        half_kernel,
        out_shape=[jax.ShapeDtypeStruct((G2 * size, wide), BF16), square],
        in_specs=[VMEM],
        out_specs=[VMEM] * 2,
        compiler_params=SMALL,
        cost_estimate=pl.CostEstimate(flops=10**9, bytes_accessed=4 * 10**6, transcendentals=0),
        name="own_half",
    )(more)
    c_one, term = pl.pallas_call(
        functools.partial(side_kernel, slots, size),
        out_shape=[c_shape, square],
        in_specs=[VMEM] * 5 + [HBM],
        out_specs=[HBM, VMEM],
        input_output_aliases={5: 0},
        scratch_shapes=near_scratch,
        compiler_params=LARGE,
        name="col_sources",
    )(col_stock, lift_t, half, right, left, c_one)

    chunk = G2 * size // cols_n
    kept = jax.ShapeDtypeStruct((3, chunk, G2 * size), F32)
    piece = jax.ShapeDtypeStruct(kept.shape, BF16)
    c_one, *sends = pl.pallas_call(
        functools.partial(row_kernel, slots, size, cols_n),
        out_shape=[c_shape, kept] + [piece] * (cols_n - 1),
        in_specs=[VMEM] * 5 + [HBM],
        out_specs=[HBM] + [VMEM] * cols_n,
        input_output_aliases={5: 0},
        scratch_shapes=[pltpu.VMEM((3, G2 * size, G2 * size), F32)] + near_scratch,
        compiler_params=LARGE,
        name="row_sources",
    )(row_stock, lift_t, term, other, pair, c_one)
    parts = [sends[0]] + [shift(sends[d], "col", d, True) for d in range(1, cols_n)]
    total = pl.pallas_call(
        sum_kernel, out_shape=piece, in_specs=[VMEM] * cols_n, out_specs=VMEM,
        compiler_params=SMALL, name="total",
    )(*parts)
    gathered = [total] + [shift(total, "col", d, True) for d in range(1, cols_n)]
    c_two = pl.pallas_call(
        functools.partial(spread_kernel, size, cols_n),
        out_shape=jax.ShapeDtypeStruct((G2, 3, G2, size, size), F32),
        in_specs=[VMEM] * cols_n,
        out_specs=HBM,
        scratch_shapes=[
            pltpu.VMEM((G2, 3, G2, size, size), F32),
            dma((G2 * size // math.gcd(chunk, size),)),
        ],
        compiler_params=SMALL,
        name="spread",
    )(*gathered)
    return (c_one[None, None], c_two[None])


def solution(mesh):
    in_specs = (
        P("row", "col", None, None, None),
        P("row", "col", None),
        P("row", "col", None),
        P("row", "col"),
        P("row", "col", None, None, None),
        P("row", "col", None),
        P("row", "col"),
        P("row", "col", None, None, None),
        P("row", "col", None),
    )
    out_specs = (
        P("row", "col", None, None, None, None, None),
        P("row", None, None, None, None, None),
    )
    return jax.shard_map(
        per_device, mesh=mesh, in_specs=in_specs, out_specs=out_specs, check_vma=False
    )
```

```python
import functools
import math

import jax
import jax.numpy as jnp
from jax import lax
from jax.experimental import pallas as pl
from jax.experimental.pallas import tpu as pltpu
from jax.sharding import PartitionSpec as P

FB = 8
CB = 2
G2 = 2
NS = 5
PB = FB * CB
UNROLL = 8
META = 16
F32 = jnp.float32
BF16 = jnp.bfloat16

VMEM = pl.BlockSpec(memory_space=pltpu.VMEM)
HBM = pl.BlockSpec(memory_space=pltpu.HBM)
SMALL = pltpu.CompilerParams(vmem_limit_bytes=4 * 1024 * 1024)
SMEM = pl.BlockSpec(memory_space=pltpu.SMEM)
LARGE = pltpu.CompilerParams(vmem_limit_bytes=20 * 1024 * 1024)
WHOLE = pltpu.CompilerParams(vmem_limit_bytes=60 * 1024 * 1024)


def pack_kernel(
    codes_at, count_at, aggs_at, blocks, second, out, held, codes, count, aggs, table, sems
):
    n_p, n_s = blocks.shape[0], second.shape[0]
    slots, cut = codes_at.shape[-1], n_p // 2
    small = [
        pltpu.make_async_copy(a, b, sems.at[n])
        for n, (a, b) in enumerate([(codes_at, codes), (count_at, count), (aggs_at, aggs)])
    ]
    large = [
        pltpu.make_async_copy(blocks.at[0:cut], held.at[0:cut], sems.at[3]),
        pltpu.make_async_copy(blocks.at[cut:n_p], held.at[cut:n_p], sems.at[4]),
        pltpu.make_async_copy(second, held.at[n_p : n_p + n_s], sems.at[5]),
    ]
    for copy in small + large:
        copy.start()
    for copy in small:
        copy.wait()
    fill_table(0, slots, table, lambda k: jnp.where(k < count[0, 0], codes[0, 0, k], PB))
    lane = lax.broadcasted_iota(jnp.int32, (META, out.shape[1]), 1)
    word = jnp.zeros(lane.shape, jnp.int32)
    for q in range(PB):
        word = jnp.where(lane == q, table[0, q], word)
    for j in range(CB):
        word = jnp.where(lane == PB + j, aggs[0, 0, j], word)
    held[n_p + n_s : n_p + n_s + META, :] = word.astype(F32).astype(BF16)
    large[0].wait()
    stores = [pltpu.make_async_copy(held.at[0:cut], out.at[0:cut], sems.at[6])]
    stores[0].start()
    large[1].wait()
    large[2].wait()
    rest = pl.ds(cut, out.shape[0] - cut)
    stores.append(pltpu.make_async_copy(held.at[rest], out.at[rest], sems.at[7]))
    stores[1].start()
    for store in stores:
        store.wait()


def fill_table(s, slots, table, code_of):
    for q in range(PB + 1):
        table[s, q] = -1
    for k in range(slots):
        table[s, code_of(k)] = k


def block_at(s, q, size, table, near):
    slot = table[s, q]
    block = near[pl.ds(pl.multiple_of(jnp.maximum(slot, 0) * size, size), size), :]
    return jnp.where(slot >= 0, block, jnp.zeros_like(block))


def lift_of(near, slots, size, agg_of):
    lines = []
    for j in range(CB):
        block = near[(slots + j) * size : (slots + j + 1) * size, :]
        lines.append(
            jnp.concatenate(
                [jnp.where(agg_of(j) == a, block, jnp.zeros_like(block)) for a in range(G2)],
                axis=1,
            )
        )
    return jnp.concatenate(lines, axis=0)


def dense_of(s, size, table, near, dense):
    for i in range(FB):
        for j in range(CB):
            dense[i * size : (i + 1) * size, j * size : (j + 1) * size] = block_at(
                s, i * CB + j, size, table, near
            )


def coarse_of(size, weight, dense, tile):
    coarse = jnp.dot(weight, dense[...], preferred_element_type=F32).astype(BF16)
    for i in range(CB):
        for j in range(CB):
            tile[i, j] = coarse[i * size : (i + 1) * size, j * size : (j + 1) * size]
    return coarse


def own_kernel(
    slots, size, rows, cols, count, codes, p_count, aggs, fine_at, own_at,
    col_at, row_at, half_at, lift_at, c_one,
    fine, own, stock, half, lift_t, turned, acc, dense, tile, table, sems,
):
    fetch_own = pltpu.make_async_copy(own_at, own, sems.at[0])
    fetch_own.start()
    fetch_fine = pltpu.make_async_copy(fine_at, fine, sems.at[1])
    fetch_fine.start()
    acc[...] = jnp.zeros_like(acc)
    turned[...] = jnp.zeros_like(turned)
    code_of = lambda k: jnp.where(k < p_count[0], codes[k], PB)
    fill_table(0, slots, table, code_of)
    fetch_own.wait()
    for k in range(slots):
        i = code_of(k) // CB
        j = pl.multiple_of((code_of(k) - i * CB) * size, size)
        turned[i, pl.ds(j, size), :] = own[k * size : (k + 1) * size, :].T
    lift_t[...] = lift_of(own, slots, size, lambda j: aggs[j]).T
    fetch_fine.wait()
    stores = [pltpu.make_async_copy(lift_t, lift_at, sems.at[0])]
    stores[0].start()

    def step(t, carry):
        products, targets = [], []
        for u in range(UNROLL):
            k = t * UNROLL + u
            products.append(jnp.dot(turned[rows[k]], fine[k], preferred_element_type=F32))
            targets.append(jnp.where(k < count[0], cols[k], NS * FB))
        for u in range(UNROLL):
            acc[targets[u]] += products[u]
        return carry

    lax.fori_loop(0, (count[0] + UNROLL - 1) // UNROLL, step, 0)
    for s in range(1, NS):
        for m in range(FB):
            stock[s - 1, :, m * size : (m + 1) * size] = acc[s * FB + m].astype(BF16)
        stock_at, n = (col_at, s - 1) if s < 3 else (row_at, s - 3)
        stores.append(pltpu.make_async_copy(stock.at[s - 1], stock_at.at[n], sems.at[1 + s]))
        stores[-1].start()
    own_weight = jnp.concatenate([acc[m].astype(BF16) for m in range(FB)], axis=1)
    dense_of(0, size, table, own, dense)
    coarse = coarse_of(size, own_weight, dense, tile)
    lift = lift_of(own, slots, size, lambda j: aggs[j])
    half[...] = jnp.dot(coarse, lift, preferred_element_type=F32)
    stores.append(pltpu.make_async_copy(half, half_at, sems.at[6]))
    stores[-1].start()
    stores.append(pltpu.make_async_copy(tile, c_one.at[:, 0], sems.at[1]))
    stores[-1].start()
    for store in stores:
        store.wait()


def near_coarse(
    base, sources, near, slots, size, stock, c_one, dense, tiles, words, codes, sems
):
    tail = (slots + CB) * size
    for n, ref in enumerate(near):
        word = ref[tail : tail + META, :].astype(F32).astype(jnp.int32)
        words[n : n + 1, :] = word[0:1, :]
    fetch = pltpu.make_async_copy(words, codes, sems.at[0])
    fetch.start()
    fetch.wait()
    parts, stores = [], []
    for n, (s, ref) in enumerate(zip(sources, near)):
        dense_of(n, size, codes, ref, dense.at[n])
        coarse = coarse_of(size, stock[s - base], dense.at[n], tiles.at[n])
        store = pltpu.make_async_copy(tiles.at[n], c_one.at[:, s], sems.at[1 + n])
        store.start()
        stores.append(store)
        lift = lift_of(ref, slots, size, lambda j: codes[n, PB + j])
        parts.append(jnp.dot(coarse, lift, preferred_element_type=F32))
    return parts, stores


def pass_kernel(lift_in, lift_t):
    lift_t[...] = lift_in[...]


def side_kernel(slots, size, stock, lift_t, half, right, left, c_in, c_one, term, *scratch):
    parts, stores = near_coarse(1, (2, 1), (right, left), slots, size, stock, c_one, *scratch)
    whole = (half[...] + parts[0] + parts[1]).astype(BF16)
    term[...] = jnp.dot(lift_t[...], whole, preferred_element_type=F32)
    for store in stores:
        store.wait()


def row_kernel(slots, size, cols_n, stock, lift_t, term, other, pair, c_in, c_one, *rest):
    sends, terms, scratch = rest[:cols_n], rest[cols_n], rest[cols_n + 1 :]
    odd = lax.rem(lax.axis_index("row"), 2)
    sources = (3 + odd, 4 - odd)
    parts, stores = near_coarse(3, sources, (other, pair), slots, size, stock, c_one, *scratch)
    terms[0] = term[...]
    for n in range(2):
        terms[sources[n] - 2] = jnp.dot(lift_t[...], parts[n].astype(BF16), preferred_element_type=F32)
    chunk = terms.shape[1] // cols_n
    me = lax.axis_index("col")
    for d in range(cols_n):
        to = pl.multiple_of(partner(me, d, cols_n) * chunk, chunk)
        sends[d][...] = terms[:, pl.ds(to, chunk), :].astype(sends[d].dtype)
    for store in stores:
        store.wait()


def sum_kernel(*refs):
    total = refs[0][...]
    for ref in refs[1:-1]:
        total = total + ref[...].astype(F32)
    refs[-1][...] = total.astype(BF16)


def spread_kernel(size, steps, *refs):
    cols_n = len(steps)
    parts, out_at, out, sems = refs[:cols_n], refs[cols_n], refs[cols_n + 1], refs[cols_n + 2]
    chunk = parts[0].shape[1]
    unit = math.gcd(chunk, size)
    per = size // unit
    me = lax.axis_index("col")
    stores = []
    for n, d in enumerate(steps):
        owner = partner(me, -d, cols_n)
        for t in range(chunk // unit):
            at = owner * (chunk // unit) + t
            a = at // per
            rows = pl.ds(pl.multiple_of(lax.rem(at, per) * unit, unit), unit)
            for g in range(3):
                for b in range(G2):
                    out[a, g, b, rows, :] = parts[n][
                        g, t * unit : (t + 1) * unit, b * size : (b + 1) * size
                    ].astype(F32)
            spot = (a, slice(None), slice(None), rows)
            stores.append(pltpu.make_async_copy(out.at[spot], out_at.at[spot], sems.at[len(stores)]))
            stores[-1].start()
    for store in stores:
        store.wait()


def shift(x, axis, step):
    n = lax.axis_size(axis)
    return lax.ppermute(x, axis, [(i, i + step) for i in range(n) if 0 <= i + step < n])


def partner(c, d, n):
    return c ^ abs(d) if n & (n - 1) == 0 else (c + d + n) % n


def exchange(x, d):
    n = lax.axis_size("col")
    return lax.ppermute(x, "col", [(i, partner(i, d, n)) for i in range(n)])


def swap(x, axis, pairs):
    return lax.ppermute(x, axis, pairs + [(j, i) for i, j in pairs])


def per_device(
    fine_blocks, fine_rows, fine_cols, fine_counts, prolong_blocks, prolong_codes,
    prolong_counts, second_blocks, second_aggs,
):
    slots, size = prolong_blocks.shape[2], prolong_blocks.shape[3]
    cap = fine_blocks.shape[2]
    cols_n = lax.axis_size("col")
    packed_rows = (slots + CB) * size + META
    wide = CB * size
    dma = pltpu.SemaphoreType.DMA
    packed = pl.pallas_call(
        pack_kernel,
        out_shape=jax.ShapeDtypeStruct((packed_rows, size), BF16),
        in_specs=[HBM] * 5,
        out_specs=HBM,
        scratch_shapes=[
            pltpu.VMEM((packed_rows, size), BF16),
            pltpu.SMEM(prolong_codes.shape, jnp.int32),
            pltpu.SMEM(prolong_counts.shape, jnp.int32),
            pltpu.SMEM(second_aggs.shape, jnp.int32),
            pltpu.SMEM((1, PB + 1), jnp.int32),
            dma((8,)),
        ],
        compiler_params=WHOLE,
        name="pack",
    )(
        prolong_codes, prolong_counts, second_aggs,
        prolong_blocks.reshape(slots * size, size),
        second_blocks.reshape(CB * size, size),
    )
    rows_n = lax.axis_size("row")
    pair = swap(packed, "row", [(i, i + 1) for i in range(0, rows_n - 1, 2)])
    other = swap(packed, "row", [(i, i + 1) for i in range(1, rows_n - 1, 2)])
    right = shift(packed, "col", -1)
    left = shift(packed, "col", 1)

    c_shape = jax.ShapeDtypeStruct((CB, NS, CB, size, size), BF16)
    square = jax.ShapeDtypeStruct((wide, G2 * size), F32)
    table = pltpu.SMEM((1, PB + 1), jnp.int32)
    col_stock, row_stock, half, lift_t, c_one = pl.pallas_call(
        functools.partial(own_kernel, slots, size),
        out_shape=[
            jax.ShapeDtypeStruct((2, wide, FB * size), BF16),
            jax.ShapeDtypeStruct((2, wide, FB * size), BF16),
            square,
            jax.ShapeDtypeStruct((G2 * size, wide), BF16),
            c_shape,
        ],
        in_specs=[SMEM] * 6 + [HBM] * 2,
        out_specs=[HBM] * 5,
        scratch_shapes=[
            pltpu.VMEM((cap, size, size), BF16),
            pltpu.VMEM((packed_rows, size), BF16),
            pltpu.VMEM((NS - 1, wide, FB * size), BF16),
            pltpu.VMEM((wide, G2 * size), F32),
            pltpu.VMEM((G2 * size, wide), BF16),
            pltpu.VMEM((FB + 1, wide, size), BF16),
            pltpu.VMEM((NS * FB + 1, wide, size), F32),
            pltpu.VMEM((FB * size, wide), BF16),
            pltpu.VMEM((CB, CB, size, size), BF16),
            table,
            dma((7,)),
        ],
        compiler_params=WHOLE,
        cost_estimate=pl.CostEstimate(flops=10**9, bytes_accessed=4 * 10**6, transcendentals=0),
        name="own_source",
    )(
        fine_rows[0, 0], fine_cols[0, 0], fine_counts[0],
        prolong_codes[0, 0], prolong_counts[0], second_aggs[0, 0],
        fine_blocks[0, 0], packed,
    )

    near_scratch = [
        pltpu.VMEM((2, FB * size, wide), BF16),
        pltpu.VMEM((2, CB, CB, size, size), BF16),
        pltpu.VMEM((8, size), jnp.int32),
        pltpu.SMEM((8, size), jnp.int32),
        dma((3,)),
    ]
    lift_t = pl.pallas_call(
        pass_kernel,
        out_shape=jax.ShapeDtypeStruct((G2 * size, wide), BF16),
        in_specs=[VMEM],
        out_specs=VMEM,
        compiler_params=SMALL,
        cost_estimate=pl.CostEstimate(flops=10**9, bytes_accessed=4 * 10**6, transcendentals=0),
        name="pass_on",
    )(lift_t)
    c_one, term = pl.pallas_call(
        functools.partial(side_kernel, slots, size),
        out_shape=[c_shape, square],
        in_specs=[VMEM] * 5 + [HBM],
        out_specs=[HBM, VMEM],
        input_output_aliases={5: 0},
        scratch_shapes=near_scratch,
        compiler_params=LARGE,
        name="col_sources",
    )(col_stock, lift_t, half, right, left, c_one)

    chunk = G2 * size // cols_n
    kept = jax.ShapeDtypeStruct((3, chunk, G2 * size), F32)
    piece = jax.ShapeDtypeStruct(kept.shape, BF16)
    c_one, *sends = pl.pallas_call(
        functools.partial(row_kernel, slots, size, cols_n),
        out_shape=[c_shape, kept] + [piece] * (cols_n - 1),
        in_specs=[VMEM] * 5 + [HBM],
        out_specs=[HBM] + [VMEM] * cols_n,
        input_output_aliases={5: 0},
        scratch_shapes=[pltpu.VMEM((3, G2 * size, G2 * size), F32)] + near_scratch,
        compiler_params=LARGE,
        name="row_sources",
    )(row_stock, lift_t, term, other, pair, c_one)
    steps = list(range(cols_n - 1, 0, -1))
    parts = [sends[0]] + [exchange(sends[d], d) for d in steps]
    total = pl.pallas_call(
        sum_kernel, out_shape=piece, in_specs=[VMEM] * cols_n, out_specs=VMEM,
        compiler_params=SMALL, name="total",
    )(*parts)
    gathered = [total] + [exchange(total, d) for d in steps]
    c_two = pl.pallas_call(
        functools.partial(spread_kernel, size, [0] + steps),
        out_shape=jax.ShapeDtypeStruct((G2, 3, G2, size, size), F32),
        in_specs=[VMEM] * cols_n,
        out_specs=HBM,
        scratch_shapes=[
            pltpu.VMEM((G2, 3, G2, size, size), F32),
            dma((G2 * size // math.gcd(chunk, size),)),
        ],
        compiler_params=SMALL,
        name="spread",
    )(*gathered)
    return (c_one[None, None], c_two[None])


def solution(mesh):
    in_specs = (
        P("row", "col", None, None, None),
        P("row", "col", None),
        P("row", "col", None),
        P("row", "col"),
        P("row", "col", None, None, None),
        P("row", "col", None),
        P("row", "col"),
        P("row", "col", None, None, None),
        P("row", "col", None),
    )
    out_specs = (
        P("row", "col", None, None, None, None, None),
        P("row", None, None, None, None, None),
    )
    return jax.shard_map(
        per_device, mesh=mesh, in_specs=in_specs, out_specs=out_specs, check_vma=False
    )
```

```python
import functools
import math

import jax
import jax.numpy as jnp
from jax import lax
from jax.experimental import pallas as pl
from jax.experimental.pallas import tpu as pltpu
from jax.sharding import PartitionSpec as P

FB = 8
CB = 2
G2 = 2
NS = 5
PB = FB * CB
UNROLL = 8
META = 16
F32 = jnp.float32
BF16 = jnp.bfloat16

VMEM = pl.BlockSpec(memory_space=pltpu.VMEM)
HBM = pl.BlockSpec(memory_space=pltpu.HBM)
SMALL = pltpu.CompilerParams(vmem_limit_bytes=4 * 1024 * 1024)
LARGE = pltpu.CompilerParams(vmem_limit_bytes=20 * 1024 * 1024)
WHOLE = pltpu.CompilerParams(vmem_limit_bytes=60 * 1024 * 1024)


def pack_kernel(
    codes_at, count_at, aggs_at, blocks, second, out, held, codes, count, aggs, table, sems
):
    n_p, n_s = blocks.shape[0], second.shape[0]
    slots, cut = codes_at.shape[-1], n_p // 2
    small = [
        pltpu.make_async_copy(a, b, sems.at[n])
        for n, (a, b) in enumerate([(codes_at, codes), (count_at, count), (aggs_at, aggs)])
    ]
    large = [
        pltpu.make_async_copy(blocks.at[0:cut], held.at[0:cut], sems.at[3]),
        pltpu.make_async_copy(blocks.at[cut:n_p], held.at[cut:n_p], sems.at[4]),
        pltpu.make_async_copy(second, held.at[n_p : n_p + n_s], sems.at[5]),
    ]
    for copy in small + large:
        copy.start()
    for copy in small:
        copy.wait()
    fill_table(0, slots, table, lambda k: jnp.where(k < count[0, 0], codes[0, 0, k], PB))
    lane = lax.broadcasted_iota(jnp.int32, (META, out.shape[1]), 1)
    word = jnp.zeros(lane.shape, jnp.int32)
    for q in range(PB):
        word = jnp.where(lane == q, table[0, q], word)
    for j in range(CB):
        word = jnp.where(lane == PB + j, aggs[0, 0, j], word)
    held[n_p + n_s : n_p + n_s + META, :] = word.astype(F32).astype(BF16)
    large[0].wait()
    stores = [pltpu.make_async_copy(held.at[0:cut], out.at[0:cut], sems.at[6])]
    stores[0].start()
    large[1].wait()
    large[2].wait()
    rest = pl.ds(cut, out.shape[0] - cut)
    stores.append(pltpu.make_async_copy(held.at[rest], out.at[rest], sems.at[7]))
    stores[1].start()
    for store in stores:
        store.wait()


def fill_table(s, slots, table, code_of):
    for q in range(PB + 1):
        table[s, q] = -1
    for k in range(slots):
        table[s, code_of(k)] = k


def block_at(s, q, size, table, near):
    slot = table[s, q]
    block = near[pl.ds(pl.multiple_of(jnp.maximum(slot, 0) * size, size), size), :]
    return jnp.where(slot >= 0, block, jnp.zeros_like(block))


def lift_of(near, slots, size, agg_of):
    lines = []
    for j in range(CB):
        block = near[(slots + j) * size : (slots + j + 1) * size, :]
        lines.append(
            jnp.concatenate(
                [jnp.where(agg_of(j) == a, block, jnp.zeros_like(block)) for a in range(G2)],
                axis=1,
            )
        )
    return jnp.concatenate(lines, axis=0)


def dense_of(s, size, table, near, dense):
    for i in range(FB):
        for j in range(CB):
            dense[i * size : (i + 1) * size, j * size : (j + 1) * size] = block_at(
                s, i * CB + j, size, table, near
            )


def coarse_of(size, weight, dense, tile):
    coarse = jnp.dot(weight, dense[...], preferred_element_type=F32).astype(BF16)
    for i in range(CB):
        for j in range(CB):
            tile[i, j] = coarse[i * size : (i + 1) * size, j * size : (j + 1) * size]
    return coarse


def own_kernel(
    slots, size, rows_at, cols_at, count_at, codes_at, p_count_at, aggs_at, fine_at, own_at,
    col_at, row_at, more_at, c_one,
    fine, own, stock, more, turned, acc, dense, tile, rows, cols, count, codes, p_count, aggs, table, sems,
):
    pairs = [
        (rows_at, rows), (cols_at, cols), (count_at, count), (codes_at, codes),
        (p_count_at, p_count), (aggs_at, aggs),
    ]
    small = [pltpu.make_async_copy(a, b, sems.at[2 + n]) for n, (a, b) in enumerate(pairs)]
    for copy in small:
        copy.start()
    fetch_own = pltpu.make_async_copy(own_at, own, sems.at[0])
    fetch_own.start()
    fetch_fine = pltpu.make_async_copy(fine_at, fine, sems.at[1])
    fetch_fine.start()
    acc[...] = jnp.zeros_like(acc)
    turned[...] = jnp.zeros_like(turned)
    for copy in small:
        copy.wait()
    code_of = lambda k: jnp.where(k < p_count[0, 0], codes[0, 0, k], PB)
    fill_table(0, slots, table, code_of)
    fetch_own.wait()
    for k in range(slots):
        i = code_of(k) // CB
        j = pl.multiple_of((code_of(k) - i * CB) * size, size)
        turned[i, pl.ds(j, size), :] = own[k * size : (k + 1) * size, :].T
    fetch_fine.wait()

    def step(t, carry):
        products, targets = [], []
        for u in range(UNROLL):
            k = t * UNROLL + u
            products.append(jnp.dot(turned[rows[0, 0, k]], fine[k], preferred_element_type=F32))
            targets.append(jnp.where(k < count[0, 0], cols[0, 0, k], NS * FB))
        for u in range(UNROLL):
            acc[targets[u]] += products[u]
        return carry

    lax.fori_loop(0, (count[0, 0] + UNROLL - 1) // UNROLL, step, 0)
    stores = []
    for s in range(1, NS):
        for m in range(FB):
            stock[s - 1, :, m * size : (m + 1) * size] = acc[s * FB + m].astype(BF16)
        stock_at, n = (col_at, s - 1) if s < 3 else (row_at, s - 3)
        stores.append(pltpu.make_async_copy(stock.at[s - 1], stock_at.at[n], sems.at[1 + s]))
        stores[-1].start()
    own_weight = jnp.concatenate([acc[m].astype(BF16) for m in range(FB)], axis=1)
    dense_of(0, size, table, own, dense)
    coarse = coarse_of(size, own_weight, dense, tile)
    lift = lift_of(own, slots, size, lambda j: aggs[0, 0, j])
    wide = CB * size
    more[0] = lift.T
    more[1] = coarse
    more[2] = lift
    stores.append(pltpu.make_async_copy(more, more_at, sems.at[0]))
    stores[-1].start()
    stores.append(pltpu.make_async_copy(tile, c_one.at[:, 0], sems.at[1]))
    stores[-1].start()
    for store in stores:
        store.wait()


def near_coarse(
    base, sources, near, slots, size, stock, c_one, dense, tiles, words, codes, sems
):
    tail = (slots + CB) * size
    for n, ref in enumerate(near):
        word = ref[tail : tail + META, :].astype(F32).astype(jnp.int32)
        words[n : n + 1, :] = word[0:1, :]
    fetch = pltpu.make_async_copy(words, codes, sems.at[0])
    fetch.start()
    fetch.wait()
    parts, stores = [], []
    for n, (s, ref) in enumerate(zip(sources, near)):
        dense_of(n, size, codes, ref, dense.at[n])
        coarse = coarse_of(size, stock[s - base], dense.at[n], tiles.at[n])
        store = pltpu.make_async_copy(tiles.at[n], c_one.at[:, s], sems.at[1 + n])
        store.start()
        stores.append(store)
        lift = lift_of(ref, slots, size, lambda j: codes[n, PB + j])
        parts.append(jnp.dot(coarse, lift, preferred_element_type=F32))
    return parts, stores


def half_kernel(more, lift_t, half):
    lift_t[...] = more[0]
    half[...] = jnp.dot(more[1], more[2], preferred_element_type=F32)


def side_kernel(slots, size, stock, lift_t, half, right, left, c_in, c_one, term, *scratch):
    parts, stores = near_coarse(1, (2, 1), (right, left), slots, size, stock, c_one, *scratch)
    whole = (half[...] + parts[0] + parts[1]).astype(BF16)
    term[...] = jnp.dot(lift_t[...], whole, preferred_element_type=F32)
    for store in stores:
        store.wait()


def row_kernel(slots, size, cols_n, stock, lift_t, term, other, pair, c_in, c_one, *rest):
    sends, terms, scratch = rest[:cols_n], rest[cols_n], rest[cols_n + 1 :]
    odd = lax.rem(lax.axis_index("row"), 2)
    sources = (3 + odd, 4 - odd)
    parts, stores = near_coarse(3, sources, (other, pair), slots, size, stock, c_one, *scratch)
    terms[0] = term[...]
    for n in range(2):
        terms[sources[n] - 2] = jnp.dot(lift_t[...], parts[n].astype(BF16), preferred_element_type=F32)
    chunk = terms.shape[1] // cols_n
    me = lax.axis_index("col")
    for d in range(cols_n):
        to = pl.multiple_of(lax.rem(me + d, cols_n) * chunk, chunk)
        sends[d][...] = terms[:, pl.ds(to, chunk), :].astype(sends[d].dtype)
    for store in stores:
        store.wait()


def sum_kernel(*refs):
    total = refs[0][...]
    for ref in refs[1:-1]:
        total = total + ref[...].astype(F32)
    refs[-1][...] = total.astype(BF16)


def spread_kernel(size, cols_n, *refs):
    parts, out_at, out, sems = refs[:cols_n], refs[cols_n], refs[cols_n + 1], refs[cols_n + 2]
    chunk = parts[0].shape[1]
    unit = math.gcd(chunk, size)
    per = size // unit
    me = lax.axis_index("col")
    stores = []
    for d in range(cols_n):
        owner = lax.rem(me - d + cols_n, cols_n)
        for t in range(chunk // unit):
            at = owner * (chunk // unit) + t
            a = at // per
            rows = pl.ds(pl.multiple_of(lax.rem(at, per) * unit, unit), unit)
            for g in range(3):
                for b in range(G2):
                    out[a, g, b, rows, :] = parts[d][
                        g, t * unit : (t + 1) * unit, b * size : (b + 1) * size
                    ].astype(F32)
            spot = (a, slice(None), slice(None), rows)
            stores.append(pltpu.make_async_copy(out.at[spot], out_at.at[spot], sems.at[len(stores)]))
            stores[-1].start()
    for store in stores:
        store.wait()


def shift(x, axis, step, wrap):
    n = lax.axis_size(axis)
    pairs = [(i, (i + step) % n) for i in range(n) if wrap or 0 <= i + step < n]
    return lax.ppermute(x, axis, pairs)


def swap(x, axis, pairs):
    return lax.ppermute(x, axis, pairs + [(j, i) for i, j in pairs])


def per_device(
    fine_blocks, fine_rows, fine_cols, fine_counts, prolong_blocks, prolong_codes,
    prolong_counts, second_blocks, second_aggs,
):
    slots, size = prolong_blocks.shape[2], prolong_blocks.shape[3]
    cap = fine_blocks.shape[2]
    cols_n = lax.axis_size("col")
    packed_rows = (slots + CB) * size + META
    wide = CB * size
    dma = pltpu.SemaphoreType.DMA
    packed = pl.pallas_call(
        pack_kernel,
        out_shape=jax.ShapeDtypeStruct((packed_rows, size), BF16),
        in_specs=[HBM] * 5,
        out_specs=HBM,
        scratch_shapes=[
            pltpu.VMEM((packed_rows, size), BF16),
            pltpu.SMEM(prolong_codes.shape, jnp.int32),
            pltpu.SMEM(prolong_counts.shape, jnp.int32),
            pltpu.SMEM(second_aggs.shape, jnp.int32),
            pltpu.SMEM((1, PB + 1), jnp.int32),
            dma((8,)),
        ],
        compiler_params=WHOLE,
        name="pack",
    )(
        prolong_codes, prolong_counts, second_aggs,
        prolong_blocks.reshape(slots * size, size),
        second_blocks.reshape(CB * size, size),
    )
    rows_n = lax.axis_size("row")
    pair = swap(packed, "row", [(i, i + 1) for i in range(0, rows_n - 1, 2)])
    other = swap(packed, "row", [(i, i + 1) for i in range(1, rows_n - 1, 2)])
    right = shift(packed, "col", -1, False)
    left = shift(packed, "col", 1, False)

    c_shape = jax.ShapeDtypeStruct((CB, NS, CB, size, size), BF16)
    table = pltpu.SMEM((1, PB + 1), jnp.int32)
    integers = (
        fine_rows, fine_cols, fine_counts, prolong_codes, prolong_counts, second_aggs
    )
    col_stock, row_stock, more, c_one = pl.pallas_call(
        functools.partial(own_kernel, slots, size),
        out_shape=[
            jax.ShapeDtypeStruct((2, wide, FB * size), BF16),
            jax.ShapeDtypeStruct((2, wide, FB * size), BF16),
            jax.ShapeDtypeStruct((3, wide, G2 * size), BF16),
            c_shape,
        ],
        in_specs=[HBM] * 8,
        out_specs=[HBM] * 4,
        scratch_shapes=[
            pltpu.VMEM((cap, size, size), BF16),
            pltpu.VMEM((packed_rows, size), BF16),
            pltpu.VMEM((NS - 1, wide, FB * size), BF16),
            pltpu.VMEM((3, wide, G2 * size), BF16),
            pltpu.VMEM((FB + 1, wide, size), BF16),
            pltpu.VMEM((NS * FB + 1, wide, size), F32),
            pltpu.VMEM((FB * size, wide), BF16),
            pltpu.VMEM((CB, CB, size, size), BF16),
            *[pltpu.SMEM(x.shape, jnp.int32) for x in integers],
            table,
            dma((8,)),
        ],
        compiler_params=WHOLE,
        cost_estimate=pl.CostEstimate(flops=10**9, bytes_accessed=4 * 10**6, transcendentals=0),
        name="own_source",
    )(
        *integers, fine_blocks[0, 0], packed,
    )

    near_scratch = [
        pltpu.VMEM((2, FB * size, wide), BF16),
        pltpu.VMEM((2, CB, CB, size, size), BF16),
        pltpu.VMEM((8, size), jnp.int32),
        pltpu.SMEM((8, size), jnp.int32),
        dma((3,)),
    ]
    square = jax.ShapeDtypeStruct((wide, G2 * size), F32)
    lift_t, half = pl.pallas_call(
        half_kernel,
        out_shape=[jax.ShapeDtypeStruct((G2 * size, wide), BF16), square],
        in_specs=[VMEM],
        out_specs=[VMEM] * 2,
        compiler_params=SMALL,
        cost_estimate=pl.CostEstimate(flops=10**9, bytes_accessed=4 * 10**6, transcendentals=0),
        name="own_half",
    )(more)
    c_one, term = pl.pallas_call(
        functools.partial(side_kernel, slots, size),
        out_shape=[c_shape, square],
        in_specs=[VMEM] * 5 + [HBM],
        out_specs=[HBM, VMEM],
        input_output_aliases={5: 0},
        scratch_shapes=near_scratch,
        compiler_params=LARGE,
        name="col_sources",
    )(col_stock, lift_t, half, right, left, c_one)

    chunk = G2 * size // cols_n
    kept = jax.ShapeDtypeStruct((3, chunk, G2 * size), F32)
    piece = jax.ShapeDtypeStruct(kept.shape, BF16)
    c_one, *sends = pl.pallas_call(
        functools.partial(row_kernel, slots, size, cols_n),
        out_shape=[c_shape, kept] + [piece] * (cols_n - 1),
        in_specs=[VMEM] * 5 + [HBM],
        out_specs=[HBM] + [VMEM] * cols_n,
        input_output_aliases={5: 0},
        scratch_shapes=[pltpu.VMEM((3, G2 * size, G2 * size), F32)] + near_scratch,
        compiler_params=LARGE,
        name="row_sources",
    )(row_stock, lift_t, term, other, pair, c_one)
    parts = [sends[0]] + [shift(sends[d], "col", d, True) for d in range(1, cols_n)]
    total = pl.pallas_call(
        sum_kernel, out_shape=piece, in_specs=[VMEM] * cols_n, out_specs=VMEM,
        compiler_params=SMALL, name="total",
    )(*parts)
    gathered = [total] + [shift(total, "col", d, True) for d in range(1, cols_n)]
    c_two = pl.pallas_call(
        functools.partial(spread_kernel, size, cols_n),
        out_shape=jax.ShapeDtypeStruct((G2, 3, G2, size, size), F32),
        in_specs=[VMEM] * cols_n,
        out_specs=HBM,
        scratch_shapes=[
            pltpu.VMEM((G2, 3, G2, size, size), F32),
            dma((G2 * size // math.gcd(chunk, size),)),
        ],
        compiler_params=SMALL,
        name="spread",
    )(*gathered)
    return (c_one[None, None], c_two[None])


def solution(mesh):
    in_specs = (
        P("row", "col", None, None, None),
        P("row", "col", None),
        P("row", "col", None),
        P("row", "col"),
        P("row", "col", None, None, None),
        P("row", "col", None),
        P("row", "col"),
        P("row", "col", None, None, None),
        P("row", "col", None),
    )
    out_specs = (
        P("row", "col", None, None, None, None, None),
        P("row", None, None, None, None, None),
    )
    return jax.shard_map(
        per_device, mesh=mesh, in_specs=in_specs, out_specs=out_specs, check_vma=False
    )
```

```python
import functools
import math

import jax
import jax.numpy as jnp
from jax import lax
from jax.experimental import pallas as pl
from jax.experimental.pallas import tpu as pltpu
from jax.sharding import PartitionSpec as P

FB = 8
CB = 2
G2 = 2
NS = 5
PB = FB * CB
UNROLL = 8
META = 16
F32 = jnp.float32
BF16 = jnp.bfloat16

VMEM = pl.BlockSpec(memory_space=pltpu.VMEM)
HBM = pl.BlockSpec(memory_space=pltpu.HBM)
SMALL = pltpu.CompilerParams(vmem_limit_bytes=4 * 1024 * 1024)
LARGE = pltpu.CompilerParams(vmem_limit_bytes=20 * 1024 * 1024)
WHOLE = pltpu.CompilerParams(vmem_limit_bytes=60 * 1024 * 1024)


def pack_kernel(
    codes_at, count_at, aggs_at, blocks, second, out, held, codes, count, aggs, table, sems
):
    n_p, n_s = blocks.shape[0], second.shape[0]
    slots, cut = codes_at.shape[-1], n_p // 2
    small = [
        pltpu.make_async_copy(a, b, sems.at[n])
        for n, (a, b) in enumerate([(codes_at, codes), (count_at, count), (aggs_at, aggs)])
    ]
    large = [
        pltpu.make_async_copy(blocks.at[0:cut], held.at[0:cut], sems.at[3]),
        pltpu.make_async_copy(blocks.at[cut:n_p], held.at[cut:n_p], sems.at[4]),
        pltpu.make_async_copy(second, held.at[n_p : n_p + n_s], sems.at[5]),
    ]
    for copy in small + large:
        copy.start()
    for copy in small:
        copy.wait()
    fill_table(0, slots, table, lambda k: jnp.where(k < count[0, 0], codes[0, 0, k], PB))
    lane = lax.broadcasted_iota(jnp.int32, (META, out.shape[1]), 1)
    word = jnp.zeros(lane.shape, jnp.int32)
    for q in range(PB):
        word = jnp.where(lane == q, table[0, q], word)
    for j in range(CB):
        word = jnp.where(lane == PB + j, aggs[0, 0, j], word)
    held[n_p + n_s : n_p + n_s + META, :] = word.astype(F32).astype(BF16)
    large[0].wait()
    stores = [pltpu.make_async_copy(held.at[0:cut], out.at[0:cut], sems.at[6])]
    stores[0].start()
    large[1].wait()
    large[2].wait()
    rest = pl.ds(cut, out.shape[0] - cut)
    stores.append(pltpu.make_async_copy(held.at[rest], out.at[rest], sems.at[7]))
    stores[1].start()
    for store in stores:
        store.wait()


def fill_table(s, slots, table, code_of):
    for q in range(PB + 1):
        table[s, q] = -1
    for k in range(slots):
        table[s, code_of(k)] = k


def block_at(s, q, size, table, near):
    slot = table[s, q]
    block = near[pl.ds(pl.multiple_of(jnp.maximum(slot, 0) * size, size), size), :]
    return jnp.where(slot >= 0, block, jnp.zeros_like(block))


def lift_of(near, slots, size, agg_of):
    lines = []
    for j in range(CB):
        block = near[(slots + j) * size : (slots + j + 1) * size, :]
        lines.append(
            jnp.concatenate(
                [jnp.where(agg_of(j) == a, block, jnp.zeros_like(block)) for a in range(G2)],
                axis=1,
            )
        )
    return jnp.concatenate(lines, axis=0)


def dense_of(s, size, table, near, dense):
    for i in range(FB):
        for j in range(CB):
            dense[i * size : (i + 1) * size, j * size : (j + 1) * size] = block_at(
                s, i * CB + j, size, table, near
            )


def coarse_of(size, weight, dense, tile):
    coarse = jnp.dot(weight, dense[...], preferred_element_type=F32).astype(BF16)
    for i in range(CB):
        for j in range(CB):
            tile[i, j] = coarse[i * size : (i + 1) * size, j * size : (j + 1) * size]
    return coarse


def own_kernel(
    slots, size, rows_at, cols_at, count_at, codes_at, p_count_at, aggs_at, fine_at, own_at,
    col_at, row_at, more_at, c_one,
    fine, own, stock, more, turned, acc, dense, tile, rows, cols, count, codes, p_count, aggs, table, sems,
):
    pairs = [
        (rows_at, rows), (cols_at, cols), (count_at, count), (codes_at, codes),
        (p_count_at, p_count), (aggs_at, aggs),
    ]
    small = [pltpu.make_async_copy(a, b, sems.at[2 + n]) for n, (a, b) in enumerate(pairs)]
    for copy in small:
        copy.start()
    fetch_own = pltpu.make_async_copy(own_at, own, sems.at[0])
    fetch_own.start()
    fetch_fine = pltpu.make_async_copy(fine_at, fine, sems.at[1])
    fetch_fine.start()
    acc[...] = jnp.zeros_like(acc)
    turned[...] = jnp.zeros_like(turned)
    for copy in small:
        copy.wait()
    code_of = lambda k: jnp.where(k < p_count[0, 0], codes[0, 0, k], PB)
    fill_table(0, slots, table, code_of)
    fetch_own.wait()
    for k in range(slots):
        i = code_of(k) // CB
        j = pl.multiple_of((code_of(k) - i * CB) * size, size)
        turned[i, pl.ds(j, size), :] = own[k * size : (k + 1) * size, :].T
    fetch_fine.wait()

    def step(t, carry):
        for u in range(UNROLL):
            k = t * UNROLL + u
            target = jnp.where(k < count[0, 0], cols[0, 0, k], NS * FB)
            acc[target] += jnp.dot(turned[rows[0, 0, k]], fine[k], preferred_element_type=F32)
        return carry

    lax.fori_loop(0, (count[0, 0] + UNROLL - 1) // UNROLL, step, 0)
    stores = []
    for s in range(1, NS):
        for m in range(FB):
            stock[s - 1, :, m * size : (m + 1) * size] = acc[s * FB + m].astype(BF16)
        stock_at, n = (col_at, s - 1) if s < 3 else (row_at, s - 3)
        stores.append(pltpu.make_async_copy(stock.at[s - 1], stock_at.at[n], sems.at[1 + s]))
        stores[-1].start()
    own_weight = jnp.concatenate([acc[m].astype(BF16) for m in range(FB)], axis=1)
    dense_of(0, size, table, own, dense)
    coarse = coarse_of(size, own_weight, dense, tile)
    lift = lift_of(own, slots, size, lambda j: aggs[0, 0, j])
    wide = CB * size
    more[0] = lift.T
    more[1] = coarse
    more[2] = lift
    stores.append(pltpu.make_async_copy(more, more_at, sems.at[0]))
    stores[-1].start()
    stores.append(pltpu.make_async_copy(tile, c_one.at[:, 0], sems.at[1]))
    stores[-1].start()
    for store in stores:
        store.wait()


def near_coarse(
    base, sources, near, slots, size, stock, c_one, dense, tiles, words, codes, sems
):
    tail = (slots + CB) * size
    for n, ref in enumerate(near):
        word = ref[tail : tail + META, :].astype(F32).astype(jnp.int32)
        words[n : n + 1, :] = word[0:1, :]
    fetch = pltpu.make_async_copy(words, codes, sems.at[0])
    fetch.start()
    fetch.wait()
    parts, stores = [], []
    for n, (s, ref) in enumerate(zip(sources, near)):
        dense_of(n, size, codes, ref, dense.at[n])
        coarse = coarse_of(size, stock[s - base], dense.at[n], tiles.at[n])
        store = pltpu.make_async_copy(tiles.at[n], c_one.at[:, s], sems.at[1 + n])
        store.start()
        stores.append(store)
        lift = lift_of(ref, slots, size, lambda j: codes[n, PB + j])
        parts.append(jnp.dot(coarse, lift, preferred_element_type=F32))
    return parts, stores


def half_kernel(more, lift_t, half):
    lift_t[...] = more[0]
    half[...] = jnp.dot(more[1], more[2], preferred_element_type=F32)


def side_kernel(slots, size, stock, lift_t, half, right, left, c_in, c_one, term, *scratch):
    parts, stores = near_coarse(1, (2, 1), (right, left), slots, size, stock, c_one, *scratch)
    whole = (half[...] + parts[0] + parts[1]).astype(BF16)
    term[...] = jnp.dot(lift_t[...], whole, preferred_element_type=F32)
    for store in stores:
        store.wait()


def row_kernel(slots, size, cols_n, stock, lift_t, term, other, pair, c_in, c_one, *rest):
    sends, terms, scratch = rest[:cols_n], rest[cols_n], rest[cols_n + 1 :]
    odd = lax.rem(lax.axis_index("row"), 2)
    sources = (3 + odd, 4 - odd)
    parts, stores = near_coarse(3, sources, (other, pair), slots, size, stock, c_one, *scratch)
    terms[0] = term[...]
    for n in range(2):
        terms[sources[n] - 2] = jnp.dot(lift_t[...], parts[n].astype(BF16), preferred_element_type=F32)
    chunk = terms.shape[1] // cols_n
    me = lax.axis_index("col")
    for d in range(cols_n):
        to = pl.multiple_of(lax.rem(me + d, cols_n) * chunk, chunk)
        sends[d][...] = terms[:, pl.ds(to, chunk), :].astype(sends[d].dtype)
    for store in stores:
        store.wait()


def sum_kernel(*refs):
    total = refs[0][...]
    for ref in refs[1:-1]:
        total = total + ref[...].astype(F32)
    refs[-1][...] = total.astype(BF16)


def spread_kernel(size, cols_n, *refs):
    parts, out_at, out, sems = refs[:cols_n], refs[cols_n], refs[cols_n + 1], refs[cols_n + 2]
    chunk = parts[0].shape[1]
    unit = math.gcd(chunk, size)
    per = size // unit
    me = lax.axis_index("col")
    stores = []
    for d in range(cols_n):
        owner = lax.rem(me - d + cols_n, cols_n)
        for t in range(chunk // unit):
            at = owner * (chunk // unit) + t
            a = at // per
            rows = pl.ds(pl.multiple_of(lax.rem(at, per) * unit, unit), unit)
            for g in range(3):
                for b in range(G2):
                    out[a, g, b, rows, :] = parts[d][
                        g, t * unit : (t + 1) * unit, b * size : (b + 1) * size
                    ].astype(F32)
            spot = (a, slice(None), slice(None), rows)
            stores.append(pltpu.make_async_copy(out.at[spot], out_at.at[spot], sems.at[len(stores)]))
            stores[-1].start()
    for store in stores:
        store.wait()


def shift(x, axis, step, wrap):
    n = lax.axis_size(axis)
    pairs = [(i, (i + step) % n) for i in range(n) if wrap or 0 <= i + step < n]
    return lax.ppermute(x, axis, pairs)


def swap(x, axis, pairs):
    return lax.ppermute(x, axis, pairs + [(j, i) for i, j in pairs])


def per_device(
    fine_blocks, fine_rows, fine_cols, fine_counts, prolong_blocks, prolong_codes,
    prolong_counts, second_blocks, second_aggs,
):
    slots, size = prolong_blocks.shape[2], prolong_blocks.shape[3]
    cap = fine_blocks.shape[2]
    cols_n = lax.axis_size("col")
    packed_rows = (slots + CB) * size + META
    wide = CB * size
    dma = pltpu.SemaphoreType.DMA
    packed = pl.pallas_call(
        pack_kernel,
        out_shape=jax.ShapeDtypeStruct((packed_rows, size), BF16),
        in_specs=[HBM] * 5,
        out_specs=HBM,
        scratch_shapes=[
            pltpu.VMEM((packed_rows, size), BF16),
            pltpu.SMEM(prolong_codes.shape, jnp.int32),
            pltpu.SMEM(prolong_counts.shape, jnp.int32),
            pltpu.SMEM(second_aggs.shape, jnp.int32),
            pltpu.SMEM((1, PB + 1), jnp.int32),
            dma((8,)),
        ],
        compiler_params=WHOLE,
        name="pack",
    )(
        prolong_codes, prolong_counts, second_aggs,
        prolong_blocks.reshape(slots * size, size),
        second_blocks.reshape(CB * size, size),
    )
    rows_n = lax.axis_size("row")
    pair = swap(packed, "row", [(i, i + 1) for i in range(0, rows_n - 1, 2)])
    other = swap(packed, "row", [(i, i + 1) for i in range(1, rows_n - 1, 2)])
    right = shift(packed, "col", -1, False)
    left = shift(packed, "col", 1, False)

    c_shape = jax.ShapeDtypeStruct((CB, NS, CB, size, size), BF16)
    table = pltpu.SMEM((1, PB + 1), jnp.int32)
    integers = (
        fine_rows, fine_cols, fine_counts, prolong_codes, prolong_counts, second_aggs
    )
    col_stock, row_stock, more, c_one = pl.pallas_call(
        functools.partial(own_kernel, slots, size),
        out_shape=[
            jax.ShapeDtypeStruct((2, wide, FB * size), BF16),
            jax.ShapeDtypeStruct((2, wide, FB * size), BF16),
            jax.ShapeDtypeStruct((3, wide, G2 * size), BF16),
            c_shape,
        ],
        in_specs=[HBM] * 8,
        out_specs=[HBM] * 4,
        scratch_shapes=[
            pltpu.VMEM((cap, size, size), BF16),
            pltpu.VMEM((packed_rows, size), BF16),
            pltpu.VMEM((NS - 1, wide, FB * size), BF16),
            pltpu.VMEM((3, wide, G2 * size), BF16),
            pltpu.VMEM((FB + 1, wide, size), BF16),
            pltpu.VMEM((NS * FB + 1, wide, size), F32),
            pltpu.VMEM((FB * size, wide), BF16),
            pltpu.VMEM((CB, CB, size, size), BF16),
            *[pltpu.SMEM(x.shape, jnp.int32) for x in integers],
            table,
            dma((8,)),
        ],
        compiler_params=WHOLE,
        cost_estimate=pl.CostEstimate(flops=10**9, bytes_accessed=4 * 10**6, transcendentals=0),
        name="own_source",
    )(
        *integers, fine_blocks[0, 0], packed,
    )

    near_scratch = [
        pltpu.VMEM((2, FB * size, wide), BF16),
        pltpu.VMEM((2, CB, CB, size, size), BF16),
        pltpu.VMEM((8, size), jnp.int32),
        pltpu.SMEM((8, size), jnp.int32),
        dma((3,)),
    ]
    square = jax.ShapeDtypeStruct((wide, G2 * size), F32)
    lift_t, half = pl.pallas_call(
        half_kernel,
        out_shape=[jax.ShapeDtypeStruct((G2 * size, wide), BF16), square],
        in_specs=[VMEM],
        out_specs=[VMEM] * 2,
        compiler_params=SMALL,
        cost_estimate=pl.CostEstimate(flops=10**9, bytes_accessed=4 * 10**6, transcendentals=0),
        name="own_half",
    )(more)
    c_one, term = pl.pallas_call(
        functools.partial(side_kernel, slots, size),
        out_shape=[c_shape, square],
        in_specs=[VMEM] * 5 + [HBM],
        out_specs=[HBM, VMEM],
        input_output_aliases={5: 0},
        scratch_shapes=near_scratch,
        compiler_params=LARGE,
        name="col_sources",
    )(col_stock, lift_t, half, right, left, c_one)

    chunk = G2 * size // cols_n
    kept = jax.ShapeDtypeStruct((3, chunk, G2 * size), F32)
    piece = jax.ShapeDtypeStruct(kept.shape, BF16)
    c_one, *sends = pl.pallas_call(
        functools.partial(row_kernel, slots, size, cols_n),
        out_shape=[c_shape, kept] + [piece] * (cols_n - 1),
        in_specs=[VMEM] * 5 + [HBM],
        out_specs=[HBM] + [VMEM] * cols_n,
        input_output_aliases={5: 0},
        scratch_shapes=[pltpu.VMEM((3, G2 * size, G2 * size), F32)] + near_scratch,
        compiler_params=LARGE,
        name="row_sources",
    )(row_stock, lift_t, term, other, pair, c_one)
    parts = [sends[0]] + [shift(sends[d], "col", d, True) for d in range(1, cols_n)]
    total = pl.pallas_call(
        sum_kernel, out_shape=piece, in_specs=[VMEM] * cols_n, out_specs=VMEM,
        compiler_params=SMALL, name="total",
    )(*parts)
    gathered = [total] + [shift(total, "col", d, True) for d in range(1, cols_n)]
    c_two = pl.pallas_call(
        functools.partial(spread_kernel, size, cols_n),
        out_shape=jax.ShapeDtypeStruct((G2, 3, G2, size, size), F32),
        in_specs=[VMEM] * cols_n,
        out_specs=HBM,
        scratch_shapes=[
            pltpu.VMEM((G2, 3, G2, size, size), F32),
            dma((G2 * size // math.gcd(chunk, size),)),
        ],
        compiler_params=SMALL,
        name="spread",
    )(*gathered)
    return (c_one[None, None], c_two[None])


def solution(mesh):
    in_specs = (
        P("row", "col", None, None, None),
        P("row", "col", None),
        P("row", "col", None),
        P("row", "col"),
        P("row", "col", None, None, None),
        P("row", "col", None),
        P("row", "col"),
        P("row", "col", None, None, None),
        P("row", "col", None),
    )
    out_specs = (
        P("row", "col", None, None, None, None, None),
        P("row", None, None, None, None, None),
    )
    return jax.shard_map(
        per_device, mesh=mesh, in_specs=in_specs, out_specs=out_specs, check_vma=False
    )
```

```python
import functools
import math

import jax
import jax.numpy as jnp
from jax import lax
from jax.experimental import pallas as pl
from jax.experimental.pallas import tpu as pltpu
from jax.sharding import PartitionSpec as P

FB = 8
CB = 2
G2 = 2
NS = 5
PB = FB * CB
UNROLL = 8
META = 16
F32 = jnp.float32
BF16 = jnp.bfloat16

VMEM = pl.BlockSpec(memory_space=pltpu.VMEM)
HBM = pl.BlockSpec(memory_space=pltpu.HBM)
SMALL = pltpu.CompilerParams(vmem_limit_bytes=4 * 1024 * 1024)
LARGE = pltpu.CompilerParams(vmem_limit_bytes=20 * 1024 * 1024)
WHOLE = pltpu.CompilerParams(vmem_limit_bytes=60 * 1024 * 1024)


def pack_kernel(
    codes_at, count_at, aggs_at, blocks, second, out, held, codes, count, aggs, table, sems
):
    n_p, n_s = blocks.shape[0], second.shape[0]
    slots, cut = codes_at.shape[-1], n_p // 2
    small = [
        pltpu.make_async_copy(a, b, sems.at[n])
        for n, (a, b) in enumerate([(codes_at, codes), (count_at, count), (aggs_at, aggs)])
    ]
    large = [
        pltpu.make_async_copy(blocks.at[0:cut], held.at[0:cut], sems.at[3]),
        pltpu.make_async_copy(blocks.at[cut:n_p], held.at[cut:n_p], sems.at[4]),
        pltpu.make_async_copy(second, held.at[n_p : n_p + n_s], sems.at[5]),
    ]
    for copy in small + large:
        copy.start()
    for copy in small:
        copy.wait()
    fill_table(0, slots, table, lambda k: jnp.where(k < count[0, 0], codes[0, 0, k], PB))
    lane = lax.broadcasted_iota(jnp.int32, (META, out.shape[1]), 1)
    word = jnp.zeros(lane.shape, jnp.int32)
    for q in range(PB):
        word = jnp.where(lane == q, table[0, q], word)
    for j in range(CB):
        word = jnp.where(lane == PB + j, aggs[0, 0, j], word)
    held[n_p + n_s : n_p + n_s + META, :] = word.astype(F32).astype(BF16)
    large[0].wait()
    stores = [pltpu.make_async_copy(held.at[0:cut], out.at[0:cut], sems.at[6])]
    stores[0].start()
    large[1].wait()
    large[2].wait()
    rest = pl.ds(cut, out.shape[0] - cut)
    stores.append(pltpu.make_async_copy(held.at[rest], out.at[rest], sems.at[7]))
    stores[1].start()
    for store in stores:
        store.wait()


def fill_table(s, slots, table, code_of):
    for q in range(PB + 1):
        table[s, q] = -1
    for k in range(slots):
        table[s, code_of(k)] = k


def block_at(s, q, size, table, near):
    slot = table[s, q]
    block = near[pl.ds(pl.multiple_of(jnp.maximum(slot, 0) * size, size), size), :]
    return jnp.where(slot >= 0, block, jnp.zeros_like(block))


def lift_of(near, slots, size, agg_of):
    lines = []
    for j in range(CB):
        block = near[(slots + j) * size : (slots + j + 1) * size, :]
        lines.append(
            jnp.concatenate(
                [jnp.where(agg_of(j) == a, block, jnp.zeros_like(block)) for a in range(G2)],
                axis=1,
            )
        )
    return jnp.concatenate(lines, axis=0)


def dense_of(s, size, table, near, dense):
    for i in range(FB):
        for j in range(CB):
            dense[i * size : (i + 1) * size, j * size : (j + 1) * size] = block_at(
                s, i * CB + j, size, table, near
            )


def coarse_of(size, weight, dense, tile):
    coarse = jnp.dot(weight, dense[...], preferred_element_type=F32).astype(BF16)
    for i in range(CB):
        for j in range(CB):
            tile[i, j] = coarse[i * size : (i + 1) * size, j * size : (j + 1) * size]
    return coarse


def other_sources():
    odd = lax.rem(lax.axis_index("row"), 2)
    return 2, 3 + odd, 1, 4 - odd


def own_kernel(
    slots, size, rows_at, cols_at, count_at, codes_at, p_count_at, aggs_at, fine_at, own_at,
    early_at, late_at, more_at, c_one,
    fine, own, stock, more, turned, acc, dense, tile, rows, cols, count, codes, p_count, aggs, table, sems,
):
    pairs = [
        (rows_at, rows), (cols_at, cols), (count_at, count), (codes_at, codes),
        (p_count_at, p_count), (aggs_at, aggs),
    ]
    small = [pltpu.make_async_copy(a, b, sems.at[2 + n]) for n, (a, b) in enumerate(pairs)]
    for copy in small:
        copy.start()
    fetch_own = pltpu.make_async_copy(own_at, own, sems.at[0])
    fetch_own.start()
    fetch_fine = pltpu.make_async_copy(fine_at, fine, sems.at[1])
    fetch_fine.start()
    acc[...] = jnp.zeros_like(acc)
    turned[...] = jnp.zeros_like(turned)
    for copy in small:
        copy.wait()
    code_of = lambda k: jnp.where(k < p_count[0, 0], codes[0, 0, k], PB)
    fill_table(0, slots, table, code_of)
    fetch_own.wait()
    for k in range(slots):
        i = code_of(k) // CB
        j = pl.multiple_of((code_of(k) - i * CB) * size, size)
        turned[i, pl.ds(j, size), :] = own[k * size : (k + 1) * size, :].T
    fetch_fine.wait()

    def step(t, carry):
        for u in range(UNROLL):
            k = t * UNROLL + u
            target = jnp.where(k < count[0, 0], cols[0, 0, k], NS * FB)
            acc[target] += jnp.dot(turned[rows[0, 0, k]], fine[k], preferred_element_type=F32)
        return carry

    lax.fori_loop(0, (count[0, 0] + UNROLL - 1) // UNROLL, step, 0)
    stores = []
    for n, s in enumerate(other_sources()):
        for m in range(FB):
            stock[n, :, m * size : (m + 1) * size] = acc[s * FB + m].astype(BF16)
        to = early_at.at[n] if n < 2 else late_at.at[n - 2]
        stores.append(pltpu.make_async_copy(stock.at[n], to, sems.at[2 + n]))
        stores[-1].start()
    own_weight = jnp.concatenate([acc[m].astype(BF16) for m in range(FB)], axis=1)
    dense_of(0, size, table, own, dense)
    coarse = coarse_of(size, own_weight, dense, tile)
    lift = lift_of(own, slots, size, lambda j: aggs[0, 0, j])
    wide = CB * size
    more[0] = lift.T
    more[1] = coarse
    more[2] = lift
    stores.append(pltpu.make_async_copy(more, more_at, sems.at[0]))
    stores[-1].start()
    stores.append(pltpu.make_async_copy(tile, c_one.at[:, 0], sems.at[1]))
    stores[-1].start()
    for store in stores:
        store.wait()


def near_coarse(
    sources, near, slots, size, stock, c_one, dense, tiles, words, codes, sems
):
    tail = (slots + CB) * size
    for n, ref in enumerate(near):
        word = ref[tail : tail + META, :].astype(F32).astype(jnp.int32)
        words[n : n + 1, :] = word[0:1, :]
    fetch = pltpu.make_async_copy(words, codes, sems.at[0])
    fetch.start()
    fetch.wait()
    parts, stores = [], []
    for n, (s, ref) in enumerate(zip(sources, near)):
        dense_of(n, size, codes, ref, dense.at[n])
        coarse = coarse_of(size, stock[n], dense.at[n], tiles.at[n])
        store = pltpu.make_async_copy(tiles.at[n], c_one.at[:, s], sems.at[1 + n])
        store.start()
        stores.append(store)
        lift = lift_of(ref, slots, size, lambda j: codes[n, PB + j])
        parts.append(jnp.dot(coarse, lift, preferred_element_type=F32))
    return parts, stores


def half_kernel(more, lift_t, half):
    lift_t[...] = more[0]
    half[...] = jnp.dot(more[1], more[2], preferred_element_type=F32)


def early_kernel(
    slots, size, stock, lift_t, half, right, other, c_in, c_one, part, term, *scratch
):
    sources = other_sources()[:2]
    parts, stores = near_coarse(sources, (right, other), slots, size, stock, c_one, *scratch)
    part[...] = half[...] + parts[0]
    term[...] = jnp.dot(lift_t[...], parts[1].astype(BF16), preferred_element_type=F32)
    for store in stores:
        store.wait()


def late_kernel(slots, size, cols_n, stock, lift_t, part, term, left, pair, c_in, c_one, *rest):
    sends, terms, scratch = rest[:cols_n], rest[cols_n], rest[cols_n + 1 :]
    sources = other_sources()
    terms[sources[1] - 2] = term[...]
    parts, stores = near_coarse(sources[2:], (left, pair), slots, size, stock, c_one, *scratch)
    for g, half in ((0, part[...] + parts[0]), (sources[3] - 2, parts[1])):
        terms[g] = jnp.dot(lift_t[...], half.astype(BF16), preferred_element_type=F32)
    chunk = terms.shape[1] // cols_n
    me = lax.axis_index("col")
    for d in range(cols_n):
        to = pl.multiple_of(lax.rem(me + d, cols_n) * chunk, chunk)
        sends[d][...] = terms[:, pl.ds(to, chunk), :].astype(sends[d].dtype)
    for store in stores:
        store.wait()


def sum_kernel(*refs):
    total = refs[0][...]
    for ref in refs[1:-1]:
        total = total + ref[...].astype(F32)
    refs[-1][...] = total.astype(BF16)


def spread_kernel(size, cols_n, *refs):
    parts, out_at, out, sems = refs[:cols_n], refs[cols_n], refs[cols_n + 1], refs[cols_n + 2]
    chunk = parts[0].shape[1]
    unit = math.gcd(chunk, size)
    per = size // unit
    me = lax.axis_index("col")
    stores = []
    for d in range(cols_n):
        owner = lax.rem(me - d + cols_n, cols_n)
        for t in range(chunk // unit):
            at = owner * (chunk // unit) + t
            a = at // per
            rows = pl.ds(pl.multiple_of(lax.rem(at, per) * unit, unit), unit)
            for g in range(3):
                for b in range(G2):
                    out[a, g, b, rows, :] = parts[d][
                        g, t * unit : (t + 1) * unit, b * size : (b + 1) * size
                    ].astype(F32)
            spot = (a, slice(None), slice(None), rows)
            stores.append(pltpu.make_async_copy(out.at[spot], out_at.at[spot], sems.at[len(stores)]))
            stores[-1].start()
    for store in stores:
        store.wait()


def shift(x, axis, step, wrap):
    n = lax.axis_size(axis)
    pairs = [(i, (i + step) % n) for i in range(n) if wrap or 0 <= i + step < n]
    return lax.ppermute(x, axis, pairs)


def swap(x, axis, pairs):
    return lax.ppermute(x, axis, pairs + [(j, i) for i, j in pairs])


def per_device(
    fine_blocks, fine_rows, fine_cols, fine_counts, prolong_blocks, prolong_codes,
    prolong_counts, second_blocks, second_aggs,
):
    slots, size = prolong_blocks.shape[2], prolong_blocks.shape[3]
    cap = fine_blocks.shape[2]
    cols_n = lax.axis_size("col")
    packed_rows = (slots + CB) * size + META
    wide = CB * size
    dma = pltpu.SemaphoreType.DMA
    packed = pl.pallas_call(
        pack_kernel,
        out_shape=jax.ShapeDtypeStruct((packed_rows, size), BF16),
        in_specs=[HBM] * 5,
        out_specs=HBM,
        scratch_shapes=[
            pltpu.VMEM((packed_rows, size), BF16),
            pltpu.SMEM(prolong_codes.shape, jnp.int32),
            pltpu.SMEM(prolong_counts.shape, jnp.int32),
            pltpu.SMEM(second_aggs.shape, jnp.int32),
            pltpu.SMEM((1, PB + 1), jnp.int32),
            dma((8,)),
        ],
        compiler_params=WHOLE,
        name="pack",
    )(
        prolong_codes, prolong_counts, second_aggs,
        prolong_blocks.reshape(slots * size, size),
        second_blocks.reshape(CB * size, size),
    )
    rows_n = lax.axis_size("row")
    pair = swap(packed, "row", [(i, i + 1) for i in range(0, rows_n - 1, 2)])
    other = swap(packed, "row", [(i, i + 1) for i in range(1, rows_n - 1, 2)])
    right = shift(packed, "col", -1, False)
    left = shift(packed, "col", 1, False)

    c_shape = jax.ShapeDtypeStruct((CB, NS, CB, size, size), BF16)
    table = pltpu.SMEM((1, PB + 1), jnp.int32)
    integers = (
        fine_rows, fine_cols, fine_counts, prolong_codes, prolong_counts, second_aggs
    )
    early_stock, late_stock, more, c_one = pl.pallas_call(
        functools.partial(own_kernel, slots, size),
        out_shape=[
            jax.ShapeDtypeStruct((2, wide, FB * size), BF16),
            jax.ShapeDtypeStruct((2, wide, FB * size), BF16),
            jax.ShapeDtypeStruct((3, wide, G2 * size), BF16),
            c_shape,
        ],
        in_specs=[HBM] * 8,
        out_specs=[HBM] * 4,
        scratch_shapes=[
            pltpu.VMEM((cap, size, size), BF16),
            pltpu.VMEM((packed_rows, size), BF16),
            pltpu.VMEM((NS - 1, wide, FB * size), BF16),
            pltpu.VMEM((3, wide, G2 * size), BF16),
            pltpu.VMEM((FB + 1, wide, size), BF16),
            pltpu.VMEM((NS * FB + 1, wide, size), F32),
            pltpu.VMEM((FB * size, wide), BF16),
            pltpu.VMEM((CB, CB, size, size), BF16),
            *[pltpu.SMEM(x.shape, jnp.int32) for x in integers],
            table,
            dma((8,)),
        ],
        compiler_params=WHOLE,
        cost_estimate=pl.CostEstimate(flops=10**9, bytes_accessed=4 * 10**6, transcendentals=0),
        name="own_source",
    )(
        *integers, fine_blocks[0, 0], packed,
    )

    near_scratch = [
        pltpu.VMEM((2, FB * size, wide), BF16),
        pltpu.VMEM((2, CB, CB, size, size), BF16),
        pltpu.VMEM((8, size), jnp.int32),
        pltpu.SMEM((8, size), jnp.int32),
        dma((3,)),
    ]
    square = jax.ShapeDtypeStruct((wide, G2 * size), F32)
    lift_t, half = pl.pallas_call(
        half_kernel,
        out_shape=[jax.ShapeDtypeStruct((G2 * size, wide), BF16), square],
        in_specs=[VMEM],
        out_specs=[VMEM] * 2,
        compiler_params=SMALL,
        cost_estimate=pl.CostEstimate(flops=10**9, bytes_accessed=4 * 10**6, transcendentals=0),
        name="own_half",
    )(more)
    c_one, part, term = pl.pallas_call(
        functools.partial(early_kernel, slots, size),
        out_shape=[c_shape, square, square],
        in_specs=[VMEM] * 5 + [HBM],
        out_specs=[HBM, VMEM, VMEM],
        input_output_aliases={5: 0},
        scratch_shapes=near_scratch,
        compiler_params=LARGE,
        name="early_sources",
    )(early_stock, lift_t, half, right, other, c_one)

    chunk = G2 * size // cols_n
    kept = jax.ShapeDtypeStruct((3, chunk, G2 * size), F32)
    piece = jax.ShapeDtypeStruct(kept.shape, BF16)
    c_one, *sends = pl.pallas_call(
        functools.partial(late_kernel, slots, size, cols_n),
        out_shape=[c_shape, kept] + [piece] * (cols_n - 1),
        in_specs=[VMEM] * 6 + [HBM],
        out_specs=[HBM] + [VMEM] * cols_n,
        input_output_aliases={6: 0},
        scratch_shapes=[pltpu.VMEM((3, G2 * size, G2 * size), F32)] + near_scratch,
        compiler_params=LARGE,
        name="late_sources",
    )(late_stock, lift_t, part, term, left, pair, c_one)
    parts = [sends[0]] + [shift(sends[d], "col", d, True) for d in range(1, cols_n)]
    total = pl.pallas_call(
        sum_kernel, out_shape=piece, in_specs=[VMEM] * cols_n, out_specs=VMEM,
        compiler_params=SMALL, name="total",
    )(*parts)
    gathered = [total] + [shift(total, "col", d, True) for d in range(1, cols_n)]
    c_two = pl.pallas_call(
        functools.partial(spread_kernel, size, cols_n),
        out_shape=jax.ShapeDtypeStruct((G2, 3, G2, size, size), F32),
        in_specs=[VMEM] * cols_n,
        out_specs=HBM,
        scratch_shapes=[
            pltpu.VMEM((G2, 3, G2, size, size), F32),
            dma((G2 * size // math.gcd(chunk, size),)),
        ],
        compiler_params=SMALL,
        name="spread",
    )(*gathered)
    return (c_one[None, None], c_two[None])


def solution(mesh):
    in_specs = (
        P("row", "col", None, None, None),
        P("row", "col", None),
        P("row", "col", None),
        P("row", "col"),
        P("row", "col", None, None, None),
        P("row", "col", None),
        P("row", "col"),
        P("row", "col", None, None, None),
        P("row", "col", None),
    )
    out_specs = (
        P("row", "col", None, None, None, None, None),
        P("row", None, None, None, None, None),
    )
    return jax.shard_map(
        per_device, mesh=mesh, in_specs=in_specs, out_specs=out_specs, check_vma=False
    )
```

```python
import functools
import math

import jax
import jax.numpy as jnp
from jax import lax
from jax.experimental import pallas as pl
from jax.experimental.pallas import tpu as pltpu
from jax.sharding import PartitionSpec as P

FB = 8
CB = 2
G2 = 2
NS = 5
PB = FB * CB
UNROLL = 8
META = 16
F32 = jnp.float32
BF16 = jnp.bfloat16

VMEM = pl.BlockSpec(memory_space=pltpu.VMEM)
HBM = pl.BlockSpec(memory_space=pltpu.HBM)
SMALL = pltpu.CompilerParams(vmem_limit_bytes=4 * 1024 * 1024)
LARGE = pltpu.CompilerParams(vmem_limit_bytes=20 * 1024 * 1024)
WHOLE = pltpu.CompilerParams(vmem_limit_bytes=60 * 1024 * 1024)


def pack_kernel(
    codes_at, count_at, aggs_at, blocks, second, out, held, codes, count, aggs, table, sems
):
    n_p, n_s = blocks.shape[0], second.shape[0]
    slots, cut = codes_at.shape[-1], n_p // 2
    small = [
        pltpu.make_async_copy(a, b, sems.at[n])
        for n, (a, b) in enumerate([(codes_at, codes), (count_at, count), (aggs_at, aggs)])
    ]
    large = [
        pltpu.make_async_copy(blocks.at[0:cut], held.at[0:cut], sems.at[3]),
        pltpu.make_async_copy(blocks.at[cut:n_p], held.at[cut:n_p], sems.at[4]),
        pltpu.make_async_copy(second, held.at[n_p : n_p + n_s], sems.at[5]),
    ]
    for copy in small + large:
        copy.start()
    for copy in small:
        copy.wait()
    fill_table(0, slots, table, lambda k: jnp.where(k < count[0, 0], codes[0, 0, k], PB))
    lane = lax.broadcasted_iota(jnp.int32, (META, out.shape[1]), 1)
    word = jnp.zeros(lane.shape, jnp.int32)
    for q in range(PB):
        word = jnp.where(lane == q, table[0, q], word)
    for j in range(CB):
        word = jnp.where(lane == PB + j, aggs[0, 0, j], word)
    held[n_p + n_s : n_p + n_s + META, :] = word.astype(F32).astype(BF16)
    large[0].wait()
    stores = [pltpu.make_async_copy(held.at[0:cut], out.at[0:cut], sems.at[6])]
    stores[0].start()
    large[1].wait()
    large[2].wait()
    rest = pl.ds(cut, out.shape[0] - cut)
    stores.append(pltpu.make_async_copy(held.at[rest], out.at[rest], sems.at[7]))
    stores[1].start()
    for store in stores:
        store.wait()


def fill_table(s, slots, table, code_of):
    for q in range(PB + 1):
        table[s, q] = -1
    for k in range(slots):
        table[s, code_of(k)] = k


def block_at(s, q, size, table, near):
    slot = table[s, q]
    block = near[pl.ds(pl.multiple_of(jnp.maximum(slot, 0) * size, size), size), :]
    return jnp.where(slot >= 0, block, jnp.zeros_like(block))


def lift_of(near, slots, size, agg_of):
    lines = []
    for j in range(CB):
        block = near[(slots + j) * size : (slots + j + 1) * size, :]
        lines.append(
            jnp.concatenate(
                [jnp.where(agg_of(j) == a, block, jnp.zeros_like(block)) for a in range(G2)],
                axis=1,
            )
        )
    return jnp.concatenate(lines, axis=0)


def dense_of(s, size, table, near, dense):
    for i in range(FB):
        for j in range(CB):
            dense[i * size : (i + 1) * size, j * size : (j + 1) * size] = block_at(
                s, i * CB + j, size, table, near
            )


def coarse_of(size, weight, dense, tile):
    coarse = jnp.dot(weight, dense[...], preferred_element_type=F32).astype(BF16)
    for i in range(CB):
        for j in range(CB):
            tile[i, j] = coarse[i * size : (i + 1) * size, j * size : (j + 1) * size]
    return coarse


def own_kernel(
    slots, size, rows_at, cols_at, count_at, codes_at, p_count_at, aggs_at, fine_at, own_at,
    col_at, row_at, more_at, c_one,
    fine, own, stock, more, turned, acc, dense, tile, rows, cols, count, codes, p_count, aggs, table, sems,
):
    pairs = [
        (rows_at, rows), (cols_at, cols), (count_at, count), (codes_at, codes),
        (p_count_at, p_count), (aggs_at, aggs),
    ]
    small = [pltpu.make_async_copy(a, b, sems.at[2 + n]) for n, (a, b) in enumerate(pairs)]
    for copy in small:
        copy.start()
    fetch_own = pltpu.make_async_copy(own_at, own, sems.at[0])
    fetch_own.start()
    fetch_fine = pltpu.make_async_copy(fine_at, fine, sems.at[1])
    fetch_fine.start()
    acc[...] = jnp.zeros_like(acc)
    turned[...] = jnp.zeros_like(turned)
    for copy in small:
        copy.wait()
    code_of = lambda k: jnp.where(k < p_count[0, 0], codes[0, 0, k], PB)
    fill_table(0, slots, table, code_of)
    fetch_own.wait()
    for k in range(slots):
        i = code_of(k) // CB
        j = pl.multiple_of((code_of(k) - i * CB) * size, size)
        turned[i, pl.ds(j, size), :] = own[k * size : (k + 1) * size, :].T
    fetch_fine.wait()

    def step(t, carry):
        products, targets = [], []
        for u in range(UNROLL):
            k = t * UNROLL + u
            products.append(jnp.dot(turned[rows[0, 0, k]], fine[k], preferred_element_type=F32))
            targets.append(jnp.where(k < count[0, 0], cols[0, 0, k], NS * FB))
        for u in range(UNROLL):
            acc[targets[u]] += products[u]
        return carry

    lax.fori_loop(0, (count[0, 0] + UNROLL - 1) // UNROLL, step, 0)
    stores = []
    for s in range(1, NS):
        for m in range(FB):
            stock[s - 1, :, m * size : (m + 1) * size] = acc[s * FB + m].astype(BF16)
        stock_at, n = (col_at, s - 1) if s < 3 else (row_at, s - 3)
        stores.append(pltpu.make_async_copy(stock.at[s - 1], stock_at.at[n], sems.at[1 + s]))
        stores[-1].start()
    own_weight = jnp.concatenate([acc[m].astype(BF16) for m in range(FB)], axis=1)
    dense_of(0, size, table, own, dense)
    coarse = coarse_of(size, own_weight, dense, tile)
    lift = lift_of(own, slots, size, lambda j: aggs[0, 0, j])
    wide = CB * size
    more[0] = lift.T
    more[1] = coarse
    more[2] = lift
    stores.append(pltpu.make_async_copy(more, more_at, sems.at[0]))
    stores[-1].start()
    stores.append(pltpu.make_async_copy(tile, c_one.at[:, 0], sems.at[1]))
    stores[-1].start()
    for store in stores:
        store.wait()


def near_coarse(
    base, sources, near, slots, size, stock, c_one, dense, tiles, words, codes, sems
):
    tail = (slots + CB) * size
    for n, ref in enumerate(near):
        word = ref[tail : tail + META, :].astype(F32).astype(jnp.int32)
        words[n : n + 1, :] = word[0:1, :]
    fetch = pltpu.make_async_copy(words, codes, sems.at[0])
    fetch.start()
    fetch.wait()
    parts, stores = [], []
    for n, (s, ref) in enumerate(zip(sources, near)):
        dense_of(n, size, codes, ref, dense.at[n])
        coarse = coarse_of(size, stock[s - base], dense.at[n], tiles.at[n])
        store = pltpu.make_async_copy(tiles.at[n], c_one.at[:, s], sems.at[1 + n])
        store.start()
        stores.append(store)
        lift = lift_of(ref, slots, size, lambda j: codes[n, PB + j])
        parts.append(jnp.dot(coarse, lift, preferred_element_type=F32))
    return parts, stores


def half_kernel(more, lift_t, half):
    lift_t[...] = more[0]
    half[...] = jnp.dot(more[1], more[2], preferred_element_type=F32)


def side_kernel(slots, size, stock, lift_t, half, right, left, c_in, c_one, term, *scratch):
    parts, stores = near_coarse(1, (2, 1), (right, left), slots, size, stock, c_one, *scratch)
    whole = (half[...] + parts[0] + parts[1]).astype(BF16)
    term[...] = jnp.dot(lift_t[...], whole, preferred_element_type=F32)
    for store in stores:
        store.wait()


def row_kernel(slots, size, cols_n, stock, lift_t, term, other, pair, c_in, c_one, *rest):
    sends, terms, scratch = rest[:cols_n], rest[cols_n], rest[cols_n + 1 :]
    odd = lax.rem(lax.axis_index("row"), 2)
    sources = (3 + odd, 4 - odd)
    parts, stores = near_coarse(3, sources, (other, pair), slots, size, stock, c_one, *scratch)
    terms[0] = term[...]
    for n in range(2):
        terms[sources[n] - 2] = jnp.dot(lift_t[...], parts[n].astype(BF16), preferred_element_type=F32)
    chunk = terms.shape[1] // cols_n
    me = lax.axis_index("col")
    for d in range(cols_n):
        to = pl.multiple_of(lax.rem(me + d, cols_n) * chunk, chunk)
        sends[d][...] = terms[:, pl.ds(to, chunk), :].astype(sends[d].dtype)
    for store in stores:
        store.wait()


def sum_kernel(*refs):
    total = refs[0][...]
    for ref in refs[1:-1]:
        total = total + ref[...].astype(F32)
    refs[-1][...] = total.astype(BF16)


def spread_kernel(size, cols_n, steps, *refs):
    parts, (out_at, out, sems) = refs[: len(steps)], refs[-3:]
    chunk = parts[0].shape[1]
    unit = math.gcd(chunk, size)
    per = size // unit
    me = lax.axis_index("col")
    stores = []
    for n, d in enumerate(steps):
        owner = lax.rem(me - d + cols_n, cols_n)
        for t in range(chunk // unit):
            at = owner * (chunk // unit) + t
            a = at // per
            rows = pl.ds(pl.multiple_of(lax.rem(at, per) * unit, unit), unit)
            for g in range(3):
                for b in range(G2):
                    out[a, g, b, rows, :] = parts[n][
                        g, t * unit : (t + 1) * unit, b * size : (b + 1) * size
                    ].astype(F32)
            spot = (a, slice(None), slice(None), rows)
            stores.append(pltpu.make_async_copy(out.at[spot], out_at.at[spot], sems.at[len(stores)]))
            stores[-1].start()
    for store in stores:
        store.wait()


def shift(x, axis, step, wrap):
    n = lax.axis_size(axis)
    pairs = [(i, (i + step) % n) for i in range(n) if wrap or 0 <= i + step < n]
    return lax.ppermute(x, axis, pairs)


def swap(x, axis, pairs):
    return lax.ppermute(x, axis, pairs + [(j, i) for i, j in pairs])


def per_device(
    fine_blocks, fine_rows, fine_cols, fine_counts, prolong_blocks, prolong_codes,
    prolong_counts, second_blocks, second_aggs,
):
    slots, size = prolong_blocks.shape[2], prolong_blocks.shape[3]
    cap = fine_blocks.shape[2]
    cols_n = lax.axis_size("col")
    packed_rows = (slots + CB) * size + META
    wide = CB * size
    dma = pltpu.SemaphoreType.DMA
    packed = pl.pallas_call(
        pack_kernel,
        out_shape=jax.ShapeDtypeStruct((packed_rows, size), BF16),
        in_specs=[HBM] * 5,
        out_specs=HBM,
        scratch_shapes=[
            pltpu.VMEM((packed_rows, size), BF16),
            pltpu.SMEM(prolong_codes.shape, jnp.int32),
            pltpu.SMEM(prolong_counts.shape, jnp.int32),
            pltpu.SMEM(second_aggs.shape, jnp.int32),
            pltpu.SMEM((1, PB + 1), jnp.int32),
            dma((8,)),
        ],
        compiler_params=WHOLE,
        name="pack",
    )(
        prolong_codes, prolong_counts, second_aggs,
        prolong_blocks.reshape(slots * size, size),
        second_blocks.reshape(CB * size, size),
    )
    rows_n = lax.axis_size("row")
    pair = swap(packed, "row", [(i, i + 1) for i in range(0, rows_n - 1, 2)])
    other = swap(packed, "row", [(i, i + 1) for i in range(1, rows_n - 1, 2)])
    right = shift(packed, "col", -1, False)
    left = shift(packed, "col", 1, False)

    c_shape = jax.ShapeDtypeStruct((CB, NS, CB, size, size), BF16)
    table = pltpu.SMEM((1, PB + 1), jnp.int32)
    integers = (
        fine_rows, fine_cols, fine_counts, prolong_codes, prolong_counts, second_aggs
    )
    col_stock, row_stock, more, c_one = pl.pallas_call(
        functools.partial(own_kernel, slots, size),
        out_shape=[
            jax.ShapeDtypeStruct((2, wide, FB * size), BF16),
            jax.ShapeDtypeStruct((2, wide, FB * size), BF16),
            jax.ShapeDtypeStruct((3, wide, G2 * size), BF16),
            c_shape,
        ],
        in_specs=[HBM] * 8,
        out_specs=[HBM] * 4,
        scratch_shapes=[
            pltpu.VMEM((cap, size, size), BF16),
            pltpu.VMEM((packed_rows, size), BF16),
            pltpu.VMEM((NS - 1, wide, FB * size), BF16),
            pltpu.VMEM((3, wide, G2 * size), BF16),
            pltpu.VMEM((FB + 1, wide, size), BF16),
            pltpu.VMEM((NS * FB + 1, wide, size), F32),
            pltpu.VMEM((FB * size, wide), BF16),
            pltpu.VMEM((CB, CB, size, size), BF16),
            *[pltpu.SMEM(x.shape, jnp.int32) for x in integers],
            table,
            dma((8,)),
        ],
        compiler_params=WHOLE,
        cost_estimate=pl.CostEstimate(flops=10**9, bytes_accessed=4 * 10**6, transcendentals=0),
        name="own_source",
    )(
        *integers, fine_blocks[0, 0], packed,
    )

    near_scratch = [
        pltpu.VMEM((2, FB * size, wide), BF16),
        pltpu.VMEM((2, CB, CB, size, size), BF16),
        pltpu.VMEM((8, size), jnp.int32),
        pltpu.SMEM((8, size), jnp.int32),
        dma((3,)),
    ]
    square = jax.ShapeDtypeStruct((wide, G2 * size), F32)
    lift_t, half = pl.pallas_call(
        half_kernel,
        out_shape=[jax.ShapeDtypeStruct((G2 * size, wide), BF16), square],
        in_specs=[VMEM],
        out_specs=[VMEM] * 2,
        compiler_params=SMALL,
        cost_estimate=pl.CostEstimate(flops=10**9, bytes_accessed=4 * 10**6, transcendentals=0),
        name="own_half",
    )(more)
    c_one, term = pl.pallas_call(
        functools.partial(side_kernel, slots, size),
        out_shape=[c_shape, square],
        in_specs=[VMEM] * 5 + [HBM],
        out_specs=[HBM, VMEM],
        input_output_aliases={5: 0},
        scratch_shapes=near_scratch,
        compiler_params=LARGE,
        name="col_sources",
    )(col_stock, lift_t, half, right, left, c_one)

    chunk = G2 * size // cols_n
    kept = jax.ShapeDtypeStruct((3, chunk, G2 * size), F32)
    piece = jax.ShapeDtypeStruct(kept.shape, BF16)
    c_one, *sends = pl.pallas_call(
        functools.partial(row_kernel, slots, size, cols_n),
        out_shape=[c_shape, kept] + [piece] * (cols_n - 1),
        in_specs=[VMEM] * 5 + [HBM],
        out_specs=[HBM] + [VMEM] * cols_n,
        input_output_aliases={5: 0},
        scratch_shapes=[pltpu.VMEM((3, G2 * size, G2 * size), F32)] + near_scratch,
        compiler_params=LARGE,
        name="row_sources",
    )(row_stock, lift_t, term, other, pair, c_one)
    parts = [sends[0]] + [shift(sends[d], "col", d, True) for d in range(1, cols_n)]
    total = pl.pallas_call(
        sum_kernel, out_shape=piece, in_specs=[VMEM] * cols_n, out_specs=VMEM,
        compiler_params=SMALL, name="total",
    )(*parts)
    gathered = [total] + [shift(total, "col", d, True) for d in range(1, cols_n)]
    c_two = None
    cut = max(1, cols_n - 1)
    for steps in (list(range(cut)), list(range(cut, cols_n))):
        if not steps:
            continue
        before = [] if c_two is None else [c_two]
        c_two = pl.pallas_call(
            functools.partial(spread_kernel, size, cols_n, steps),
            out_shape=jax.ShapeDtypeStruct((G2, 3, G2, size, size), F32),
            in_specs=[VMEM] * len(steps) + [HBM] * len(before),
            out_specs=HBM,
            input_output_aliases={len(steps): 0} if before else {},
            scratch_shapes=[
                pltpu.VMEM((G2, 3, G2, size, size), F32),
                dma((len(steps) * (chunk // math.gcd(chunk, size)),)),
            ],
            compiler_params=SMALL,
            name="spread",
        )(*[gathered[d] for d in steps], *before)
    return (c_one[None, None], c_two[None])


def solution(mesh):
    in_specs = (
        P("row", "col", None, None, None),
        P("row", "col", None),
        P("row", "col", None),
        P("row", "col"),
        P("row", "col", None, None, None),
        P("row", "col", None),
        P("row", "col"),
        P("row", "col", None, None, None),
        P("row", "col", None),
    )
    out_specs = (
        P("row", "col", None, None, None, None, None),
        P("row", None, None, None, None, None),
    )
    return jax.shard_map(
        per_device, mesh=mesh, in_specs=in_specs, out_specs=out_specs, check_vma=False
    )
```

```python
import functools
import math

import jax
import jax.numpy as jnp
from jax import lax
from jax.experimental import pallas as pl
from jax.experimental.pallas import tpu as pltpu
from jax.sharding import PartitionSpec as P

FB = 8
CB = 2
G2 = 2
NS = 5
PB = FB * CB
UNROLL = 8
META = 16
F32 = jnp.float32
BF16 = jnp.bfloat16

VMEM = pl.BlockSpec(memory_space=pltpu.VMEM)
HBM = pl.BlockSpec(memory_space=pltpu.HBM)
SMALL = pltpu.CompilerParams(vmem_limit_bytes=4 * 1024 * 1024)
LARGE = pltpu.CompilerParams(vmem_limit_bytes=20 * 1024 * 1024)
WHOLE = pltpu.CompilerParams(vmem_limit_bytes=60 * 1024 * 1024)


def pack_kernel(
    codes_at, count_at, aggs_at, blocks, second, out, held, codes, count, aggs, table, sems
):
    n_p, n_s = blocks.shape[0], second.shape[0]
    slots, cut = codes_at.shape[-1], n_p // 2
    small = [
        pltpu.make_async_copy(a, b, sems.at[n])
        for n, (a, b) in enumerate([(codes_at, codes), (count_at, count), (aggs_at, aggs)])
    ]
    large = [
        pltpu.make_async_copy(blocks.at[0:cut], held.at[0:cut], sems.at[3]),
        pltpu.make_async_copy(blocks.at[cut:n_p], held.at[cut:n_p], sems.at[4]),
        pltpu.make_async_copy(second, held.at[n_p : n_p + n_s], sems.at[5]),
    ]
    for copy in small + large:
        copy.start()
    for copy in small:
        copy.wait()
    fill_table(0, slots, table, lambda k: jnp.where(k < count[0, 0], codes[0, 0, k], PB))
    lane = lax.broadcasted_iota(jnp.int32, (META, out.shape[1]), 1)
    word = jnp.zeros(lane.shape, jnp.int32)
    for q in range(PB):
        word = jnp.where(lane == q, table[0, q], word)
    for j in range(CB):
        word = jnp.where(lane == PB + j, aggs[0, 0, j], word)
    held[n_p + n_s : n_p + n_s + META, :] = word.astype(F32).astype(BF16)
    large[0].wait()
    stores = [pltpu.make_async_copy(held.at[0:cut], out.at[0:cut], sems.at[6])]
    stores[0].start()
    large[1].wait()
    large[2].wait()
    rest = pl.ds(cut, out.shape[0] - cut)
    stores.append(pltpu.make_async_copy(held.at[rest], out.at[rest], sems.at[7]))
    stores[1].start()
    for store in stores:
        store.wait()


def fill_table(s, slots, table, code_of):
    for q in range(PB + 1):
        table[s, q] = -1
    for k in range(slots):
        table[s, code_of(k)] = k


def block_at(s, q, size, table, near):
    slot = table[s, q]
    block = near[pl.ds(pl.multiple_of(jnp.maximum(slot, 0) * size, size), size), :]
    return jnp.where(slot >= 0, block, jnp.zeros_like(block))


def lift_of(near, slots, size, agg_of):
    lines = []
    for j in range(CB):
        block = near[(slots + j) * size : (slots + j + 1) * size, :]
        lines.append(
            jnp.concatenate(
                [jnp.where(agg_of(j) == a, block, jnp.zeros_like(block)) for a in range(G2)],
                axis=1,
            )
        )
    return jnp.concatenate(lines, axis=0)


def dense_of(s, size, table, near, dense):
    for i in range(FB):
        for j in range(CB):
            dense[i * size : (i + 1) * size, j * size : (j + 1) * size] = block_at(
                s, i * CB + j, size, table, near
            )


def coarse_of(size, weight, dense, tile):
    coarse = jnp.dot(weight, dense[...], preferred_element_type=F32).astype(BF16)
    for i in range(CB):
        for j in range(CB):
            tile[i, j] = coarse[i * size : (i + 1) * size, j * size : (j + 1) * size]
    return coarse


def own_kernel(
    slots, size, rows_at, cols_at, count_at, codes_at, p_count_at, aggs_at, fine_at, own_at,
    col_at, row_at, more_at, c_one,
    fine, own, stock, more, turned, acc, dense, tile, rows, cols, count, codes, p_count, aggs, table, sems,
):
    pairs = [
        (rows_at, rows), (cols_at, cols), (count_at, count), (codes_at, codes),
        (p_count_at, p_count), (aggs_at, aggs),
    ]
    small = [pltpu.make_async_copy(a, b, sems.at[2 + n]) for n, (a, b) in enumerate(pairs)]
    for copy in small:
        copy.start()
    fetch_own = pltpu.make_async_copy(own_at, own, sems.at[0])
    fetch_own.start()
    fetch_fine = pltpu.make_async_copy(fine_at, fine, sems.at[1])
    fetch_fine.start()
    acc[...] = jnp.zeros_like(acc)
    turned[...] = jnp.zeros_like(turned)
    for copy in small:
        copy.wait()
    code_of = lambda k: jnp.where(k < p_count[0, 0], codes[0, 0, k], PB)
    fill_table(0, slots, table, code_of)
    fetch_own.wait()
    for k in range(slots):
        i = code_of(k) // CB
        j = pl.multiple_of((code_of(k) - i * CB) * size, size)
        turned[i, pl.ds(j, size), :] = own[k * size : (k + 1) * size, :].T
    fetch_fine.wait()

    def step(t, carry):
        products, targets = [], []
        for u in range(UNROLL):
            k = t * UNROLL + u
            products.append(jnp.dot(turned[rows[0, 0, k]], fine[k], preferred_element_type=F32))
            targets.append(jnp.where(k < count[0, 0], cols[0, 0, k], NS * FB))
        for u in range(UNROLL):
            acc[targets[u]] += products[u]
        return carry

    lax.fori_loop(0, (count[0, 0] + UNROLL - 1) // UNROLL, step, 0)
    stores = []
    for s in range(1, NS):
        for m in range(FB):
            stock[s - 1, :, m * size : (m + 1) * size] = acc[s * FB + m].astype(BF16)
        stock_at, n = (col_at, s - 1) if s < 3 else (row_at, s - 3)
        stores.append(pltpu.make_async_copy(stock.at[s - 1], stock_at.at[n], sems.at[1 + s]))
        stores[-1].start()
    own_weight = jnp.concatenate([acc[m].astype(BF16) for m in range(FB)], axis=1)
    dense_of(0, size, table, own, dense)
    coarse = coarse_of(size, own_weight, dense, tile)
    lift = lift_of(own, slots, size, lambda j: aggs[0, 0, j])
    wide = CB * size
    more[0] = lift.T
    more[1] = coarse
    more[2] = lift
    stores.append(pltpu.make_async_copy(more, more_at, sems.at[0]))
    stores[-1].start()
    stores.append(pltpu.make_async_copy(tile, c_one.at[:, 0], sems.at[1]))
    stores[-1].start()
    for store in stores:
        store.wait()


def near_coarse(
    base, sources, near, slots, size, stock, c_one, dense, tiles, words, codes, sems
):
    tail = (slots + CB) * size
    for n, ref in enumerate(near):
        word = ref[tail : tail + META, :].astype(F32).astype(jnp.int32)
        words[n : n + 1, :] = word[0:1, :]
    fetch = pltpu.make_async_copy(words, codes, sems.at[0])
    fetch.start()
    fetch.wait()
    parts, stores = [], []
    for n, (s, ref) in enumerate(zip(sources, near)):
        dense_of(n, size, codes, ref, dense.at[n])
        coarse = coarse_of(size, stock[s - base], dense.at[n], tiles.at[n])
        store = pltpu.make_async_copy(tiles.at[n], c_one.at[:, s], sems.at[1 + n])
        store.start()
        stores.append(store)
        lift = lift_of(ref, slots, size, lambda j: codes[n, PB + j])
        parts.append(jnp.dot(coarse, lift, preferred_element_type=F32))
    return parts, stores


def half_kernel(more, lift_t, half):
    lift_t[...] = more[0]
    half[...] = jnp.dot(more[1], more[2], preferred_element_type=F32)


def side_kernel(slots, size, stock, lift_t, half, right, left, c_in, c_one, term, *scratch):
    parts, stores = near_coarse(1, (2, 1), (right, left), slots, size, stock, c_one, *scratch)
    whole = (half[...] + parts[0] + parts[1]).astype(BF16)
    term[...] = jnp.dot(lift_t[...], whole, preferred_element_type=F32)
    for store in stores:
        store.wait()


def row_kernel(slots, size, cols_n, stock, lift_t, term, other, pair, c_in, c_one, *rest):
    sends, terms, scratch = rest[:cols_n], rest[cols_n], rest[cols_n + 1 :]
    odd = lax.rem(lax.axis_index("row"), 2)
    sources = (3 + odd, 4 - odd)
    parts, stores = near_coarse(3, sources, (other, pair), slots, size, stock, c_one, *scratch)
    terms[0] = term[...]
    for n in range(2):
        terms[sources[n] - 2] = jnp.dot(lift_t[...], parts[n].astype(BF16), preferred_element_type=F32)
    chunk = terms.shape[1] // cols_n
    me = lax.axis_index("col")
    for d in range(cols_n):
        to = pl.multiple_of(lax.rem(me + d, cols_n) * chunk, chunk)
        sends[d][...] = terms[:, pl.ds(to, chunk), :].astype(sends[d].dtype)
    for store in stores:
        store.wait()


def sum_kernel(*refs):
    total = refs[0][...]
    for ref in refs[1:-1]:
        total = total + ref[...].astype(F32)
    refs[-1][...] = total.astype(BF16)


def spread_kernel(size, cols_n, *refs):
    parts, out_at, out, sems = refs[:cols_n], refs[cols_n], refs[cols_n + 1], refs[cols_n + 2]
    chunk = parts[0].shape[1]
    unit = math.gcd(chunk, size)
    per = size // unit
    me = lax.axis_index("col")
    stores = []
    for d in range(cols_n):
        owner = lax.rem(me - d + cols_n, cols_n)
        for t in range(chunk // unit):
            at = owner * (chunk // unit) + t
            a = at // per
            rows = pl.ds(pl.multiple_of(lax.rem(at, per) * unit, unit), unit)
            for g in range(3):
                for b in range(G2):
                    out[a, g, b, rows, :] = parts[d][
                        g, t * unit : (t + 1) * unit, b * size : (b + 1) * size
                    ].astype(F32)
            spot = (a, slice(None), slice(None), rows)
            stores.append(pltpu.make_async_copy(out.at[spot], out_at.at[spot], sems.at[len(stores)]))
            stores[-1].start()
    for store in stores:
        store.wait()


def shift(x, axis, step, wrap):
    n = lax.axis_size(axis)
    pairs = [(i, (i + step) % n) for i in range(n) if wrap or 0 <= i + step < n]
    return lax.ppermute(x, axis, pairs)


def swap(x, axis, pairs):
    return lax.ppermute(x, axis, pairs + [(j, i) for i, j in pairs])


def per_device(
    fine_blocks, fine_rows, fine_cols, fine_counts, prolong_blocks, prolong_codes,
    prolong_counts, second_blocks, second_aggs,
):
    slots, size = prolong_blocks.shape[2], prolong_blocks.shape[3]
    cap = fine_blocks.shape[2]
    cols_n = lax.axis_size("col")
    packed_rows = (slots + CB) * size + META
    wide = CB * size
    dma = pltpu.SemaphoreType.DMA
    packed = pl.pallas_call(
        pack_kernel,
        out_shape=jax.ShapeDtypeStruct((packed_rows, size), BF16),
        in_specs=[HBM] * 5,
        out_specs=HBM,
        scratch_shapes=[
            pltpu.VMEM((packed_rows, size), BF16),
            pltpu.SMEM(prolong_codes.shape, jnp.int32),
            pltpu.SMEM(prolong_counts.shape, jnp.int32),
            pltpu.SMEM(second_aggs.shape, jnp.int32),
            pltpu.SMEM((1, PB + 1), jnp.int32),
            dma((8,)),
        ],
        compiler_params=WHOLE,
        name="pack",
    )(
        prolong_codes, prolong_counts, second_aggs,
        prolong_blocks.reshape(slots * size, size),
        second_blocks.reshape(CB * size, size),
    )
    rows_n = lax.axis_size("row")
    pair = swap(packed, "row", [(i, i + 1) for i in range(0, rows_n - 1, 2)])
    other = swap(packed, "row", [(i, i + 1) for i in range(1, rows_n - 1, 2)])
    right = shift(packed, "col", -1, False)
    left = shift(packed, "col", 1, False)

    c_shape = jax.ShapeDtypeStruct((CB, NS, CB, size, size), BF16)
    table = pltpu.SMEM((1, PB + 1), jnp.int32)
    integers = (
        fine_rows, fine_cols, fine_counts, prolong_codes, prolong_counts, second_aggs
    )
    col_stock, row_stock, more, c_one = pl.pallas_call(
        functools.partial(own_kernel, slots, size),
        out_shape=[
            jax.ShapeDtypeStruct((2, wide, FB * size), BF16),
            jax.ShapeDtypeStruct((2, wide, FB * size), BF16),
            jax.ShapeDtypeStruct((3, wide, G2 * size), BF16),
            c_shape,
        ],
        in_specs=[HBM] * 8,
        out_specs=[HBM] * 4,
        scratch_shapes=[
            pltpu.VMEM((cap, size, size), BF16),
            pltpu.VMEM((packed_rows, size), BF16),
            pltpu.VMEM((NS - 1, wide, FB * size), BF16),
            pltpu.VMEM((3, wide, G2 * size), BF16),
            pltpu.VMEM((FB + 1, wide, size), BF16),
            pltpu.VMEM((NS * FB + 1, wide, size), F32),
            pltpu.VMEM((FB * size, wide), BF16),
            pltpu.VMEM((CB, CB, size, size), BF16),
            *[pltpu.SMEM(x.shape, jnp.int32) for x in integers],
            table,
            dma((8,)),
        ],
        compiler_params=WHOLE,
        cost_estimate=pl.CostEstimate(flops=10**9, bytes_accessed=4 * 10**6, transcendentals=0),
        name="own_source",
    )(
        *integers, fine_blocks[0, 0], packed,
    )

    near_scratch = [
        pltpu.VMEM((2, FB * size, wide), BF16),
        pltpu.VMEM((2, CB, CB, size, size), BF16),
        pltpu.VMEM((8, size), jnp.int32),
        pltpu.SMEM((8, size), jnp.int32),
        dma((3,)),
    ]
    square = jax.ShapeDtypeStruct((wide, G2 * size), F32)
    lift_t, half = pl.pallas_call(
        half_kernel,
        out_shape=[jax.ShapeDtypeStruct((G2 * size, wide), BF16), square],
        in_specs=[VMEM],
        out_specs=[VMEM] * 2,
        compiler_params=SMALL,
        cost_estimate=pl.CostEstimate(flops=10**9, bytes_accessed=4 * 10**6, transcendentals=0),
        name="own_half",
    )(more)
    c_one, term = pl.pallas_call(
        functools.partial(side_kernel, slots, size),
        out_shape=[c_shape, square],
        in_specs=[VMEM] * 5 + [HBM],
        out_specs=[HBM, VMEM],
        input_output_aliases={5: 0},
        scratch_shapes=near_scratch,
        compiler_params=LARGE,
        name="col_sources",
    )(col_stock, lift_t, half, right, left, c_one)

    chunk = G2 * size // cols_n
    kept = jax.ShapeDtypeStruct((3, chunk, G2 * size), F32)
    piece = jax.ShapeDtypeStruct(kept.shape, BF16)
    c_one, *sends = pl.pallas_call(
        functools.partial(row_kernel, slots, size, cols_n),
        out_shape=[c_shape, kept] + [piece] * (cols_n - 1),
        in_specs=[VMEM] * 5 + [HBM],
        out_specs=[HBM] + [VMEM] * cols_n,
        input_output_aliases={5: 0},
        scratch_shapes=[pltpu.VMEM((3, G2 * size, G2 * size), F32)] + near_scratch,
        compiler_params=LARGE,
        name="row_sources",
    )(row_stock, lift_t, term, other, pair, c_one)
    farthest = sorted(range(1, cols_n), key=lambda d: -min(d, cols_n - d))
    parts = [sends[0]] + [shift(sends[d], "col", d, True) for d in farthest]
    total = pl.pallas_call(
        sum_kernel, out_shape=piece, in_specs=[VMEM] * cols_n, out_specs=VMEM,
        compiler_params=SMALL, name="total",
    )(*parts)
    gathered = [total] + [shift(total, "col", d, True) for d in range(1, cols_n)]
    c_two = pl.pallas_call(
        functools.partial(spread_kernel, size, cols_n),
        out_shape=jax.ShapeDtypeStruct((G2, 3, G2, size, size), F32),
        in_specs=[VMEM] * cols_n,
        out_specs=HBM,
        scratch_shapes=[
            pltpu.VMEM((G2, 3, G2, size, size), F32),
            dma((G2 * size // math.gcd(chunk, size),)),
        ],
        compiler_params=SMALL,
        name="spread",
    )(*gathered)
    return (c_one[None, None], c_two[None])


def solution(mesh):
    in_specs = (
        P("row", "col", None, None, None),
        P("row", "col", None),
        P("row", "col", None),
        P("row", "col"),
        P("row", "col", None, None, None),
        P("row", "col", None),
        P("row", "col"),
        P("row", "col", None, None, None),
        P("row", "col", None),
    )
    out_specs = (
        P("row", "col", None, None, None, None, None),
        P("row", None, None, None, None, None),
    )
    return jax.shard_map(
        per_device, mesh=mesh, in_specs=in_specs, out_specs=out_specs, check_vma=False
    )
```

```python
import functools
import math

import jax
import jax.numpy as jnp
from jax import lax
from jax.experimental import pallas as pl
from jax.experimental.pallas import tpu as pltpu
from jax.sharding import PartitionSpec as P

FB = 8
CB = 2
G2 = 2
NS = 5
PB = FB * CB
UNROLL = 8
META = 16
F32 = jnp.float32
BF16 = jnp.bfloat16

VMEM = pl.BlockSpec(memory_space=pltpu.VMEM)
HBM = pl.BlockSpec(memory_space=pltpu.HBM)
SMALL = pltpu.CompilerParams(vmem_limit_bytes=4 * 1024 * 1024)
LARGE = pltpu.CompilerParams(vmem_limit_bytes=20 * 1024 * 1024)
WHOLE = pltpu.CompilerParams(vmem_limit_bytes=60 * 1024 * 1024)


def pack_kernel(
    codes_at, count_at, aggs_at, blocks, second, out, held, codes, count, aggs, table, sems
):
    n_p, n_s = blocks.shape[0], second.shape[0]
    slots, cut = codes_at.shape[-1], n_p // 2
    small = [
        pltpu.make_async_copy(a, b, sems.at[n])
        for n, (a, b) in enumerate([(codes_at, codes), (count_at, count), (aggs_at, aggs)])
    ]
    large = [
        pltpu.make_async_copy(blocks.at[0:cut], held.at[0:cut], sems.at[3]),
        pltpu.make_async_copy(blocks.at[cut:n_p], held.at[cut:n_p], sems.at[4]),
        pltpu.make_async_copy(second, held.at[n_p : n_p + n_s], sems.at[5]),
    ]
    for copy in small + large:
        copy.start()
    for copy in small:
        copy.wait()
    fill_table(0, slots, table, lambda k: jnp.where(k < count[0, 0], codes[0, 0, k], PB))
    lane = lax.broadcasted_iota(jnp.int32, (META, out.shape[1]), 1)
    word = jnp.zeros(lane.shape, jnp.int32)
    for q in range(PB):
        word = jnp.where(lane == q, table[0, q], word)
    for j in range(CB):
        word = jnp.where(lane == PB + j, aggs[0, 0, j], word)
    held[n_p + n_s : n_p + n_s + META, :] = word.astype(F32).astype(BF16)
    large[0].wait()
    stores = [pltpu.make_async_copy(held.at[0:cut], out.at[0:cut], sems.at[6])]
    stores[0].start()
    large[1].wait()
    large[2].wait()
    rest = pl.ds(cut, out.shape[0] - cut)
    stores.append(pltpu.make_async_copy(held.at[rest], out.at[rest], sems.at[7]))
    stores[1].start()
    for store in stores:
        store.wait()


def fill_table(s, slots, table, code_of):
    for q in range(PB + 1):
        table[s, q] = -1
    for k in range(slots):
        table[s, code_of(k)] = k


def block_at(s, q, size, table, near):
    slot = table[s, q]
    block = near[pl.ds(pl.multiple_of(jnp.maximum(slot, 0) * size, size), size), :]
    return jnp.where(slot >= 0, block, jnp.zeros_like(block))


def lift_of(near, slots, size, agg_of):
    lines = []
    for j in range(CB):
        block = near[(slots + j) * size : (slots + j + 1) * size, :]
        lines.append(
            jnp.concatenate(
                [jnp.where(agg_of(j) == a, block, jnp.zeros_like(block)) for a in range(G2)],
                axis=1,
            )
        )
    return jnp.concatenate(lines, axis=0)


def dense_of(s, size, table, near, dense):
    for i in range(FB):
        for j in range(CB):
            dense[i * size : (i + 1) * size, j * size : (j + 1) * size] = block_at(
                s, i * CB + j, size, table, near
            )


def coarse_of(size, weight, dense, tile):
    coarse = jnp.dot(weight, dense[...], preferred_element_type=F32).astype(BF16)
    for i in range(CB):
        for j in range(CB):
            tile[i, j] = coarse[i * size : (i + 1) * size, j * size : (j + 1) * size]
    return coarse


def own_kernel(
    slots, size, rows_at, cols_at, count_at, codes_at, p_count_at, aggs_at, fine_at, own_at,
    col_at, row_at, more_at, c_one,
    fine, own, stock, more, turned, acc, dense, tile, rows, cols, count, codes, p_count, aggs, table, sems,
):
    pairs = [
        (rows_at, rows), (cols_at, cols), (count_at, count), (codes_at, codes),
        (p_count_at, p_count), (aggs_at, aggs),
    ]
    small = [pltpu.make_async_copy(a, b, sems.at[2 + n]) for n, (a, b) in enumerate(pairs)]
    for copy in small:
        copy.start()
    fetch_own = pltpu.make_async_copy(own_at, own, sems.at[0])
    fetch_own.start()
    fetch_fine = pltpu.make_async_copy(fine_at, fine, sems.at[1])
    fetch_fine.start()
    acc[...] = jnp.zeros_like(acc)
    turned[...] = jnp.zeros_like(turned)
    for copy in small:
        copy.wait()
    code_of = lambda k: jnp.where(k < p_count[0, 0], codes[0, 0, k], PB)
    fill_table(0, slots, table, code_of)
    fetch_own.wait()
    for k in range(slots):
        i = code_of(k) // CB
        j = pl.multiple_of((code_of(k) - i * CB) * size, size)
        turned[i, pl.ds(j, size), :] = own[k * size : (k + 1) * size, :].T
    fetch_fine.wait()

    def step(t, carry):
        products, targets = [], []
        for u in range(UNROLL):
            k = t * UNROLL + u
            products.append(jnp.dot(turned[rows[0, 0, k]], fine[k], preferred_element_type=F32))
            targets.append(jnp.where(k < count[0, 0], cols[0, 0, k], NS * FB))
        for u in range(UNROLL):
            acc[targets[u]] += products[u]
        return carry

    lax.fori_loop(0, (count[0, 0] + UNROLL - 1) // UNROLL, step, 0)
    stores = []
    for s in range(1, NS):
        for m in range(FB):
            stock[s - 1, :, m * size : (m + 1) * size] = acc[s * FB + m].astype(BF16)
        stock_at, n = (col_at, s - 1) if s < 3 else (row_at, s - 3)
        stores.append(pltpu.make_async_copy(stock.at[s - 1], stock_at.at[n], sems.at[1 + s]))
        stores[-1].start()
    own_weight = jnp.concatenate([acc[m].astype(BF16) for m in range(FB)], axis=1)
    dense_of(0, size, table, own, dense)
    coarse = coarse_of(size, own_weight, dense, tile)
    lift = lift_of(own, slots, size, lambda j: aggs[0, 0, j])
    wide = CB * size
    more[0] = lift.T
    more[1] = coarse
    more[2] = lift
    stores.append(pltpu.make_async_copy(more, more_at, sems.at[0]))
    stores[-1].start()
    stores.append(pltpu.make_async_copy(tile, c_one.at[:, 0], sems.at[1]))
    stores[-1].start()
    for store in stores:
        store.wait()


def near_coarse(
    base, sources, near, slots, size, stock, c_one, dense, tiles, words, codes, sems
):
    tail = (slots + CB) * size
    for n, ref in enumerate(near):
        word = ref[tail : tail + META, :].astype(F32).astype(jnp.int32)
        words[n : n + 1, :] = word[0:1, :]
    fetch = pltpu.make_async_copy(words, codes, sems.at[0])
    fetch.start()
    fetch.wait()
    parts, stores = [], []
    for n, (s, ref) in enumerate(zip(sources, near)):
        dense_of(n, size, codes, ref, dense.at[n])
        coarse = coarse_of(size, stock[s - base], dense.at[n], tiles.at[n])
        store = pltpu.make_async_copy(tiles.at[n], c_one.at[:, s], sems.at[1 + n])
        store.start()
        stores.append(store)
        lift = lift_of(ref, slots, size, lambda j: codes[n, PB + j])
        parts.append(jnp.dot(coarse, lift, preferred_element_type=F32))
    return parts, stores


def half_kernel(more, lift_t, half):
    lift_t[...] = more[0]
    half[...] = jnp.dot(more[1], more[2], preferred_element_type=F32)


def side_kernel(slots, size, stock, lift_t, half, right, left, c_in, c_one, term, *scratch):
    parts, stores = near_coarse(1, (2, 1), (right, left), slots, size, stock, c_one, *scratch)
    whole = (half[...] + parts[0] + parts[1]).astype(BF16)
    term[...] = jnp.dot(lift_t[...], whole, preferred_element_type=F32)
    for store in stores:
        store.wait()


def row_kernel(slots, size, cols_n, stock, lift_t, term, other, pair, c_in, c_one, *rest):
    sends, terms, scratch = rest[:cols_n], rest[cols_n], rest[cols_n + 1 :]
    odd = lax.rem(lax.axis_index("row"), 2)
    sources = (3 + odd, 4 - odd)
    parts, stores = near_coarse(3, sources, (other, pair), slots, size, stock, c_one, *scratch)
    terms[0] = term[...]
    for n in range(2):
        terms[sources[n] - 2] = jnp.dot(lift_t[...], parts[n].astype(BF16), preferred_element_type=F32)
    chunk = terms.shape[1] // cols_n
    me = lax.axis_index("col")
    for d in range(cols_n):
        to = pl.multiple_of(lax.rem(me + d, cols_n) * chunk, chunk)
        sends[d][...] = terms[:, pl.ds(to, chunk), :].astype(sends[d].dtype)
    for store in stores:
        store.wait()


def sum_kernel(*refs):
    total = refs[0][...]
    for ref in refs[1:-1]:
        total = total + ref[...].astype(F32)
    refs[-1][...] = total.astype(BF16)


def spread_kernel(size, steps, *refs):
    cols_n = len(steps)
    parts, out_at, out, sems = refs[:cols_n], refs[cols_n], refs[cols_n + 1], refs[cols_n + 2]
    chunk = parts[0].shape[1]
    unit = math.gcd(chunk, size)
    per = size // unit
    me = lax.axis_index("col")
    stores = []
    for n, d in enumerate(steps):
        owner = lax.rem(me - d + cols_n, cols_n)
        for t in range(chunk // unit):
            at = owner * (chunk // unit) + t
            a = at // per
            rows = pl.ds(pl.multiple_of(lax.rem(at, per) * unit, unit), unit)
            for g in range(3):
                for b in range(G2):
                    out[a, g, b, rows, :] = parts[n][
                        g, t * unit : (t + 1) * unit, b * size : (b + 1) * size
                    ].astype(F32)
            spot = (a, slice(None), slice(None), rows)
            stores.append(pltpu.make_async_copy(out.at[spot], out_at.at[spot], sems.at[len(stores)]))
            stores[-1].start()
    for store in stores:
        store.wait()


def shift(x, axis, step, wrap):
    n = lax.axis_size(axis)
    pairs = [(i, (i + step) % n) for i in range(n) if wrap or 0 <= i + step < n]
    return lax.ppermute(x, axis, pairs)


def swap(x, axis, pairs):
    return lax.ppermute(x, axis, pairs + [(j, i) for i, j in pairs])


def per_device(
    fine_blocks, fine_rows, fine_cols, fine_counts, prolong_blocks, prolong_codes,
    prolong_counts, second_blocks, second_aggs,
):
    slots, size = prolong_blocks.shape[2], prolong_blocks.shape[3]
    cap = fine_blocks.shape[2]
    cols_n = lax.axis_size("col")
    packed_rows = (slots + CB) * size + META
    wide = CB * size
    dma = pltpu.SemaphoreType.DMA
    packed = pl.pallas_call(
        pack_kernel,
        out_shape=jax.ShapeDtypeStruct((packed_rows, size), BF16),
        in_specs=[HBM] * 5,
        out_specs=HBM,
        scratch_shapes=[
            pltpu.VMEM((packed_rows, size), BF16),
            pltpu.SMEM(prolong_codes.shape, jnp.int32),
            pltpu.SMEM(prolong_counts.shape, jnp.int32),
            pltpu.SMEM(second_aggs.shape, jnp.int32),
            pltpu.SMEM((1, PB + 1), jnp.int32),
            dma((8,)),
        ],
        compiler_params=WHOLE,
        name="pack",
    )(
        prolong_codes, prolong_counts, second_aggs,
        prolong_blocks.reshape(slots * size, size),
        second_blocks.reshape(CB * size, size),
    )
    rows_n = lax.axis_size("row")
    pair = swap(packed, "row", [(i, i + 1) for i in range(0, rows_n - 1, 2)])
    other = swap(packed, "row", [(i, i + 1) for i in range(1, rows_n - 1, 2)])
    right = shift(packed, "col", -1, False)
    left = shift(packed, "col", 1, False)

    c_shape = jax.ShapeDtypeStruct((CB, NS, CB, size, size), BF16)
    table = pltpu.SMEM((1, PB + 1), jnp.int32)
    integers = (
        fine_rows, fine_cols, fine_counts, prolong_codes, prolong_counts, second_aggs
    )
    col_stock, row_stock, more, c_one = pl.pallas_call(
        functools.partial(own_kernel, slots, size),
        out_shape=[
            jax.ShapeDtypeStruct((2, wide, FB * size), BF16),
            jax.ShapeDtypeStruct((2, wide, FB * size), BF16),
            jax.ShapeDtypeStruct((3, wide, G2 * size), BF16),
            c_shape,
        ],
        in_specs=[HBM] * 8,
        out_specs=[HBM] * 4,
        scratch_shapes=[
            pltpu.VMEM((cap, size, size), BF16),
            pltpu.VMEM((packed_rows, size), BF16),
            pltpu.VMEM((NS - 1, wide, FB * size), BF16),
            pltpu.VMEM((3, wide, G2 * size), BF16),
            pltpu.VMEM((FB + 1, wide, size), BF16),
            pltpu.VMEM((NS * FB + 1, wide, size), F32),
            pltpu.VMEM((FB * size, wide), BF16),
            pltpu.VMEM((CB, CB, size, size), BF16),
            *[pltpu.SMEM(x.shape, jnp.int32) for x in integers],
            table,
            dma((8,)),
        ],
        compiler_params=WHOLE,
        cost_estimate=pl.CostEstimate(flops=10**9, bytes_accessed=4 * 10**6, transcendentals=0),
        name="own_source",
    )(
        *integers, fine_blocks[0, 0], packed,
    )

    near_scratch = [
        pltpu.VMEM((2, FB * size, wide), BF16),
        pltpu.VMEM((2, CB, CB, size, size), BF16),
        pltpu.VMEM((8, size), jnp.int32),
        pltpu.SMEM((8, size), jnp.int32),
        dma((3,)),
    ]
    square = jax.ShapeDtypeStruct((wide, G2 * size), F32)
    lift_t, half = pl.pallas_call(
        half_kernel,
        out_shape=[jax.ShapeDtypeStruct((G2 * size, wide), BF16), square],
        in_specs=[VMEM],
        out_specs=[VMEM] * 2,
        compiler_params=SMALL,
        cost_estimate=pl.CostEstimate(flops=10**9, bytes_accessed=4 * 10**6, transcendentals=0),
        name="own_half",
    )(more)
    c_one, term = pl.pallas_call(
        functools.partial(side_kernel, slots, size),
        out_shape=[c_shape, square],
        in_specs=[VMEM] * 5 + [HBM],
        out_specs=[HBM, VMEM],
        input_output_aliases={5: 0},
        scratch_shapes=near_scratch,
        compiler_params=LARGE,
        name="col_sources",
    )(col_stock, lift_t, half, right, left, c_one)

    chunk = G2 * size // cols_n
    kept = jax.ShapeDtypeStruct((3, chunk, G2 * size), F32)
    piece = jax.ShapeDtypeStruct(kept.shape, BF16)
    c_one, *sends = pl.pallas_call(
        functools.partial(row_kernel, slots, size, cols_n),
        out_shape=[c_shape, kept] + [piece] * (cols_n - 1),
        in_specs=[VMEM] * 5 + [HBM],
        out_specs=[HBM] + [VMEM] * cols_n,
        input_output_aliases={5: 0},
        scratch_shapes=[pltpu.VMEM((3, G2 * size, G2 * size), F32)] + near_scratch,
        compiler_params=LARGE,
        name="row_sources",
    )(row_stock, lift_t, term, other, pair, c_one)
    farthest = sorted(range(1, cols_n), key=lambda d: -min(d, cols_n - d))
    parts = [sends[0]] + [shift(sends[d], "col", d, True) for d in farthest]
    total = pl.pallas_call(
        sum_kernel, out_shape=piece, in_specs=[VMEM] * cols_n, out_specs=VMEM,
        compiler_params=SMALL, name="total",
    )(*parts)
    nearest = farthest[::-1]
    gathered = [total] + [shift(total, "col", d, True) for d in nearest]
    c_two = pl.pallas_call(
        functools.partial(spread_kernel, size, [0] + nearest),
        out_shape=jax.ShapeDtypeStruct((G2, 3, G2, size, size), F32),
        in_specs=[VMEM] * cols_n,
        out_specs=HBM,
        scratch_shapes=[
            pltpu.VMEM((G2, 3, G2, size, size), F32),
            dma((G2 * size // math.gcd(chunk, size),)),
        ],
        compiler_params=SMALL,
        name="spread",
    )(*gathered)
    return (c_one[None, None], c_two[None])


def solution(mesh):
    in_specs = (
        P("row", "col", None, None, None),
        P("row", "col", None),
        P("row", "col", None),
        P("row", "col"),
        P("row", "col", None, None, None),
        P("row", "col", None),
        P("row", "col"),
        P("row", "col", None, None, None),
        P("row", "col", None),
    )
    out_specs = (
        P("row", "col", None, None, None, None, None),
        P("row", None, None, None, None, None),
    )
    return jax.shard_map(
        per_device, mesh=mesh, in_specs=in_specs, out_specs=out_specs, check_vma=False
    )
```
